512 devices in a mesh: tm: 32 (over x_lo, y, core), mp: 16 (over x_hi, z).
Axes of the slice: x: 4 (x_hi: 2, x_lo: 2; x = x_hi * 2 + x_lo), y: 8, z: 8, core: 2. Of those that a mesh axis runs over, the one named last changes fastest.
Arguments:
- tokens: bfloat16 [65536, 1024], P('tm', 'mp'), may hold values from -45 to 45
- ln_conv_gain: float32 [1024], replicated, may hold values from 0.25 to 1.75
- glu_weight: bfloat16 [1024, 2, 1024], P(None, None, 'mp'), may hold values from -0.1875 to 0.1875
- depth_weight: float32 [31, 1024], P(None, 'mp'), may hold values from -1 to 1
- bn_gain: float32 [1024], P('mp'), may hold values from 0.25 to 1.75
- bn_shift: float32 [1024], P('mp'), may hold values from -1 to 1
- conv_out_weight: bfloat16 [1024, 1024], P(None, 'mp'), may hold values from -0.1875 to 0.1875
- ln_ff_gain: float32 [1024], replicated, may hold values from 0.25 to 1.75
- ff_in_weight: bfloat16 [1024, 4096], P(None, 'mp'), may hold values from -0.1875 to 0.1875
- ff_out_weight: bfloat16 [4096, 1024], P('mp'), may hold values from -0.125 to 0.125
Outputs:
- block_out: bfloat16 [65536, 1024], P('tm', 'mp')
The draws below stay inside these ranges and needn't reach their ends.
All inputs are finite; a program needn't handle non-finite values.
Results may differ from the reference program's by a relative error of at most 0.009.
Values may be sent and summed in bfloat16 or wider, within the bound.
No kernel may reach another device: no remote copies, remote signals or barrier semaphores. Data moves between devices by JAX's collectives and lax.ppermute only.
A program may use at most 64 MiB of HBM per device.

```python
import math
import jax
import jax.numpy as jnp
from jax import lax

D = 1024
FF = 4096
KERNEL = 31
TOK_DEV = 2048
TOKENS = 65536
N_MP = 16


def draw_tokens(key, part):
    key_noise, key_common, key_scale = jax.random.split(key, 3)
    position = jnp.arange(TOKENS, dtype=jnp.float32) / TOKENS
    row_scale = jnp.exp(jax.random.uniform(key_scale, (TOKENS, 1), jnp.float32, math.log(0.3), math.log(3.0)))
    noise = jnp.clip(jax.random.normal(key_noise, (TOKENS, D), jnp.float32), -4.0, 4.0)
    common = jnp.clip(jax.random.normal(key_common, (D,), jnp.float32), -3.0, 3.0)
    ramp = 0.2 + 1.8 * position
    return (row_scale * (ramp[:, None] * common[None, :] + noise)).astype(jnp.bfloat16)


def with_spikes(array, own_key, source, target, shards_of, factor):
    def block_of(dim):
        return (jnp.arange(array.shape[dim]) // (array.shape[dim] // shards_of)).reshape((-1,) + (1,) * (array.ndim - 1 - dim))

    first = jax.random.permutation(own_key, shards_of)[block_of(target)]
    far = (block_of(target) + shards_of // 2) % shards_of
    return jnp.where((block_of(source) == first) | (block_of(source) == far), factor * array, array)


def steps_of(key, dims, shards, least, high):
    gain, own = 1.0, jax.random.fold_in(key, 6)
    for dim, parts in shards:
        steps = jnp.exp(jax.random.uniform(jax.random.fold_in(own, dim), (parts,), jnp.float32, least / len(shards), high / len(shards)))
        gain = gain * jnp.repeat(steps, dims[dim] // parts).reshape([-1 if axis == dim else 1 for axis in range(len(dims))])
    return gain


def bell_draw(key, dims, scale, limit, shards=(), held_as=jnp.bfloat16):
    drawn = scale * jax.random.normal(key, dims, jnp.float32)
    if shards:
        drawn = drawn * steps_of(key, dims, shards, -0.22, 0.18)
    return jnp.clip(drawn, -limit, limit).astype(held_as)


def gaussian_with(key, extent, scale, most, pieces, heavy, kind=jnp.bfloat16):
    result = scale * jax.random.normal(key, extent, jnp.float32)
    if pieces:
        result = result * steps_of(key, extent, pieces, -0.22, 0.18)
    return jnp.clip(with_spikes(result, jax.random.fold_in(key, 3), *heavy), -most, most).astype(kind)


def setup_inputs(seed: int = 0) -> dict:
    streams_of = jax.random.split(jax.random.key(seed), 11)
    return {
        "tokens": draw_tokens(jax.random.fold_in(streams_of[10], 71), 0),
        "ln_conv_gain": jnp.clip(1.0 + 0.15 * jax.random.normal(streams_of[1], (D,), jnp.float32), 0.25, 1.75),
        "glu_weight": bell_draw(streams_of[2], (D, 2, D), D ** -0.5, 0.1875, ((2, 16),)),
        "depth_weight": bell_draw(streams_of[3], (KERNEL, D), KERNEL ** -0.5, 1.0, ((1, 16),), jnp.float32),
        "bn_gain": jnp.clip(1.0 + 0.15 * jax.random.normal(streams_of[4], (D,), jnp.float32), 0.25, 1.75),
        "bn_shift": jnp.clip(jax.random.uniform(streams_of[5], (D,), jnp.float32, -1.0, 1.0) * steps_of(streams_of[5], (D,), ((0, 16),), -0.4, 0.0), -1.0, 1.0),
        "conv_out_weight": bell_draw(streams_of[6], (D, D), D ** -0.5, 0.1875, ((1, 16),)),
        "ln_ff_gain": jnp.clip(1.0 + 0.15 * jax.random.normal(streams_of[7], (D,), jnp.float32), 0.25, 1.75),
        "ff_in_weight": bell_draw(streams_of[8], (D, FF), D ** -0.5, 0.1875, ((1, 16),)),
        "ff_out_weight": gaussian_with(streams_of[9], (FF, D), FF ** -0.5, 0.125, ((0, 16),), (0, 1, 16, 2.0)),
    }


def layer_norm(values, scale_gain):
    centre = lax.optimization_barrier(jnp.mean(values, axis=-1, keepdims=True))
    spread = lax.optimization_barrier(jnp.mean((values - centre) * (values - centre), axis=-1, keepdims=True))
    return (values - centre) * lax.rsqrt(spread + 1e-05) * scale_gain

def reference(tokens, ln_conv_gain, glu_weight, depth_weight, bn_gain, bn_shift, conv_out_weight, ln_ff_gain, ff_in_weight, ff_out_weight):
    inputs = tokens.astype(jnp.float32)
    normed = layer_norm(inputs, ln_conv_gain).astype(jnp.bfloat16)
    paired = jnp.dot(normed, glu_weight.reshape(D, 2 * D), preferred_element_type=jnp.float32)
    paired = paired.reshape(TOKENS, 2, D)
    gated = (paired[:, 0, :] * jax.nn.sigmoid(paired[:, 1, :])).astype(jnp.bfloat16)
    half_span = (KERNEL - 1) // 2
    padded = jnp.pad(gated.astype(jnp.float32), ((half_span, half_span), (0, 0)))
    convolved = jnp.zeros((TOKENS, D), jnp.float32)
    for offset in range(KERNEL):
        convolved = convolved + depth_weight[offset][None, :] * padded[offset:offset + TOKENS]
    channel_mean = lax.optimization_barrier(jnp.mean(convolved, axis=0))
    centred = convolved - channel_mean[None, :]
    variance = lax.optimization_barrier(jnp.mean(centred * centred, axis=0))
    normal_bn = centred * lax.rsqrt(variance + 1e-05)[None, :] * bn_gain[None, :] + bn_shift[None, :]
    activated = (normal_bn * jax.nn.sigmoid(normal_bn)).astype(jnp.bfloat16)
    block_mid = (inputs + jnp.dot(activated, conv_out_weight, preferred_element_type=jnp.float32)).astype(jnp.bfloat16)
    grouped_out = ff_out_weight.reshape(N_MP, FF // N_MP, D).astype(jnp.float32)

    def ff_block(rows):
        rows_float = rows.astype(jnp.float32)
        normed_ff = layer_norm(rows_float, ln_ff_gain).astype(jnp.bfloat16)
        pre_act = jnp.dot(normed_ff, ff_in_weight, preferred_element_type=jnp.float32)
        hidden = (pre_act * jax.nn.sigmoid(pre_act)).astype(jnp.bfloat16)
        split_hidden = hidden.reshape(rows.shape[0], N_MP, FF // N_MP).astype(jnp.float32)
        partials = jnp.einsum('tmf,mfd->mtd', split_hidden, grouped_out)
        rounded = lax.optimization_barrier(partials.astype(jnp.bfloat16)).astype(jnp.float32)
        ff_sum = lax.optimization_barrier(jnp.sum(rounded, axis=0))
        return (rows_float + 0.5 * ff_sum).astype(jnp.bfloat16)
    blocks = block_mid.reshape(TOKENS // TOK_DEV, TOK_DEV, D)
    return lax.map(ff_block, blocks).reshape(TOKENS, D)
```

```python
import jax
import jax.numpy as jnp
from jax import lax
from jax.sharding import Mesh, PartitionSpec as P

XLO, Y, CORE, XHI, Z = ("xlo", "y", "core", "xhi", "z")
BF, F32 = (jnp.bfloat16, jnp.float32)


def swap(x, axis):
    return lax.ppermute(x, axis, [(0, 1), (1, 0)])


def ordered(index, own, other):
    first = index == 0
    return jnp.where(first, own, other), jnp.where(first, other, own)


def group_gather(x, core, xhi):
    across = swap(x, XHI)
    beside = swap(x, CORE)
    far = swap(across, CORE)
    near = ordered(xhi, x, across)
    away = ordered(xhi, beside, far)
    return [[ordered(core, near[h], away[h])[c] for h in range(2)] for c in range(2)]


def split3(x):
    hi = x.astype(BF)
    rest = x - hi.astype(F32)
    mid = rest.astype(BF)
    return hi, mid, (rest - mid.astype(F32)).astype(BF)


def layer_norm(values, gain, axis):
    centre = jnp.mean(values, axis=axis, keepdims=True)
    spread = jnp.mean((values - centre) * (values - centre), axis=axis, keepdims=True)
    return (values - centre) * lax.rsqrt(spread + 1e-05) * gain


def combine(mean, square, count, axes):
    n = lax.axis_size(axes)
    stats = jnp.stack([mean, square])
    stats = lax.all_to_all(
        jnp.broadcast_to(stats[None], (n,) + stats.shape), axes, 0, 0, tiled=True
    )
    whole = jnp.mean(stats[:, 0], axis=0)
    apart = stats[:, 0] - whole
    return whole, jnp.sum(stats[:, 1], axis=0) + count * jnp.sum(apart * apart, axis=0)


def body(
    tokens,
    ln_conv_gain,
    glu_weight,
    depth_weight,
    bn_gain,
    bn_shift,
    conv_out_weight,
    ln_ff_gain,
    ff_in_weight,
    ff_out_weight,
):
    core, xhi = (lax.axis_index(CORE), lax.axis_index(XHI))
    nz = lax.axis_size(Z)
    frames, width = tokens.shape
    full = ln_conv_gain.shape[0]
    half = width // 2
    run = frames // nz
    taps = depth_weight.shape[0]
    span = (taps - 1) // 2
    total = frames * lax.axis_size((XLO, Y, CORE))

    def mine(x, axis, size):
        return lax.dynamic_slice_in_dim(x, core * size, size, axis=axis)

    glu = mine(glu_weight.transpose(1, 2, 0), 1, half).reshape(2 * half, full)
    conv_out = mine(conv_out_weight.T, 0, half)
    small = jnp.concatenate([depth_weight, bn_gain[None], bn_shift[None]], axis=0)
    small = mine(small.T, 0, half)
    small = jnp.concatenate(split3(small), axis=1)
    small = jnp.pad(small, ((0, 0), (0, 128 - small.shape[1]))).reshape(-1, full)
    first = lax.all_gather(jnp.concatenate([glu, conv_out, small], axis=0), Z)
    units = ff_in_weight.shape[1] // 2
    ff_in = mine(ff_in_weight, 1, units).T
    ff_out = mine(ff_out_weight, 0, units)
    second = lax.all_gather(jnp.concatenate([ff_in, ff_out], axis=0), Z)

    glu = first[:, : 2 * half].reshape(nz, 2, half, full).transpose(1, 0, 2, 3).reshape(-1, full)
    conv_out = first[:, 2 * half : 3 * half].reshape(-1, full)
    small = first[:, 3 * half :].reshape(nz * half, 128).astype(F32)
    n = taps + 2
    small = small[:, :n] + (small[:, n : 2 * n] + small[:, 2 * n : 3 * n])
    tap_weights, gain, shift = (small[:, :taps], small[:, taps], small[:, taps + 1])
    ff_in = second[:, :units].reshape(-1, full)
    ff_out = second[:, units:].reshape(-1, full)

    tok = tokens.T
    tm = lax.axis_size((XLO, Y, CORE))
    up = [(i, i + 1) for i in range(tm - 1)]
    left = lax.ppermute(tok[:, frames - span :], (XLO, Y, CORE), up)
    right = lax.ppermute(tok[:, :span], (XLO, Y, CORE), [(j, i) for i, j in up])
    lefts = [left] + [tok[:, k * run - span : k * run] for k in range(1, nz)]
    rights = [tok[:, k * run : k * run + span] for k in range(1, nz)] + [right]
    pad = jnp.zeros((width, 128 - 2 * span), BF)
    parts = [
        jnp.concatenate([tok[:, k * run : (k + 1) * run], lefts[k], rights[k], pad], axis=1)
        for k in range(nz)
    ]
    parts = lax.all_to_all(jnp.stack(parts), Z, 0, 0, tiled=True)
    here = group_gather(parts.reshape(nz * width, run + 128), core, xhi)
    whole = jnp.concatenate([jnp.concatenate(c, axis=0) for c in here], axis=1)
    normed = layer_norm(whole.astype(F32), ln_conv_gain[:, None], 0).astype(BF)
    paired = jnp.dot(glu, normed, preferred_element_type=F32)
    mid = nz * half
    gated = (paired[:mid] * jax.nn.sigmoid(paired[mid:])).astype(BF)
    gated = gated.reshape(mid, 2, run + 128).astype(F32)
    window = jnp.concatenate(
        [gated[:, :, run : run + span], gated[:, :, :run], gated[:, :, run + span : run + 2 * span]],
        axis=2,
    )
    convolved = jnp.zeros((mid, 2, run), F32)
    for j in range(taps):
        convolved = convolved + tap_weights[:, j][:, None, None] * window[:, :, j : j + run]
    convolved = convolved.reshape(mid, 2 * run)
    mean = jnp.mean(convolved, axis=1)
    apart = convolved - mean[:, None]
    square = jnp.sum(apart * apart, axis=1)
    count = 2 * run
    mean, square = combine(mean, square, count, (Z,))
    mean, square = combine(mean, square, count * nz, (XLO, Y))
    variance = square / total
    normal_bn = (convolved - mean[:, None]) * lax.rsqrt(variance + 1e-05)[:, None] * gain[
        :, None
    ] + shift[:, None]
    activated = (normal_bn * jax.nn.sigmoid(normal_bn)).astype(BF)

    def natural(blocks):
        cols = blocks[0][0].shape[1]
        x = jnp.stack([jnp.stack([b.reshape(nz, half, cols) for b in c]) for c in blocks])
        return x.transpose(1, 2, 0, 3, 4).reshape(full, cols)

    mixed = jnp.dot(
        conv_out, natural(group_gather(activated, core, xhi)), preferred_element_type=F32
    )
    rows = lax.dynamic_slice_in_dim(whole, xhi * nz * width, nz * width, axis=0)
    rows = rows.reshape(nz, width, 2, run + 128)[..., :run]
    residual = mine(rows, 1, half).reshape(mid, 2 * run)
    block = (residual.astype(F32) + mixed).astype(BF)
    block = natural(group_gather(block, core, xhi))
    normed_ff = layer_norm(block.astype(F32), ln_ff_gain[:, None], 0).astype(BF)
    pre_act = jnp.dot(ff_in, normed_ff, preferred_element_type=F32)
    hidden = (pre_act * jax.nn.sigmoid(pre_act)).astype(BF)
    partial = lax.dot_general(
        ff_out, hidden, (((0,), (0,)), ((), ())), preferred_element_type=F32
    )
    keep, give = ordered(core, partial[:, :run], partial[:, run:])
    keep = keep + swap(give.astype(BF), CORE).astype(F32)
    keep, give = ordered(xhi, keep[: full // 2], keep[full // 2 :])
    keep = keep + swap(give.astype(BF), XHI).astype(F32)
    block = lax.dynamic_slice(block, (xhi * (full // 2), core * run), (full // 2, run))
    out = (block.astype(F32) + 0.5 * keep).astype(BF)
    out = lax.all_to_all(out.reshape(nz, width, run), Z, 0, 0, tiled=True)
    return out.transpose(1, 0, 2).reshape(width, frames).T


def solution(mesh):
    fine = Mesh(mesh.devices.reshape(2, 8, 2, 2, 8), (XLO, Y, CORE, XHI, Z))
    tm, mp = ((XLO, Y, CORE), (XHI, Z))
    in_specs = (
        P(tm, mp),
        P(),
        P(None, None, mp),
        P(None, mp),
        P(mp),
        P(mp),
        P(None, mp),
        P(),
        P(None, mp),
        P(mp, None),
    )
    return jax.shard_map(body, mesh=fine, in_specs=in_specs, out_specs=P(tm, mp), check_vma=False)
```

```python
import jax
import jax.numpy as jnp
from jax import lax
from jax.experimental import pallas as pl
from jax.experimental.pallas import tpu as pltpu
from jax.sharding import Mesh, PartitionSpec as P

XLO, Y, CORE, XHI, Z = ("xlo", "y", "core", "xhi", "z")
BF, F32 = (jnp.bfloat16, jnp.float32)
EPS = 1e-05
LANES = 128
SPAN = 15
VMEM = pl.BlockSpec(memory_space=pltpu.VMEM)
SMEM = pl.BlockSpec(memory_space=pltpu.SMEM)
ANY = pl.BlockSpec(memory_space=pl.ANY)
PARAMS = pltpu.CompilerParams(vmem_limit_bytes=40 << 20)


def shape(dims, dtype):
    return jax.ShapeDtypeStruct(dims, dtype)


def swap(x, axis):
    return lax.ppermute(x, axis, [(0, 1), (1, 0)])


def group_gather(x):
    across = swap(x, XHI)
    beside = swap(x, CORE)
    return x, across, beside, swap(across, CORE)


def split3(x):
    hi = x.astype(BF)
    rest = x - hi.astype(F32)
    mid = rest.astype(BF)
    return hi, mid, (rest - mid.astype(F32)).astype(BF)


def norm_rows(x, gain):
    inv = 1.0 / x.shape[0]
    centred = x - jnp.sum(x, axis=0, keepdims=True) * inv
    spread = jnp.sum(centred * centred, axis=0, keepdims=True) * inv
    return (centred * lax.rsqrt(spread + EPS) * gain).astype(BF)


def at(start, size, step):
    return pl.ds(pl.multiple_of(start, step), size)


def pack_kernel(tok, left, right, out):
    lane = lax.broadcasted_iota(jnp.int32, (16, LANES), 1)
    nz = out.shape[0]
    for z in range(nz):
        out[z, 0:64] = tok[:, 2 * z * LANES : (2 * z + 1) * LANES]
        out[z, 64:128] = tok[:, (2 * z + 1) * LANES : (2 * z + 2) * LANES]
        packed = jnp.zeros((16, LANES), F32)
        for i in range(4):
            rows = slice(16 * i, 16 * i + 16)
            if z == 0:
                before = left[rows]
            else:
                before = tok[rows, (2 * z - 1) * LANES : 2 * z * LANES]
            if z == nz - 1:
                after = right[rows]
            else:
                after = tok[rows, (2 * z + 2) * LANES : (2 * z + 3) * LANES]
            low = pltpu.roll(before.astype(F32), (32 * i + SPAN) % LANES, 1)
            high = pltpu.roll(after.astype(F32), 32 * i + SPAN, 1)
            packed = jnp.where((lane >= 32 * i) & (lane < 32 * i + SPAN), low, packed)
            packed = jnp.where(
                (lane >= 32 * i + SPAN) & (lane < 32 * i + 2 * SPAN), high, packed
            )
        out[z, 128:144] = packed.astype(BF)


def conv_kernel(
    place, own, across, beside, far, glu, small, gain,
    conv, stats, par, res,
    tok, edge, win, taps,
):
    core, xhi = place[0], place[1]
    lane = lax.broadcasted_iota(jnp.int32, (16, LANES), 1)
    nz = glu.shape[0]
    for near, away, side in ((own, beside, xhi), (across, far, 1 - xhi)):
        for z in range(nz):
            row = side * (64 * nz) + 64 * z
            for c, blk in ((0, near), (1, away)):
                tok[at(row, 64, 64), 256 * c : 256 * c + 128] = blk[z, 0:64]
                tok[at(row, 64, 64), 256 * c + 128 : 256 * c + 256] = blk[z, 64:128]
            one = near[z, 128:144].astype(F32)
            two = away[z, 128:144].astype(F32)
            for i in range(4):
                low = pltpu.roll(one, (LANES - 32 * i) % LANES, 1)
                high = pltpu.roll(two, (LANES + 32 - 32 * i) % LANES, 1)
                part = jnp.where(lane < 32, low, jnp.where(lane < 64, high, 0.0))
                edge[at(row + 16 * i, 16, 16), :] = part
    for z in range(nz):
        row = xhi * (64 * nz) + 64 * z + 32 * core
        res[32 * z : 32 * z + 32, :] = tok[at(row, 32, 32), :]

    for z in range(nz):
        s = small[z].astype(F32)
        for i in range(2):
            hi = s[:, LANES * i : LANES * (i + 1)]
            mid = s[:, LANES * (2 + i) : LANES * (3 + i)]
            low = s[:, LANES * (4 + i) : LANES * (5 + i)]
            taps[32 * z + 16 * i : 32 * z + 16 * i + 16, :] = hi + (mid + low)
    table = [taps[0:128, :].T, taps[128:256, :].T]
    for h in range(2):
        par[:, LANES * h : LANES * (h + 1)] = table[h][31:39]

    weight = glu[...].reshape(glu.shape[0] * glu.shape[1], glu.shape[2])
    scale = gain[...]
    for c in range(3):
        x = edge[...] if c == 2 else tok[:, 256 * c : 256 * (c + 1)].astype(F32)
        paired = jnp.dot(weight, norm_rows(x, scale), preferred_element_type=F32)
        cols = x.shape[1]
        paired = paired.reshape(nz, 2, 32, cols)
        gated = (paired[:, 0] * jax.nn.sigmoid(paired[:, 1])).astype(BF).astype(F32)
        gated = gated.reshape(32 * nz, cols).T
        if c < 2:
            win[c, 16:272, :] = gated
        else:
            for r in range(2):
                win[r, 1:16, :] = gated[32 * r : 32 * r + 15]
                win[r, 272:287, :] = gated[32 * r + 15 : 32 * r + 30]

    step = 64
    for h in range(2):
        cols = slice(LANES * h, LANES * (h + 1))
        total = jnp.zeros((1, LANES), F32)
        for r in range(2):
            for k in range(256 // step):
                acc = jnp.zeros((step, LANES), F32)
                for j in range(31):
                    first = step * k + 1 + j
                    acc = acc + table[h][j : j + 1] * win[r, first : first + step, cols]
                conv[256 * r + step * k : 256 * r + step * (k + 1), cols] = acc
                total = total + jnp.sum(acc, axis=0, keepdims=True)
        mean = total * (1.0 / 512)
        apart = conv[:, cols] - mean
        square = jnp.sum(apart * apart, axis=0, keepdims=True)
        n = stats.shape[0]
        stats[:, h : h + 1, :] = jnp.broadcast_to(mean[None], (n, 1, LANES))
        stats[:, 2 + h : 3 + h, :] = jnp.broadcast_to(square[None], (n, 1, LANES))


def bn_kernel(conv, stats, par, out):
    n, frames = stats.shape[0], conv.shape[0]
    s = stats[...]
    total = jnp.sum(s, axis=0)
    mean = total * (1.0 / n)
    apart = s - mean[None]
    apart = jnp.sum(apart * apart, axis=0)
    for h in range(2):
        cols = slice(LANES * h, LANES * (h + 1))
        square = total[2 + h : 3 + h] + frames * apart[h : h + 1]
        scale = lax.rsqrt(square * (1.0 / (n * frames)) + EPS) * par[0:1, cols]
        value = (conv[:, cols] - mean[h : h + 1]) * scale + par[1:2, cols]
        out[cols, :] = (value * jax.nn.sigmoid(value)).T.astype(BF)


def place_blocks(place, own, across, beside, far, whole):
    core, xhi = place[0], place[1]
    nz, half = 8, 256
    for blk, c, x in ((own, core, xhi), (across, core, 1 - xhi)):
        for z in range(nz):
            row = x * 512 + 64 * z + 32 * c
            whole[at(row, 32, 32), :] = blk[32 * z : 32 * z + 32, :]
    for blk, c, x in ((beside, 1 - core, xhi), (far, 1 - core, 1 - xhi)):
        for z in range(nz):
            row = x * 512 + 64 * z + 32 * c
            whole[at(row, 32, 32), :half] = blk[32 * z : 32 * z + 32, half:]
            whole[at(row, 32, 32), half:] = blk[32 * z : 32 * z + 32, :half]


def mix_kernel(place, own, across, beside, far, weight, res, out, whole):
    place_blocks(place, own, across, beside, far, whole)
    w = weight[...].reshape(256, weight.shape[2])
    mixed = jnp.dot(w, whole[...], preferred_element_type=F32)
    out[...] = (res[...].astype(F32) + mixed).astype(BF)


def ff_kernel(
    place, own, across, beside, far, weights, gain,
    keep, give, res,
    whole, normed, hidden, w, sem,
):
    copy = pltpu.make_async_copy(weights, w, sem)
    copy.start()
    place_blocks(place, own, across, beside, far, whole)
    half = 256
    res[...] = whole[at(place[1] * 512, 512, 512), :half]
    for c in range(2):
        cols = slice(half * c, half * (c + 1))
        normed[:, cols] = norm_rows(whole[:, cols].astype(F32), gain[...])
    copy.wait()
    for z in range(0, 8, 2):
        rows = [jnp.concatenate([w[z + i, k] for k in range(8)], axis=1) for i in range(2)]
        value = jnp.dot(
            jnp.concatenate(rows, axis=0), normed[...], preferred_element_type=F32
        )
        hidden[LANES * z : LANES * (z + 2), :] = (value * jax.nn.sigmoid(value)).astype(BF)
    for k in range(0, 8, 2):
        rows = [jnp.concatenate([w[z, 8 + k + i] for z in range(8)], axis=1) for i in range(2)]
        value = jnp.dot(
            jnp.concatenate(rows, axis=0), hidden[...], preferred_element_type=F32
        )
        keep[LANES * k : LANES * (k + 2), :] = value[:, :half]
        give[LANES * k : LANES * (k + 2), :] = value[:, half:].astype(BF)


def body(
    tokens,
    ln_conv_gain,
    glu_weight,
    depth_weight,
    bn_gain,
    bn_shift,
    conv_out_weight,
    ln_ff_gain,
    ff_in_weight,
    ff_out_weight,
):
    core, xhi = (lax.axis_index(CORE), lax.axis_index(XHI))
    place = jnp.stack([core, xhi]).astype(jnp.int32)
    nz = lax.axis_size(Z)
    frames, width = tokens.shape
    full = ln_conv_gain.shape[0]
    half = width // 2
    run = frames // nz

    def mine(x, axis, size):
        return lax.dynamic_slice_in_dim(x, core * size, size, axis=axis)

    glu = mine(glu_weight.transpose(1, 2, 0), 1, half).reshape(2 * half, full)
    conv_out = mine(conv_out_weight.T, 0, half)
    small = jnp.concatenate([depth_weight, bn_gain[None], bn_shift[None]], axis=0)
    small = mine(small.T, 0, half)
    small = jnp.pad(small, ((0, 0), (0, LANES - small.shape[1])))
    small = [p[16 * i : 16 * i + 16] for p in split3(small) for i in range(2)]
    small = jnp.pad(jnp.concatenate(small, axis=1), ((0, 0), (0, full - 6 * LANES)))
    first = lax.all_gather(jnp.concatenate([glu, conv_out, small], axis=0), Z)

    tok = tokens.T
    tm = lax.axis_size((XLO, Y, CORE))
    up = [(i, i + 1) for i in range(tm - 1)]
    left = lax.ppermute(tok[:, frames - LANES :], (XLO, Y, CORE), up)
    right = lax.ppermute(tok[:, :LANES], (XLO, Y, CORE), [(j, i) for i, j in up])
    parts = pl.pallas_call(
        pack_kernel,
        out_shape=shape((nz, 144, LANES), BF),
        in_specs=[VMEM] * 3,
        out_specs=VMEM,
        compiler_params=PARAMS,
        name="pack",
    )(tok, left, right)
    parts = lax.all_to_all(parts, Z, 0, 0, tiled=True)

    ff_in_weight, ff_out_weight, parts = lax.optimization_barrier(
        (ff_in_weight, ff_out_weight, parts)
    )
    ff_in = mine(ff_in_weight, 1, LANES).reshape(8, LANES, LANES).transpose(0, 2, 1)
    ff_out = mine(ff_out_weight, 0, LANES).reshape(LANES, 8, LANES).transpose(1, 2, 0)
    second = lax.all_gather(jnp.concatenate([ff_in, ff_out], axis=0), Z)

    whole = group_gather(parts)
    peers = lax.axis_size((XLO, Y, Z))
    conv, stats, par, res = pl.pallas_call(
        conv_kernel,
        out_shape=(
            shape((2 * run, 256), F32),
            shape((peers, 4, LANES), F32),
            shape((8, 256), F32),
            shape((256, 2 * run), BF),
        ),
        grid=(1,),
        in_specs=[SMEM]
        + [VMEM] * 4
        + [
            pl.BlockSpec((nz, 64, full), lambda i: (0, 0, 0)),
            pl.BlockSpec((nz, 16, full), lambda i: (0, 6, 0)),
            VMEM,
        ],
        out_specs=(VMEM,) * 4,
        scratch_shapes=[
            pltpu.VMEM((full, 2 * run), BF),
            pltpu.VMEM((full, LANES), F32),
            pltpu.VMEM((2, run + 40, 256), F32),
            pltpu.VMEM((256, LANES), F32),
        ],
        compiler_params=PARAMS,
        name="conv",
    )(place, *whole, first, first, ln_conv_gain[:, None])
    stats = lax.all_to_all(stats, (XLO, Y, Z), 0, 0, tiled=True)
    activated = pl.pallas_call(
        bn_kernel,
        out_shape=shape((256, 2 * run), BF),
        in_specs=[VMEM] * 3,
        out_specs=VMEM,
        compiler_params=PARAMS,
        name="bn",
    )(conv, stats, par)
    block = pl.pallas_call(
        mix_kernel,
        out_shape=shape((256, 2 * run), BF),
        grid=(1,),
        in_specs=[SMEM]
        + [VMEM] * 4
        + [pl.BlockSpec((nz, 32, full), lambda i: (0, 2, 0)), VMEM],
        out_specs=VMEM,
        scratch_shapes=[pltpu.VMEM((full, 2 * run), BF)],
        compiler_params=PARAMS,
        name="mix",
    )(place, *group_gather(activated), first, res)
    keep, give, res = pl.pallas_call(
        ff_kernel,
        out_shape=(
            shape((full, run), F32),
            shape((full, run), BF),
            shape((full // 2, run), BF),
        ),
        in_specs=[SMEM] + [VMEM] * 4 + [ANY, VMEM],
        out_specs=(VMEM,) * 3,
        scratch_shapes=[
            pltpu.VMEM((full, 2 * run), BF),
            pltpu.VMEM((full, 2 * run), BF),
            pltpu.VMEM((full, 2 * run), BF),
            pltpu.VMEM((8, 16, LANES, LANES), BF),
            pltpu.SemaphoreType.DMA,
        ],
        compiler_params=PARAMS,
        name="ff",
    )(place, *group_gather(block), second, ln_ff_gain[:, None])
    other = swap(give, CORE)
    size = full // 2

    def part(x, index):
        return lax.dynamic_slice_in_dim(x, index * size, size, axis=0).astype(F32)

    give = (part(keep, 1 - xhi) + part(other, 1 - xhi)).astype(BF)
    keep = part(keep, xhi) + part(other, xhi) + swap(give, XHI).astype(F32)
    out = (res.astype(F32) + 0.5 * keep).astype(BF)
    out = lax.all_to_all(out.reshape(nz, width, run), Z, 0, 0, tiled=True)
    return out.transpose(1, 0, 2).reshape(width, frames).T


def solution(mesh):
    fine = Mesh(mesh.devices.reshape(2, 8, 2, 2, 8), (XLO, Y, CORE, XHI, Z))
    tm, mp = ((XLO, Y, CORE), (XHI, Z))
    in_specs = (
        P(tm, mp),
        P(),
        P(None, None, mp),
        P(None, mp),
        P(mp),
        P(mp),
        P(None, mp),
        P(),
        P(None, mp),
        P(mp, None),
    )
    return jax.shard_map(body, mesh=fine, in_specs=in_specs, out_specs=P(tm, mp), check_vma=False)
```

```python
import jax
import jax.numpy as jnp
from jax import lax
from jax.experimental import pallas as pl
from jax.experimental.pallas import tpu as pltpu
from jax.sharding import Mesh, PartitionSpec as P

XLO, Y, CORE, XHI, Z = ("xlo", "y", "core", "xhi", "z")
BF, F32 = (jnp.bfloat16, jnp.float32)
EPS = 1e-05
LANES = 128
SPAN = 15
VMEM = pl.BlockSpec(memory_space=pltpu.VMEM)
SMEM = pl.BlockSpec(memory_space=pltpu.SMEM)
ANY = pl.BlockSpec(memory_space=pl.ANY)
PARAMS = pltpu.CompilerParams(vmem_limit_bytes=40 << 20)


def shape(dims, dtype):
    return jax.ShapeDtypeStruct(dims, dtype)


def swap(x, axis):
    return lax.ppermute(x, axis, [(0, 1), (1, 0)])


def group_gather(x):
    across = swap(x, XHI)
    beside = swap(x, CORE)
    return x, across, beside, swap(across, CORE)


def norm_rows(x, gain):
    inv = 1.0 / x.shape[0]
    centred = x - jnp.sum(x, axis=0, keepdims=True) * inv
    spread = jnp.sum(centred * centred, axis=0, keepdims=True) * inv
    return (centred * lax.rsqrt(spread + EPS) * gain).astype(BF)


def at(start, size, step):
    return pl.ds(pl.multiple_of(start, step), size)


def weight_kernel(place, glu, depth, gain, shift, out, table):
    core = place[0]
    lane = lax.broadcasted_iota(jnp.int32, table.shape, 1)
    table[...] = jnp.zeros_like(table)
    width, taps = depth.shape[1], depth.shape[0]
    table[0:taps, 0:width] = depth[...]
    table[taps : taps + 1, 0:width] = gain[...]
    table[taps + 1 : taps + 2, 0:width] = shift[...]
    rest = jnp.where(core == 0, table[...], pltpu.roll(table[...], LANES - 32, 1))
    rest = jnp.where(lane < 32, rest, 0.0)
    packed = jnp.zeros_like(rest)
    for i in range(3):
        piece = rest.astype(BF).astype(F32)
        packed = packed + (piece if i == 0 else pltpu.roll(piece, 32 * i, 1))
        rest = rest - piece
    nz = out.shape[0]
    for k in range(8):
        for v in range(2):
            tile = glu[v, at(32 * core, 32, 32), LANES * k : LANES * (k + 1)]
            for z in range(nz):
                out[z, 64 * k + 32 * v : 64 * k + 32 * v + 32] = tile
    for z in range(nz):
        out[z, 512:560] = packed.astype(BF)


def block_kernel(place, ff_in, ff_out, conv_out, out):
    half = at(place[0] * LANES, LANES, LANES)
    for k in range(8):
        tile = slice(LANES * k, LANES * (k + 1))
        out[k] = ff_in[tile, half].astype(F32).T.astype(BF)
        out[8 + k] = ff_out[half, tile].astype(F32).T.astype(BF)
        rows = slice(32 * (k % 4), 32 * (k % 4) + 32)
        out[16 + k // 4, rows, :] = conv_out[at(place[0] * 32, 32, 32), tile]


def pack_kernel(tok, left, right, out):
    lane = lax.broadcasted_iota(jnp.int32, (16, LANES), 1)
    nz = out.shape[0]
    for z in range(nz):
        out[z, 0:64] = tok[:, 2 * z * LANES : (2 * z + 1) * LANES]
        out[z, 64:128] = tok[:, (2 * z + 1) * LANES : (2 * z + 2) * LANES]
        packed = jnp.zeros((16, LANES), F32)
        for i in range(4):
            rows = slice(16 * i, 16 * i + 16)
            if z == 0:
                before = left[rows]
            else:
                before = tok[rows, (2 * z - 1) * LANES : 2 * z * LANES]
            if z == nz - 1:
                after = right[rows]
            else:
                after = tok[rows, (2 * z + 2) * LANES : (2 * z + 3) * LANES]
            low = pltpu.roll(before.astype(F32), (32 * i + SPAN) % LANES, 1)
            high = pltpu.roll(after.astype(F32), 32 * i + SPAN, 1)
            packed = jnp.where((lane >= 32 * i) & (lane < 32 * i + SPAN), low, packed)
            packed = jnp.where(
                (lane >= 32 * i + SPAN) & (lane < 32 * i + 2 * SPAN), high, packed
            )
        out[z, 128:144] = packed.astype(BF)


def conv_kernel(
    place, own, across, beside, far, glu, gain,
    conv, stats, par, res,
    tok, edge, win, weight,
):
    core, xhi = place[0], place[1]
    lane = lax.broadcasted_iota(jnp.int32, (16, LANES), 1)
    nz = glu.shape[0]
    for near, away, side in ((own, beside, xhi), (across, far, 1 - xhi)):
        for z in range(nz):
            row = side * (64 * nz) + 64 * z
            for c, blk in ((0, near), (1, away)):
                tok[at(row, 64, 64), 256 * c : 256 * c + 128] = blk[z, 0:64]
                tok[at(row, 64, 64), 256 * c + 128 : 256 * c + 256] = blk[z, 64:128]
            one = near[z, 128:144].astype(F32)
            two = away[z, 128:144].astype(F32)
            for i in range(4):
                low = pltpu.roll(one, (LANES - 32 * i) % LANES, 1)
                high = pltpu.roll(two, (LANES + 32 - 32 * i) % LANES, 1)
                part = jnp.where(lane < 32, low, jnp.where(lane < 64, high, 0.0))
                edge[at(row + 16 * i, 16, 16), :] = part
    for z in range(nz):
        row = xhi * (64 * nz) + 64 * z + 32 * core
        res[32 * z : 32 * z + 32, :] = tok[at(row, 32, 32), :]

    table = []
    lane = lax.broadcasted_iota(jnp.int32, (48, LANES), 1)
    for h in range(2):
        total = jnp.zeros((48, LANES), F32)
        for i in range(4):
            x = glu[4 * h + i, 512:560].astype(F32)
            x = x + (pltpu.roll(x, LANES - 32, 1) + pltpu.roll(x, LANES - 64, 1))
            x = jnp.where(lane < 32, x, 0.0)
            total = total + (x if i == 0 else pltpu.roll(x, 32 * i, 1))
        par[:, LANES * h : LANES * (h + 1)] = total[31:39]
        table.append(total)
    for z in range(nz):
        for k in range(8):
            weight[64 * z : 64 * z + 64, LANES * k : LANES * (k + 1)] = glu[z, 64 * k : 64 * k + 64]

    scale = gain[...]
    for c in range(3):
        x = edge[...] if c == 2 else tok[:, 256 * c : 256 * (c + 1)].astype(F32)
        paired = jnp.dot(weight[...], norm_rows(x, scale), preferred_element_type=F32)
        cols = x.shape[1]
        paired = paired.reshape(nz, 2, 32, cols)
        gated = (paired[:, 0] * jax.nn.sigmoid(paired[:, 1])).astype(BF).astype(F32)
        gated = gated.reshape(32 * nz, cols).T
        if c < 2:
            win[c, 16:272, :] = gated
        else:
            for r in range(2):
                win[r, 1:16, :] = gated[32 * r : 32 * r + 15]
                win[r, 272:287, :] = gated[32 * r + 15 : 32 * r + 30]

    step = 64
    for h in range(2):
        cols = slice(LANES * h, LANES * (h + 1))
        total = jnp.zeros((1, LANES), F32)
        for r in range(2):
            for k in range(256 // step):
                acc = jnp.zeros((step, LANES), F32)
                for j in range(31):
                    first = step * k + 1 + j
                    acc = acc + table[h][j : j + 1] * win[r, first : first + step, cols]
                conv[256 * r + step * k : 256 * r + step * (k + 1), cols] = acc
                total = total + jnp.sum(acc, axis=0, keepdims=True)
        mean = total * (1.0 / 512)
        apart = conv[:, cols] - mean
        square = jnp.sum(apart * apart, axis=0, keepdims=True)
        n = stats.shape[0]
        stats[:, h : h + 1, :] = jnp.broadcast_to(mean[None], (n, 1, LANES))
        stats[:, 2 + h : 3 + h, :] = jnp.broadcast_to(square[None], (n, 1, LANES))


def bn_kernel(conv, stats, par, out):
    n, frames = stats.shape[0], conv.shape[0]
    s = stats[...]
    total = jnp.sum(s, axis=0)
    mean = total * (1.0 / n)
    apart = s - mean[None]
    apart = jnp.sum(apart * apart, axis=0)
    for h in range(2):
        cols = slice(LANES * h, LANES * (h + 1))
        square = total[2 + h : 3 + h] + frames * apart[h : h + 1]
        scale = lax.rsqrt(square * (1.0 / (n * frames)) + EPS) * par[0:1, cols]
        value = (conv[:, cols] - mean[h : h + 1]) * scale + par[1:2, cols]
        out[cols, :] = (value * jax.nn.sigmoid(value)).T.astype(BF)


def place_blocks(place, own, across, beside, far, whole):
    core, xhi = place[0], place[1]
    nz, half = 8, 256
    for blk, c, x in ((own, core, xhi), (across, core, 1 - xhi)):
        for z in range(nz):
            row = x * 512 + 64 * z + 32 * c
            whole[at(row, 32, 32), :] = blk[32 * z : 32 * z + 32, :]
    for blk, c, x in ((beside, 1 - core, xhi), (far, 1 - core, 1 - xhi)):
        for z in range(nz):
            row = x * 512 + 64 * z + 32 * c
            whole[at(row, 32, 32), :half] = blk[32 * z : 32 * z + 32, half:]
            whole[at(row, 32, 32), half:] = blk[32 * z : 32 * z + 32, :half]


def mix_kernel(place, own, across, beside, far, blocks, res, out, whole, weight):
    place_blocks(place, own, across, beside, far, whole)
    for z in range(8):
        for k in range(8):
            rows = slice(32 * (k % 4), 32 * (k % 4) + 32)
            weight[32 * z : 32 * z + 32, LANES * k : LANES * (k + 1)] = blocks[z, k // 4, rows, :]
    mixed = jnp.dot(weight[...], whole[...], preferred_element_type=F32)
    out[...] = (res[...].astype(F32) + mixed).astype(BF)


def ff_kernel(
    place, own, across, beside, far, weights, gain,
    keep, give,
    whole, normed, hidden, w, sem,
):
    copy = pltpu.make_async_copy(weights.at[:, 0:16], w, sem)
    copy.start()
    place_blocks(place, own, across, beside, far, whole)
    half = 256
    for c in range(2):
        cols = slice(half * c, half * (c + 1))
        normed[:, cols] = norm_rows(whole[:, cols].astype(F32), gain[...])
    copy.wait()
    for z in range(0, 8, 2):
        rows = [jnp.concatenate([w[z + i, k] for k in range(8)], axis=1) for i in range(2)]
        value = jnp.dot(
            jnp.concatenate(rows, axis=0), normed[...], preferred_element_type=F32
        )
        hidden[LANES * z : LANES * (z + 2), :] = (value * jax.nn.sigmoid(value)).astype(BF)
    for k in range(0, 8, 2):
        rows = [jnp.concatenate([w[z, 8 + k + i] for z in range(8)], axis=1) for i in range(2)]
        value = jnp.dot(
            jnp.concatenate(rows, axis=0), hidden[...], preferred_element_type=F32
        )
        rows = slice(LANES * k, LANES * (k + 2))
        mine = jnp.where(place[1] == k // 4, 1.0, 0.0)
        keep[rows, :] = 0.5 * value[:, :half] + mine * whole[rows, :half].astype(F32)
        give[rows, :] = (0.5 * value[:, half:]).astype(BF)


def body(
    tokens,
    ln_conv_gain,
    glu_weight,
    depth_weight,
    bn_gain,
    bn_shift,
    conv_out_weight,
    ln_ff_gain,
    ff_in_weight,
    ff_out_weight,
):
    core, xhi = (lax.axis_index(CORE), lax.axis_index(XHI))
    place = jnp.stack([core, xhi]).astype(jnp.int32)
    nz = lax.axis_size(Z)
    frames, width = tokens.shape
    full = ln_conv_gain.shape[0]
    run = frames // nz

    tok = tokens.T
    tm = lax.axis_size((XLO, Y, CORE))
    up = [(i, i + 1) for i in range(tm - 1)]
    left = lax.ppermute(tok[:, frames - LANES :], (XLO, Y, CORE), up)
    right = lax.ppermute(tok[:, :LANES], (XLO, Y, CORE), [(j, i) for i, j in up])
    glu = pl.pallas_call(
        weight_kernel,
        out_shape=shape((nz, 560, LANES), BF),
        in_specs=[SMEM] + [VMEM] * 4,
        out_specs=VMEM,
        scratch_shapes=[pltpu.VMEM((48, LANES), F32)],
        compiler_params=PARAMS,
        name="weights",
    )(place, glu_weight.transpose(1, 2, 0), depth_weight, bn_gain[None], bn_shift[None])
    parts = pl.pallas_call(
        pack_kernel,
        out_shape=shape((nz, 144, LANES), BF),
        in_specs=[VMEM] * 3,
        out_specs=VMEM,
        compiler_params=PARAMS,
        name="pack",
    )(tok, left, right)
    parts, glu = lax.optimization_barrier((parts, glu))
    parts = lax.all_to_all(parts, Z, 0, 0, tiled=True)
    glu = lax.all_to_all(glu, Z, 0, 0, tiled=True)

    blocks = pl.pallas_call(
        block_kernel,
        out_shape=shape((18, LANES, LANES), BF),
        in_specs=[SMEM] + [VMEM] * 3,
        out_specs=VMEM,
        compiler_params=PARAMS,
        name="blocks",
    )(place, ff_in_weight, ff_out_weight, conv_out_weight.T)
    blocks, parts = lax.optimization_barrier((blocks, parts))
    blocks = lax.all_gather(blocks, Z)

    whole = group_gather(parts)
    peers = lax.axis_size((XLO, Y, Z))
    conv, stats, par, res = pl.pallas_call(
        conv_kernel,
        out_shape=(
            shape((2 * run, 256), F32),
            shape((peers, 4, LANES), F32),
            shape((8, 256), F32),
            shape((256, 2 * run), BF),
        ),
        in_specs=[SMEM] + [VMEM] * 6,
        out_specs=(VMEM,) * 4,
        scratch_shapes=[
            pltpu.VMEM((full, 2 * run), BF),
            pltpu.VMEM((full, LANES), F32),
            pltpu.VMEM((2, run + 40, 256), F32),
            pltpu.VMEM((512, full), BF),
        ],
        compiler_params=PARAMS,
        name="conv",
    )(place, *whole, glu, ln_conv_gain[:, None])
    stats = lax.all_to_all(stats, (XLO, Y, Z), 0, 0, tiled=True)
    activated = pl.pallas_call(
        bn_kernel,
        out_shape=shape((256, 2 * run), BF),
        in_specs=[VMEM] * 3,
        out_specs=VMEM,
        compiler_params=PARAMS,
        name="bn",
    )(conv, stats, par)
    block = pl.pallas_call(
        mix_kernel,
        out_shape=shape((256, 2 * run), BF),
        grid=(1,),
        in_specs=[SMEM]
        + [VMEM] * 4
        + [pl.BlockSpec((nz, 2, LANES, LANES), lambda i: (0, 8, 0, 0)), VMEM],
        out_specs=VMEM,
        scratch_shapes=[pltpu.VMEM((full, 2 * run), BF), pltpu.VMEM((256, full), BF)],
        compiler_params=PARAMS,
        name="mix",
    )(place, *group_gather(activated), blocks, res)
    keep, give = pl.pallas_call(
        ff_kernel,
        out_shape=(shape((full, run), F32), shape((full, run), BF)),
        in_specs=[SMEM] + [VMEM] * 4 + [ANY, VMEM],
        out_specs=(VMEM,) * 2,
        scratch_shapes=[
            pltpu.VMEM((full, 2 * run), BF),
            pltpu.VMEM((full, 2 * run), BF),
            pltpu.VMEM((full, 2 * run), BF),
            pltpu.VMEM((8, 16, LANES, LANES), BF),
            pltpu.SemaphoreType.DMA,
        ],
        compiler_params=pltpu.CompilerParams(vmem_limit_bytes=58 << 20),
        name="ff",
    )(place, *group_gather(block), blocks, ln_ff_gain[:, None])
    keep = (keep + swap(give, CORE).astype(F32)).astype(BF)
    keep = lax.all_to_all(keep.reshape(2 * nz, width, run), (XHI, Z), 0, 0, tiled=True)
    out = (keep[:nz].astype(F32) + keep[nz:].astype(F32)).astype(BF)
    return out.transpose(1, 0, 2).reshape(width, frames).T


def solution(mesh):
    fine = Mesh(mesh.devices.reshape(2, 8, 2, 2, 8), (XLO, Y, CORE, XHI, Z))
    tm, mp = ((XLO, Y, CORE), (XHI, Z))
    in_specs = (
        P(tm, mp),
        P(),
        P(None, None, mp),
        P(None, mp),
        P(mp),
        P(mp),
        P(None, mp),
        P(),
        P(None, mp),
        P(mp, None),
    )
    return jax.shard_map(body, mesh=fine, in_specs=in_specs, out_specs=P(tm, mp), check_vma=False)
```

```python
import jax
import jax.numpy as jnp
from jax import lax
from jax.experimental import pallas as pl
from jax.experimental.pallas import tpu as pltpu
from jax.sharding import Mesh, PartitionSpec as P

XLO, Y, CORE, XHI, Z = ("xlo", "y", "core", "xhi", "z")
BF, F32 = (jnp.bfloat16, jnp.float32)
EPS = 1e-05
LANES = 128
SPAN = 15
VMEM = pl.BlockSpec(memory_space=pltpu.VMEM)
SMEM = pl.BlockSpec(memory_space=pltpu.SMEM)
PARAMS = pltpu.CompilerParams(vmem_limit_bytes=40 << 20)


def shape(dims, dtype):
    return jax.ShapeDtypeStruct(dims, dtype)


def swap(x, axis):
    return lax.ppermute(x, axis, [(0, 1), (1, 0)])


def group_gather(x):
    across = swap(x, XHI)
    beside = swap(x, CORE)
    return x, across, beside, swap(across, CORE)


def norm_rows(x, gain):
    inv = 1.0 / x.shape[0]
    centred = x - jnp.sum(x, axis=0, keepdims=True) * inv
    spread = jnp.sum(centred * centred, axis=0, keepdims=True) * inv
    return (centred * lax.rsqrt(spread + EPS) * gain).astype(BF)


def at(start, size, step):
    return pl.ds(pl.multiple_of(start, step), size)


def weight_kernel(place, glu, conv_out, depth, gain, shift, out, table):
    core = place[0]
    lane = lax.broadcasted_iota(jnp.int32, table.shape, 1)
    table[...] = jnp.zeros_like(table)
    width, taps = depth.shape[1], depth.shape[0]
    table[0:taps, 0:width] = depth[...]
    table[taps : taps + 1, 0:width] = gain[...]
    table[taps + 1 : taps + 2, 0:width] = shift[...]
    rest = jnp.where(core == 0, table[...], pltpu.roll(table[...], LANES - 32, 1))
    rest = jnp.where(lane < 32, rest, 0.0)
    packed = jnp.zeros_like(rest)
    for i in range(3):
        piece = rest.astype(BF).astype(F32)
        packed = packed + (piece if i == 0 else pltpu.roll(piece, 32 * i, 1))
        rest = rest - piece
    half = at(32 * core, 32, 32)
    for k in range(8):
        tile = slice(LANES * k, LANES * (k + 1))
        for v in range(2):
            out[64 * k + 32 * v : 64 * k + 32 * v + 32] = glu[v, half, tile]
        out[512 + 32 * k : 512 + 32 * k + 32] = conv_out[half, tile]
    out[768:816] = packed.astype(BF)


def block_kernel(place, ff_in, ff_out, out):
    half = at(place[0] * LANES, LANES, LANES)
    for k in range(8):
        tile = slice(LANES * k, LANES * (k + 1))
        out[k] = ff_in[tile, half].astype(F32).T.astype(BF)
        out[8 + k] = ff_out[half, tile].astype(F32).T.astype(BF)


def pack_kernel(tok, left, right, out):
    lane = lax.broadcasted_iota(jnp.int32, (16, LANES), 1)
    nz = out.shape[0]
    for z in range(nz):
        out[z, 0:64] = tok[:, 2 * z * LANES : (2 * z + 1) * LANES]
        out[z, 64:128] = tok[:, (2 * z + 1) * LANES : (2 * z + 2) * LANES]
        packed = jnp.zeros((16, LANES), F32)
        for i in range(4):
            rows = slice(16 * i, 16 * i + 16)
            if z == 0:
                before = left[rows]
            else:
                before = tok[rows, (2 * z - 1) * LANES : 2 * z * LANES]
            if z == nz - 1:
                after = right[rows]
            else:
                after = tok[rows, (2 * z + 2) * LANES : (2 * z + 3) * LANES]
            low = pltpu.roll(before.astype(F32), (32 * i + SPAN) % LANES, 1)
            high = pltpu.roll(after.astype(F32), 32 * i + SPAN, 1)
            packed = jnp.where((lane >= 32 * i) & (lane < 32 * i + SPAN), low, packed)
            packed = jnp.where(
                (lane >= 32 * i + SPAN) & (lane < 32 * i + 2 * SPAN), high, packed
            )
        out[z, 128:144] = packed.astype(BF)


def conv_kernel(
    place, own, across, beside, far, glu, small, gain,
    conv, stats, par, res,
    tok, edge, win, weight,
):
    core, xhi = place[0], place[1]
    lane = lax.broadcasted_iota(jnp.int32, (16, LANES), 1)
    nz = glu.shape[0]
    for near, away, side in ((own, beside, xhi), (across, far, 1 - xhi)):
        for z in range(nz):
            row = side * (64 * nz) + 64 * z
            for c, blk in ((0, near), (1, away)):
                tok[at(row, 64, 64), 256 * c : 256 * c + 128] = blk[z, 0:64]
                tok[at(row, 64, 64), 256 * c + 128 : 256 * c + 256] = blk[z, 64:128]
            one = near[z, 128:144].astype(F32)
            two = away[z, 128:144].astype(F32)
            for i in range(4):
                low = pltpu.roll(one, (LANES - 32 * i) % LANES, 1)
                high = pltpu.roll(two, (LANES + 32 - 32 * i) % LANES, 1)
                part = jnp.where(lane < 32, low, jnp.where(lane < 64, high, 0.0))
                edge[at(row + 16 * i, 16, 16), :] = part
    for z in range(nz):
        row = xhi * (64 * nz) + 64 * z + 32 * core
        res[32 * z : 32 * z + 32, :] = tok[at(row, 32, 32), :]

    table = []
    lane = lax.broadcasted_iota(jnp.int32, (48, LANES), 1)
    for h in range(2):
        total = jnp.zeros((48, LANES), F32)
        for i in range(4):
            x = small[4 * h + i].astype(F32)
            x = x + (pltpu.roll(x, LANES - 32, 1) + pltpu.roll(x, LANES - 64, 1))
            x = jnp.where(lane < 32, x, 0.0)
            total = total + (x if i == 0 else pltpu.roll(x, 32 * i, 1))
        par[:, LANES * h : LANES * (h + 1)] = total[31:39]
        table.append(total)
    for z in range(nz):
        for k in range(8):
            weight[64 * z : 64 * z + 64, LANES * k : LANES * (k + 1)] = glu[z, 64 * k : 64 * k + 64]

    scale = gain[...]
    for c in range(3):
        x = edge[...] if c == 2 else tok[:, 256 * c : 256 * (c + 1)].astype(F32)
        paired = jnp.dot(weight[...], norm_rows(x, scale), preferred_element_type=F32)
        cols = x.shape[1]
        paired = paired.reshape(nz, 2, 32, cols)
        gated = (paired[:, 0] * jax.nn.sigmoid(paired[:, 1])).astype(BF).astype(F32)
        gated = gated.reshape(32 * nz, cols).T
        if c < 2:
            win[c, 16:272, :] = gated
        else:
            for r in range(2):
                win[r, 1:16, :] = gated[32 * r : 32 * r + 15]
                win[r, 272:287, :] = gated[32 * r + 15 : 32 * r + 30]

    step = 64
    for h in range(2):
        cols = slice(LANES * h, LANES * (h + 1))
        total = jnp.zeros((1, LANES), F32)
        for r in range(2):
            for k in range(256 // step):
                acc = jnp.zeros((step, LANES), F32)
                for j in range(31):
                    first = step * k + 1 + j
                    acc = acc + table[h][j : j + 1] * win[r, first : first + step, cols]
                conv[256 * r + step * k : 256 * r + step * (k + 1), cols] = acc
                total = total + jnp.sum(acc, axis=0, keepdims=True)
        mean = total * (1.0 / 512)
        apart = conv[:, cols] - mean
        square = jnp.sum(apart * apart, axis=0, keepdims=True)
        n = stats.shape[0]
        stats[:, h : h + 1, :] = jnp.broadcast_to(mean[None], (n, 1, LANES))
        stats[:, 2 + h : 3 + h, :] = jnp.broadcast_to(square[None], (n, 1, LANES))


def bn_kernel(conv, stats, par, out):
    n, frames = stats.shape[0], conv.shape[0]
    s = stats[...]
    total = jnp.sum(s, axis=0)
    mean = total * (1.0 / n)
    apart = s - mean[None]
    apart = jnp.sum(apart * apart, axis=0)
    for h in range(2):
        cols = slice(LANES * h, LANES * (h + 1))
        square = total[2 + h : 3 + h] + frames * apart[h : h + 1]
        scale = lax.rsqrt(square * (1.0 / (n * frames)) + EPS) * par[0:1, cols]
        value = (conv[:, cols] - mean[h : h + 1]) * scale + par[1:2, cols]
        out[cols, :] = (value * jax.nn.sigmoid(value)).T.astype(BF)


def place_blocks(place, own, across, beside, far, whole):
    core, xhi = place[0], place[1]
    nz, half = 8, 256
    for blk, c, x in ((own, core, xhi), (across, core, 1 - xhi)):
        for z in range(nz):
            row = x * 512 + 64 * z + 32 * c
            whole[at(row, 32, 32), :] = blk[32 * z : 32 * z + 32, :]
    for blk, c, x in ((beside, 1 - core, xhi), (far, 1 - core, 1 - xhi)):
        for z in range(nz):
            row = x * 512 + 64 * z + 32 * c
            whole[at(row, 32, 32), :half] = blk[32 * z : 32 * z + 32, half:]
            whole[at(row, 32, 32), half:] = blk[32 * z : 32 * z + 32, :half]


def mix_kernel(place, own, across, beside, far, blocks, res, out, whole, weight):
    place_blocks(place, own, across, beside, far, whole)
    for z in range(8):
        for k in range(8):
            tile = slice(LANES * k, LANES * (k + 1))
            weight[32 * z : 32 * z + 32, tile] = blocks[z, 32 * k : 32 * k + 32]
    mixed = jnp.dot(weight[...], whole[...], preferred_element_type=F32)
    out[...] = (res[...].astype(F32) + mixed).astype(BF)


def ff_kernel(
    place, own, across, beside, far, w, gain,
    keep, give,
    whole, normed, hidden,
):
    place_blocks(place, own, across, beside, far, whole)
    half = 256
    for c in range(2):
        cols = slice(half * c, half * (c + 1))
        normed[:, cols] = norm_rows(whole[:, cols].astype(F32), gain[...])
    for z in range(0, 8, 2):
        rows = [jnp.concatenate([w[z + i, k] for k in range(8)], axis=1) for i in range(2)]
        value = jnp.dot(
            jnp.concatenate(rows, axis=0), normed[...], preferred_element_type=F32
        )
        hidden[LANES * z : LANES * (z + 2), :] = (value * jax.nn.sigmoid(value)).astype(BF)
    for k in range(0, 8, 2):
        rows = [jnp.concatenate([w[z, 8 + k + i] for z in range(8)], axis=1) for i in range(2)]
        value = jnp.dot(
            jnp.concatenate(rows, axis=0), hidden[...], preferred_element_type=F32
        )
        rows = slice(LANES * k, LANES * (k + 2))
        mine = jnp.where(place[1] == k // 4, 1.0, 0.0)
        keep[rows, :] = 0.5 * value[:, :half] + mine * whole[rows, :half].astype(F32)
        give[rows, :] = (0.5 * value[:, half:]).astype(BF)


def sum_kernel(parts, out):
    nz, run = parts.shape[0] // 2, parts.shape[2]
    for z in range(nz):
        value = parts[z].astype(F32) + parts[nz + z].astype(F32)
        out[:, run * z : run * (z + 1)] = value.astype(BF)


def body(
    tokens,
    ln_conv_gain,
    glu_weight,
    depth_weight,
    bn_gain,
    bn_shift,
    conv_out_weight,
    ln_ff_gain,
    ff_in_weight,
    ff_out_weight,
):
    core, xhi = (lax.axis_index(CORE), lax.axis_index(XHI))
    place = jnp.stack([core, xhi]).astype(jnp.int32)
    nz = lax.axis_size(Z)
    frames, width = tokens.shape
    full = ln_conv_gain.shape[0]
    run = frames // nz

    first = pl.pallas_call(
        weight_kernel,
        out_shape=shape((816, LANES), BF),
        in_specs=[SMEM] + [VMEM] * 5,
        out_specs=VMEM,
        scratch_shapes=[pltpu.VMEM((48, LANES), F32)],
        compiler_params=PARAMS,
        name="weights",
    )(
        place,
        glu_weight.transpose(1, 2, 0),
        conv_out_weight.T,
        depth_weight,
        bn_gain[None],
        bn_shift[None],
    )
    first, tokens = lax.optimization_barrier((first, tokens))
    first = lax.all_gather(first, Z)

    tok = tokens.T
    tm = lax.axis_size((XLO, Y, CORE))
    up = [(i, i + 1) for i in range(tm - 1)]
    left = lax.ppermute(tok[:, frames - LANES :], (XLO, Y, CORE), up)
    right = lax.ppermute(tok[:, :LANES], (XLO, Y, CORE), [(j, i) for i, j in up])
    parts = pl.pallas_call(
        pack_kernel,
        out_shape=shape((nz, 144, LANES), BF),
        in_specs=[VMEM] * 3,
        out_specs=VMEM,
        compiler_params=PARAMS,
        name="pack",
    )(tok, left, right)
    parts = lax.all_to_all(parts, Z, 0, 0, tiled=True)

    blocks = pl.pallas_call(
        block_kernel,
        out_shape=shape((16, LANES, LANES), BF),
        in_specs=[SMEM] + [VMEM] * 2,
        out_specs=VMEM,
        compiler_params=PARAMS,
        name="blocks",
    )(place, ff_in_weight, ff_out_weight)
    blocks, parts = lax.optimization_barrier((blocks, parts))
    blocks = lax.all_gather(blocks, Z)

    whole = group_gather(parts)
    peers = lax.axis_size((XLO, Y, Z))
    conv, stats, par, res = pl.pallas_call(
        conv_kernel,
        out_shape=(
            shape((2 * run, 256), F32),
            shape((peers, 4, LANES), F32),
            shape((8, 256), F32),
            shape((256, 2 * run), BF),
        ),
        grid=(1,),
        in_specs=[SMEM]
        + [VMEM] * 4
        + [
            pl.BlockSpec((nz, 512, LANES), lambda i: (0, 0, 0)),
            pl.BlockSpec((nz, 48, LANES), lambda i: (0, 16, 0)),
            VMEM,
        ],
        out_specs=(VMEM,) * 4,
        scratch_shapes=[
            pltpu.VMEM((full, 2 * run), BF),
            pltpu.VMEM((full, LANES), F32),
            pltpu.VMEM((2, run + 40, 256), F32),
            pltpu.VMEM((512, full), BF),
        ],
        compiler_params=PARAMS,
        name="conv",
    )(place, *whole, first, first, ln_conv_gain[:, None])
    stats = lax.all_to_all(stats, (XLO, Y, Z), 0, 0, tiled=True)
    activated = pl.pallas_call(
        bn_kernel,
        out_shape=shape((256, 2 * run), BF),
        in_specs=[VMEM] * 3,
        out_specs=VMEM,
        compiler_params=PARAMS,
        name="bn",
    )(conv, stats, par)
    block = pl.pallas_call(
        mix_kernel,
        out_shape=shape((256, 2 * run), BF),
        grid=(1,),
        in_specs=[SMEM]
        + [VMEM] * 4
        + [pl.BlockSpec((nz, 256, LANES), lambda i: (0, 2, 0)), VMEM],
        out_specs=VMEM,
        scratch_shapes=[pltpu.VMEM((full, 2 * run), BF), pltpu.VMEM((256, full), BF)],
        compiler_params=PARAMS,
        name="mix",
    )(place, *group_gather(activated), first, res)
    keep, give = pl.pallas_call(
        ff_kernel,
        out_shape=(shape((full, run), F32), shape((full, run), BF)),
        in_specs=[SMEM] + [VMEM] * 6,
        out_specs=(VMEM,) * 2,
        scratch_shapes=[
            pltpu.VMEM((full, 2 * run), BF),
            pltpu.VMEM((full, 2 * run), BF),
            pltpu.VMEM((full, 2 * run), BF),
        ],
        compiler_params=PARAMS,
        name="ff",
    )(place, *group_gather(block), blocks, ln_ff_gain[:, None])
    keep = (keep + swap(give, CORE).astype(F32)).astype(BF)
    keep = lax.all_to_all(keep.reshape(2 * nz, width, run), (XHI, Z), 0, 0, tiled=True)
    out = pl.pallas_call(
        sum_kernel,
        out_shape=shape((width, frames), BF),
        in_specs=[VMEM],
        out_specs=VMEM,
        compiler_params=PARAMS,
        name="sum",
    )(keep)
    return out.T


def solution(mesh):
    fine = Mesh(mesh.devices.reshape(2, 8, 2, 2, 8), (XLO, Y, CORE, XHI, Z))
    tm, mp = ((XLO, Y, CORE), (XHI, Z))
    in_specs = (
        P(tm, mp),
        P(),
        P(None, None, mp),
        P(None, mp),
        P(mp),
        P(mp),
        P(None, mp),
        P(),
        P(None, mp),
        P(mp, None),
    )
    return jax.shard_map(body, mesh=fine, in_specs=in_specs, out_specs=P(tm, mp), check_vma=False)
```

```python
import jax
import jax.numpy as jnp
from jax import lax
from jax.experimental import pallas as pl
from jax.experimental.pallas import tpu as pltpu
from jax.sharding import Mesh, PartitionSpec as P

XLO, Y, CORE, XHI, Z = ("xlo", "y", "core", "xhi", "z")
BF, F32 = (jnp.bfloat16, jnp.float32)
EPS = 1e-05
LANES = 128
SPAN = 15
VMEM = pl.BlockSpec(memory_space=pltpu.VMEM)
HBM = pl.BlockSpec(memory_space=pltpu.HBM)
PARAMS = pltpu.CompilerParams(vmem_limit_bytes=40 << 20)


def shape(dims, dtype):
    return jax.ShapeDtypeStruct(dims, dtype)


def in_hbm(*arrays):
    return [pltpu.with_memory_space_constraint(x, pltpu.HBM) for x in arrays]


def swap(x, axis):
    return lax.ppermute(x, axis, [(0, 1), (1, 0)])


def group_gather(x):
    across = swap(x, XHI)
    beside = swap(x, CORE)
    return x, across, beside, swap(across, CORE)


def norm_rows(x, gain):
    inv = 1.0 / x.shape[0]
    centred = x - jnp.sum(x, axis=0, keepdims=True) * inv
    spread = jnp.sum(centred * centred, axis=0, keepdims=True) * inv
    return (centred * lax.rsqrt(spread + EPS) * gain).astype(BF)


def place():
    return lax.axis_index(CORE), lax.axis_index(XHI)


def at(start, size, step):
    return pl.ds(pl.multiple_of(start, step), size)


def weight_kernel(
    glu, conv_out, depth, gain, shift, tok,
    out, near, first, last,
    table, parts, small, sems,
):
    core, _ = place()
    half = at(32 * core, 32, 32)
    taps, width = depth.shape
    loads = [
        pltpu.make_async_copy(depth, small.at[0:taps], sems.at[0]),
        pltpu.make_async_copy(gain, small.at[32:33], sems.at[1]),
        pltpu.make_async_copy(shift, small.at[40:41], sems.at[2]),
    ]
    stores = []
    for k in range(8):
        tile = slice(LANES * k, LANES * (k + 1))
        for v in range(2):
            stores.append((glu.at[v, half, tile], 64 * k + 32 * v))
        stores.append((conv_out.at[half, tile], 512 + 32 * k))
    stores = [
        pltpu.make_async_copy(ref, out.at[row : row + 32], sems.at[4 + i])
        for i, (ref, row) in enumerate(stores)
    ]
    frames = tok.shape[1]
    stores += [
        pltpu.make_async_copy(tok.at[:, 0:LANES], first, sems.at[28]),
        pltpu.make_async_copy(tok.at[:, frames - LANES : frames], last, sems.at[29]),
        pltpu.make_async_copy(tok, near, sems.at[30]),
    ]
    for copy in loads + stores:
        copy.start()
    table[...] = jnp.zeros_like(table)
    for copy in loads:
        copy.wait()
    table[0:taps, 0:width] = small[0:taps]
    table[taps : taps + 1, 0:width] = small[32:33]
    table[taps + 1 : taps + 2, 0:width] = small[40:41]
    lane = lax.broadcasted_iota(jnp.int32, table.shape, 1)
    rest = jnp.where(core == 0, table[...], pltpu.roll(table[...], LANES - 32, 1))
    rest = jnp.where(lane < 32, rest, 0.0)
    packed = jnp.zeros_like(rest)
    for i in range(3):
        piece = rest.astype(BF).astype(F32)
        packed = packed + (piece if i == 0 else pltpu.roll(piece, 32 * i, 1))
        rest = rest - piece
    parts[...] = packed.astype(BF)
    final = pltpu.make_async_copy(parts, out.at[768:816], sems.at[3])
    final.start()
    for copy in stores + [final]:
        copy.wait()


def block_kernel(ff_in, ff_out, out):
    half = at(place()[0] * LANES, LANES, LANES)
    for k in range(8):
        tile = slice(LANES * k, LANES * (k + 1))
        out[k] = ff_in[tile, half].astype(F32).T.astype(BF)
        out[8 + k] = ff_out[half, tile].astype(F32).T.astype(BF)


def pack_kernel(tok, left, right, out):
    lane = lax.broadcasted_iota(jnp.int32, (16, LANES), 1)
    nz = out.shape[0]
    for z in range(nz):
        out[z, 0:64] = tok[:, 2 * z * LANES : (2 * z + 1) * LANES]
        out[z, 64:128] = tok[:, (2 * z + 1) * LANES : (2 * z + 2) * LANES]
        packed = jnp.zeros((16, LANES), F32)
        for i in range(4):
            rows = slice(16 * i, 16 * i + 16)
            if z == 0:
                before = left[rows]
            else:
                before = tok[rows, (2 * z - 1) * LANES : 2 * z * LANES]
            if z == nz - 1:
                after = right[rows]
            else:
                after = tok[rows, (2 * z + 2) * LANES : (2 * z + 3) * LANES]
            low = pltpu.roll(before.astype(F32), (32 * i + SPAN) % LANES, 1)
            high = pltpu.roll(after.astype(F32), 32 * i + SPAN, 1)
            packed = jnp.where((lane >= 32 * i) & (lane < 32 * i + SPAN), low, packed)
            packed = jnp.where(
                (lane >= 32 * i + SPAN) & (lane < 32 * i + 2 * SPAN), high, packed
            )
        out[z, 128:144] = packed.astype(BF)


def conv_kernel(
    own, across, beside, far, first, gain,
    conv, stats, par, res,
    tok, edge, win, weight, glu, small, sems,
):
    loads = [
        pltpu.make_async_copy(first.at[:, 0:512], glu, sems.at[0]),
        pltpu.make_async_copy(first.at[:, 768:816], small, sems.at[1]),
    ]
    for copy in loads:
        copy.start()
    core, xhi = place()
    lane = lax.broadcasted_iota(jnp.int32, (16, LANES), 1)
    nz = glu.shape[0]
    for near, away, side in ((own, beside, xhi), (across, far, 1 - xhi)):
        for z in range(nz):
            row = side * (64 * nz) + 64 * z
            for c, blk in ((0, near), (1, away)):
                tok[at(row, 64, 64), 256 * c : 256 * c + 128] = blk[z, 0:64]
                tok[at(row, 64, 64), 256 * c + 128 : 256 * c + 256] = blk[z, 64:128]
            one = near[z, 128:144].astype(F32)
            two = away[z, 128:144].astype(F32)
            for i in range(4):
                low = pltpu.roll(one, (LANES - 32 * i) % LANES, 1)
                high = pltpu.roll(two, (LANES + 32 - 32 * i) % LANES, 1)
                part = jnp.where(lane < 32, low, jnp.where(lane < 64, high, 0.0))
                edge[at(row + 16 * i, 16, 16), :] = part
    for z in range(nz):
        row = xhi * (64 * nz) + 64 * z + 32 * core
        res[32 * z : 32 * z + 32, :] = tok[at(row, 32, 32), :]

    for copy in loads:
        copy.wait()
    table = []
    lane = lax.broadcasted_iota(jnp.int32, (48, LANES), 1)
    for h in range(2):
        total = jnp.zeros((48, LANES), F32)
        for i in range(4):
            x = small[4 * h + i].astype(F32)
            x = x + (pltpu.roll(x, LANES - 32, 1) + pltpu.roll(x, LANES - 64, 1))
            x = jnp.where(lane < 32, x, 0.0)
            total = total + (x if i == 0 else pltpu.roll(x, 32 * i, 1))
        par[:, LANES * h : LANES * (h + 1)] = total[31:39]
        table.append(total)
    for z in range(nz):
        for k in range(8):
            weight[64 * z : 64 * z + 64, LANES * k : LANES * (k + 1)] = glu[z, 64 * k : 64 * k + 64]

    scale = gain[...]
    for c in range(3):
        x = edge[...] if c == 2 else tok[:, 256 * c : 256 * (c + 1)].astype(F32)
        paired = jnp.dot(weight[...], norm_rows(x, scale), preferred_element_type=F32)
        cols = x.shape[1]
        paired = paired.reshape(nz, 2, 32, cols)
        gated = (paired[:, 0] * jax.nn.sigmoid(paired[:, 1])).astype(BF).astype(F32)
        gated = gated.reshape(32 * nz, cols).T
        if c < 2:
            win[c, 16:272, :] = gated
        else:
            for r in range(2):
                win[r, 1:16, :] = gated[32 * r : 32 * r + 15]
                win[r, 272:287, :] = gated[32 * r + 15 : 32 * r + 30]

    step = 64
    for h in range(2):
        cols = slice(LANES * h, LANES * (h + 1))
        total = jnp.zeros((1, LANES), F32)
        for r in range(2):
            for k in range(256 // step):
                acc = jnp.zeros((step, LANES), F32)
                for j in range(31):
                    first = step * k + 1 + j
                    acc = acc + table[h][j : j + 1] * win[r, first : first + step, cols]
                conv[256 * r + step * k : 256 * r + step * (k + 1), cols] = acc
                total = total + jnp.sum(acc, axis=0, keepdims=True)
        mean = total * (1.0 / 512)
        apart = conv[:, cols] - mean
        square = jnp.sum(apart * apart, axis=0, keepdims=True)
        n = stats.shape[0]
        stats[:, h : h + 1, :] = jnp.broadcast_to(mean[None], (n, 1, LANES))
        stats[:, 2 + h : 3 + h, :] = jnp.broadcast_to(square[None], (n, 1, LANES))


def merged(stats, count):
    total = jnp.sum(stats, axis=0)
    mean = total * (1.0 / stats.shape[0])
    apart = stats - mean[None]
    apart = jnp.sum(apart * apart, axis=0)
    return mean[0:2], total[2:4] + count * apart[0:2]


def merge_kernel(stats, out):
    mean, square = merged(stats[...], 512)
    out[:, 0:2] = jnp.broadcast_to(mean[None], (out.shape[0],) + mean.shape)
    out[:, 2:4] = jnp.broadcast_to(square[None], (out.shape[0],) + square.shape)


def bn_kernel(conv, stats, par, out):
    frames = 8 * conv.shape[0]
    mean, square = merged(stats[...], frames)
    scale = lax.rsqrt(square * (1.0 / (frames * stats.shape[0])) + EPS)
    for h in range(2):
        cols = slice(LANES * h, LANES * (h + 1))
        value = (conv[:, cols] - mean[h : h + 1]) * (scale[h : h + 1] * par[0:1, cols])
        value = value + par[1:2, cols]
        out[cols, :] = (value * jax.nn.sigmoid(value)).T.astype(BF)


def place_blocks(own, across, beside, far, whole):
    core, xhi = place()
    nz, half = 8, 256
    for blk, c, x in ((own, core, xhi), (across, core, 1 - xhi)):
        for z in range(nz):
            row = x * 512 + 64 * z + 32 * c
            whole[at(row, 32, 32), :] = blk[32 * z : 32 * z + 32, :]
    for blk, c, x in ((beside, 1 - core, xhi), (far, 1 - core, 1 - xhi)):
        for z in range(nz):
            row = x * 512 + 64 * z + 32 * c
            whole[at(row, 32, 32), :half] = blk[32 * z : 32 * z + 32, half:]
            whole[at(row, 32, 32), half:] = blk[32 * z : 32 * z + 32, :half]


def mix_kernel(own, across, beside, far, blocks, res, out, whole, weight):
    place_blocks(own, across, beside, far, whole)
    for z in range(8):
        for k in range(8):
            tile = slice(LANES * k, LANES * (k + 1))
            weight[32 * z : 32 * z + 32, tile] = blocks[z, 32 * k : 32 * k + 32]
    mixed = jnp.dot(weight[...], whole[...], preferred_element_type=F32)
    out[...] = (res[...].astype(F32) + mixed).astype(BF)


def ff_kernel(
    own, across, beside, far, blocks, gain,
    keep, give,
    whole, normed, hidden, w, sems,
):
    loads = [
        pltpu.make_async_copy(blocks.at[2 * i : 2 * i + 2, 0:8], w.at[2 * i : 2 * i + 2, 0:8], sems.at[i])
        for i in range(4)
    ]
    loads.append(pltpu.make_async_copy(blocks.at[:, 8:16], w.at[:, 8:16], sems.at[4]))
    for copy in loads:
        copy.start()
    xhi = place()[1]
    place_blocks(own, across, beside, far, whole)
    half = 256
    for c in range(2):
        cols = slice(half * c, half * (c + 1))
        normed[:, cols] = norm_rows(whole[:, cols].astype(F32), gain[...])
    for z in range(0, 8, 2):
        loads[z // 2].wait()
        rows = [jnp.concatenate([w[z + i, k] for k in range(8)], axis=1) for i in range(2)]
        value = jnp.dot(
            jnp.concatenate(rows, axis=0), normed[...], preferred_element_type=F32
        )
        hidden[LANES * z : LANES * (z + 2), :] = (value * jax.nn.sigmoid(value)).astype(BF)
    loads[4].wait()
    for k in range(0, 8, 2):
        rows = [jnp.concatenate([w[z, 8 + k + i] for z in range(8)], axis=1) for i in range(2)]
        value = jnp.dot(
            jnp.concatenate(rows, axis=0), hidden[...], preferred_element_type=F32
        )
        rows = slice(LANES * k, LANES * (k + 2))
        mine = jnp.where(xhi == k // 4, 1.0, 0.0)
        keep[rows, :] = 0.5 * value[:, :half] + mine * whole[rows, :half].astype(F32)
        give[rows, :] = (0.5 * value[:, half:]).astype(BF)


def sum_kernel(parts, out):
    nz, run = parts.shape[0] // 2, parts.shape[2]
    for z in range(nz):
        value = parts[z].astype(F32) + parts[nz + z].astype(F32)
        out[:, run * z : run * (z + 1)] = value.astype(BF)


def body(
    tokens,
    ln_conv_gain,
    glu_weight,
    depth_weight,
    bn_gain,
    bn_shift,
    conv_out_weight,
    ln_ff_gain,
    ff_in_weight,
    ff_out_weight,
):
    nz = lax.axis_size(Z)
    frames, width = tokens.shape
    full = ln_conv_gain.shape[0]
    run = frames // nz

    first, tok, head, tail = pl.pallas_call(
        weight_kernel,
        out_shape=(
            shape((816, LANES), BF),
            shape((width, frames), BF),
            shape((width, LANES), BF),
            shape((width, LANES), BF),
        ),
        in_specs=[HBM] * 6,
        out_specs=(HBM, VMEM, VMEM, VMEM),
        scratch_shapes=[
            pltpu.VMEM((48, LANES), F32),
            pltpu.VMEM((48, LANES), BF),
            pltpu.VMEM((48, width), F32),
            pltpu.SemaphoreType.DMA((31,)),
        ],
        compiler_params=PARAMS,
        name="weights",
    )(
        *in_hbm(
            glu_weight.transpose(1, 2, 0),
            conv_out_weight.T,
            depth_weight,
            bn_gain[None],
            bn_shift[None],
            tokens.T,
        )
    )
    first = lax.all_gather(first, Z)

    tm = lax.axis_size((XLO, Y, CORE))
    up = [(i, i + 1) for i in range(tm - 1)]
    left = lax.ppermute(tail, (XLO, Y, CORE), up)
    right = lax.ppermute(head, (XLO, Y, CORE), [(j, i) for i, j in up])
    parts = pl.pallas_call(
        pack_kernel,
        out_shape=shape((nz, 144, LANES), BF),
        in_specs=[VMEM] * 3,
        out_specs=VMEM,
        compiler_params=PARAMS,
        name="pack",
    )(tok, left, right)
    parts = lax.all_to_all(parts, Z, 0, 0, tiled=True)

    blocks = pl.pallas_call(
        block_kernel,
        out_shape=shape((16, LANES, LANES), BF),
        in_specs=[VMEM] * 2,
        out_specs=VMEM,
        compiler_params=PARAMS,
        name="blocks",
    )(ff_in_weight, ff_out_weight)
    blocks, parts = lax.optimization_barrier((blocks, parts))
    blocks = lax.all_gather(blocks, Z)

    whole = group_gather(parts)
    conv, stats, par, res = pl.pallas_call(
        conv_kernel,
        out_shape=(
            shape((2 * run, 256), F32),
            shape((nz, 4, LANES), F32),
            shape((8, 256), F32),
            shape((256, 2 * run), BF),
        ),
        in_specs=[VMEM] * 4 + [HBM, VMEM],
        out_specs=(VMEM,) * 4,
        scratch_shapes=[
            pltpu.VMEM((full, 2 * run), BF),
            pltpu.VMEM((full, LANES), F32),
            pltpu.VMEM((2, run + 40, 256), F32),
            pltpu.VMEM((512, full), BF),
            pltpu.VMEM((nz, 512, LANES), BF),
            pltpu.VMEM((nz, 48, LANES), BF),
            pltpu.SemaphoreType.DMA((2,)),
        ],
        compiler_params=PARAMS,
        name="conv",
    )(*whole, *in_hbm(first), ln_conv_gain[:, None])
    stats = lax.all_to_all(stats, Z, 0, 0, tiled=True)
    stats = pl.pallas_call(
        merge_kernel,
        out_shape=shape((lax.axis_size((XLO, Y)), 4, LANES), F32),
        in_specs=[VMEM],
        out_specs=VMEM,
        compiler_params=PARAMS,
        name="merge",
    )(stats)
    stats = lax.all_to_all(stats, (XLO, Y), 0, 0, tiled=True)
    activated = pl.pallas_call(
        bn_kernel,
        out_shape=shape((256, 2 * run), BF),
        in_specs=[VMEM] * 3,
        out_specs=VMEM,
        compiler_params=PARAMS,
        name="bn",
    )(conv, stats, par)
    block = pl.pallas_call(
        mix_kernel,
        out_shape=shape((256, 2 * run), BF),
        grid=(1,),
        in_specs=[VMEM] * 4
        + [
            pl.BlockSpec((nz, 256, LANES), lambda i: (0, 2, 0)),
            VMEM,
        ],
        out_specs=VMEM,
        scratch_shapes=[pltpu.VMEM((full, 2 * run), BF), pltpu.VMEM((256, full), BF)],
        compiler_params=PARAMS,
        name="mix",
    )(*group_gather(activated), first, res)
    keep, give = pl.pallas_call(
        ff_kernel,
        out_shape=(shape((full, run), F32), shape((full, run), BF)),
        in_specs=[VMEM] * 4 + [HBM, VMEM],
        out_specs=(VMEM,) * 2,
        scratch_shapes=[
            pltpu.VMEM((full, 2 * run), BF),
            pltpu.VMEM((full, 2 * run), BF),
            pltpu.VMEM((full, 2 * run), BF),
            pltpu.VMEM((nz, 16, LANES, LANES), BF),
            pltpu.SemaphoreType.DMA((5,)),
        ],
        compiler_params=PARAMS,
        name="ff",
    )(*group_gather(block), *in_hbm(blocks), ln_ff_gain[:, None])
    keep = (keep + swap(give, CORE).astype(F32)).astype(BF)
    keep = lax.all_to_all(keep.reshape(2 * nz, width, run), (XHI, Z), 0, 0, tiled=True)
    out = pl.pallas_call(
        sum_kernel,
        out_shape=shape((width, frames), BF),
        in_specs=[VMEM],
        out_specs=VMEM,
        compiler_params=PARAMS,
        name="sum",
    )(keep)
    return out.T


def solution(mesh):
    fine = Mesh(mesh.devices.reshape(2, 8, 2, 2, 8), (XLO, Y, CORE, XHI, Z))
    tm, mp = ((XLO, Y, CORE), (XHI, Z))
    in_specs = (
        P(tm, mp),
        P(),
        P(None, None, mp),
        P(None, mp),
        P(mp),
        P(mp),
        P(None, mp),
        P(),
        P(None, mp),
        P(mp, None),
    )
    return jax.shard_map(body, mesh=fine, in_specs=in_specs, out_specs=P(tm, mp), check_vma=False)
```

```python
import jax
import jax.numpy as jnp
from jax import lax
from jax.experimental import pallas as pl
from jax.experimental.pallas import tpu as pltpu
from jax.sharding import Mesh, PartitionSpec as P

XLO, Y, CORE, XHI, Z = ("xlo", "y", "core", "xhi", "z")
BF, F32 = (jnp.bfloat16, jnp.float32)
EPS = 1e-05
LANES = 128
SPAN = 15
VMEM = pl.BlockSpec(memory_space=pltpu.VMEM)
HBM = pl.BlockSpec(memory_space=pltpu.HBM)
PARAMS = pltpu.CompilerParams(vmem_limit_bytes=40 << 20)


def shape(dims, dtype):
    return jax.ShapeDtypeStruct(dims, dtype)


def in_hbm(*arrays):
    return [pltpu.with_memory_space_constraint(x, pltpu.HBM) for x in arrays]


def swap(x, axis):
    return lax.ppermute(x, axis, [(0, 1), (1, 0)])


def group_gather(x):
    across = swap(x, XHI)
    beside = swap(x, CORE)
    return x, across, beside, swap(across, CORE)


def norm_rows(x, gain):
    inv = 1.0 / x.shape[0]
    centred = x - jnp.sum(x, axis=0, keepdims=True) * inv
    spread = jnp.sum(centred * centred, axis=0, keepdims=True) * inv
    return (centred * lax.rsqrt(spread + EPS) * gain).astype(BF)


def place():
    return lax.axis_index(CORE), lax.axis_index(XHI)


def at(start, size, step):
    return pl.ds(pl.multiple_of(start, step), size)


def weight_kernel(
    glu, conv_out, depth, gain, shift, tok,
    out, near, first, last,
    table, parts, small, sems,
):
    core, _ = place()
    half = at(32 * core, 32, 32)
    taps, width = depth.shape
    frames = tok.shape[1]
    pairs = [
        (depth, small.at[0:taps]),
        (gain, small.at[32:33]),
        (shift, small.at[40:41]),
        (glu.at[0, half], parts.at[0:32]),
        (glu.at[1, half], parts.at[32:64]),
        (conv_out.at[half], parts.at[64:96]),
        (tok.at[:, 0:LANES], first),
        (tok.at[:, frames - LANES : frames], last),
        (tok, near),
    ]
    loads = [pltpu.make_async_copy(a, b, sems.at[i]) for i, (a, b) in enumerate(pairs)]
    for copy in loads:
        copy.start()
    table[...] = jnp.zeros_like(table)
    for copy in loads[:3]:
        copy.wait()
    table[0:taps, 0:width] = small[0:taps]
    table[taps : taps + 1, 0:width] = small[32:33]
    table[taps + 1 : taps + 2, 0:width] = small[40:41]
    lane = lax.broadcasted_iota(jnp.int32, table.shape, 1)
    rest = jnp.where(core == 0, table[...], pltpu.roll(table[...], LANES - 32, 1))
    rest = jnp.where(lane < 32, rest, 0.0)
    packed = jnp.zeros_like(rest)
    for i in range(3):
        piece = rest.astype(BF).astype(F32)
        packed = packed + (piece if i == 0 else pltpu.roll(piece, 32 * i, 1))
        rest = rest - piece
    parts[96:112] = jnp.zeros((16, parts.shape[1]), BF)
    for i in range(3):
        parts[96:112, LANES * i : LANES * (i + 1)] = packed[16 * i : 16 * i + 16].astype(BF)
    for copy in loads[3:6]:
        copy.wait()
    final = pltpu.make_async_copy(parts, out, sems.at[9])
    final.start()
    for copy in loads[6:] + [final]:
        copy.wait()


def block_kernel(ff_in, ff_out, out):
    half = at(place()[0] * LANES, LANES, LANES)
    for k in range(8):
        tile = slice(LANES * k, LANES * (k + 1))
        out[k] = ff_in[tile, half].astype(F32).T.astype(BF)
        out[8 + k] = ff_out[half, tile].astype(F32).T.astype(BF)


def pack_kernel(tok, left, right, out):
    lane = lax.broadcasted_iota(jnp.int32, (16, LANES), 1)
    nz = out.shape[0]
    for z in range(nz):
        out[z, 0:64] = tok[:, 2 * z * LANES : (2 * z + 1) * LANES]
        out[z, 64:128] = tok[:, (2 * z + 1) * LANES : (2 * z + 2) * LANES]
        packed = jnp.zeros((16, LANES), F32)
        for i in range(4):
            rows = slice(16 * i, 16 * i + 16)
            if z == 0:
                before = left[rows]
            else:
                before = tok[rows, (2 * z - 1) * LANES : 2 * z * LANES]
            if z == nz - 1:
                after = right[rows]
            else:
                after = tok[rows, (2 * z + 2) * LANES : (2 * z + 3) * LANES]
            low = pltpu.roll(before.astype(F32), (32 * i + SPAN) % LANES, 1)
            high = pltpu.roll(after.astype(F32), 32 * i + SPAN, 1)
            packed = jnp.where((lane >= 32 * i) & (lane < 32 * i + SPAN), low, packed)
            packed = jnp.where(
                (lane >= 32 * i + SPAN) & (lane < 32 * i + 2 * SPAN), high, packed
            )
        out[z, 128:144] = packed.astype(BF)


def conv_kernel(
    own, across, beside, far, first, gain,
    conv, stats, par, res,
    tok, edge, win, weight, small, sems,
):
    loads = [
        pltpu.make_async_copy(first.at[:, 0:64], weight, sems.at[0]),
        pltpu.make_async_copy(first.at[:, 96:112, 0:384], small, sems.at[1]),
    ]
    for copy in loads:
        copy.start()
    core, xhi = place()
    lane = lax.broadcasted_iota(jnp.int32, (16, LANES), 1)
    nz = small.shape[0]
    for near, away, side in ((own, beside, xhi), (across, far, 1 - xhi)):
        for z in range(nz):
            row = side * (64 * nz) + 64 * z
            for c, blk in ((0, near), (1, away)):
                tok[at(row, 64, 64), 256 * c : 256 * c + 128] = blk[z, 0:64]
                tok[at(row, 64, 64), 256 * c + 128 : 256 * c + 256] = blk[z, 64:128]
            one = near[z, 128:144].astype(F32)
            two = away[z, 128:144].astype(F32)
            for i in range(4):
                low = pltpu.roll(one, (LANES - 32 * i) % LANES, 1)
                high = pltpu.roll(two, (LANES + 32 - 32 * i) % LANES, 1)
                part = jnp.where(lane < 32, low, jnp.where(lane < 64, high, 0.0))
                edge[at(row + 16 * i, 16, 16), :] = part
    for z in range(nz):
        row = xhi * (64 * nz) + 64 * z + 32 * core
        res[32 * z : 32 * z + 32, :] = tok[at(row, 32, 32), :]

    for copy in loads:
        copy.wait()
    table = []
    lane = lax.broadcasted_iota(jnp.int32, (48, LANES), 1)
    for h in range(2):
        total = jnp.zeros((48, LANES), F32)
        for i in range(4):
            x = [small[4 * h + i, :, LANES * k : LANES * (k + 1)] for k in range(3)]
            x = jnp.concatenate(x, axis=0).astype(F32)
            x = x + (pltpu.roll(x, LANES - 32, 1) + pltpu.roll(x, LANES - 64, 1))
            x = jnp.where(lane < 32, x, 0.0)
            total = total + (x if i == 0 else pltpu.roll(x, 32 * i, 1))
        par[:, LANES * h : LANES * (h + 1)] = total[31:39]
        table.append(total)
    glu = weight[...].reshape(64 * nz, weight.shape[2])
    scale = gain[...]
    for c in range(3):
        x = edge[...] if c == 2 else tok[:, 256 * c : 256 * (c + 1)].astype(F32)
        paired = jnp.dot(glu, norm_rows(x, scale), preferred_element_type=F32)
        cols = x.shape[1]
        paired = paired.reshape(nz, 2, 32, cols)
        gated = (paired[:, 0] * jax.nn.sigmoid(paired[:, 1])).astype(BF).astype(F32)
        gated = gated.reshape(32 * nz, cols).T
        if c < 2:
            win[c, 16:272, :] = gated
        else:
            for r in range(2):
                win[r, 1:16, :] = gated[32 * r : 32 * r + 15]
                win[r, 272:287, :] = gated[32 * r + 15 : 32 * r + 30]

    step = 64
    for h in range(2):
        cols = slice(LANES * h, LANES * (h + 1))
        total = jnp.zeros((1, LANES), F32)
        for r in range(2):
            for k in range(256 // step):
                acc = jnp.zeros((step, LANES), F32)
                for j in range(31):
                    first = step * k + 1 + j
                    acc = acc + table[h][j : j + 1] * win[r, first : first + step, cols]
                conv[256 * r + step * k : 256 * r + step * (k + 1), cols] = acc
                total = total + jnp.sum(acc, axis=0, keepdims=True)
        mean = total * (1.0 / 512)
        apart = conv[:, cols] - mean
        square = jnp.sum(apart * apart, axis=0, keepdims=True)
        n = stats.shape[0]
        stats[:, h : h + 1, :] = jnp.broadcast_to(mean[None], (n, 1, LANES))
        stats[:, 2 + h : 3 + h, :] = jnp.broadcast_to(square[None], (n, 1, LANES))


def merged(stats, count):
    total = jnp.sum(stats, axis=0)
    mean = total * (1.0 / stats.shape[0])
    apart = stats - mean[None]
    apart = jnp.sum(apart * apart, axis=0)
    return mean[0:2], total[2:4] + count * apart[0:2]


def merge_kernel(stats, out):
    out[0:2], out[2:4] = merged(stats[...], 512)


def bn_kernel(conv, near, away, par, out):
    frames = 64 * conv.shape[0]
    mean, square = merged(jnp.stack([near[...], away[...]]), frames)
    scale = lax.rsqrt(square * (1.0 / (2 * frames)) + EPS)
    for h in range(2):
        cols = slice(LANES * h, LANES * (h + 1))
        value = (conv[:, cols] - mean[h : h + 1]) * (scale[h : h + 1] * par[0:1, cols])
        value = value + par[1:2, cols]
        out[cols, :] = (value * jax.nn.sigmoid(value)).T.astype(BF)


def place_blocks(own, across, beside, far, whole):
    core, xhi = place()
    nz, half = 8, 256
    for blk, c, x in ((own, core, xhi), (across, core, 1 - xhi)):
        for z in range(nz):
            row = x * 512 + 64 * z + 32 * c
            whole[at(row, 32, 32), :] = blk[32 * z : 32 * z + 32, :]
    for blk, c, x in ((beside, 1 - core, xhi), (far, 1 - core, 1 - xhi)):
        for z in range(nz):
            row = x * 512 + 64 * z + 32 * c
            whole[at(row, 32, 32), :half] = blk[32 * z : 32 * z + 32, half:]
            whole[at(row, 32, 32), half:] = blk[32 * z : 32 * z + 32, :half]


def mix_kernel(own, across, beside, far, blocks, res, out, whole):
    place_blocks(own, across, beside, far, whole)
    weight = blocks[...].reshape(256, blocks.shape[2])
    mixed = jnp.dot(weight, whole[...], preferred_element_type=F32)
    out[...] = (res[...].astype(F32) + mixed).astype(BF)


def ff_kernel(
    own, across, beside, far, blocks, gain,
    keep, give,
    whole, normed, hidden, w, sems,
):
    loads = [
        pltpu.make_async_copy(blocks.at[2 * i : 2 * i + 2, 0:8], w.at[2 * i : 2 * i + 2, 0:8], sems.at[i])
        for i in range(4)
    ]
    loads.append(pltpu.make_async_copy(blocks.at[:, 8:16], w.at[:, 8:16], sems.at[4]))
    for copy in loads:
        copy.start()
    xhi = place()[1]
    place_blocks(own, across, beside, far, whole)
    half = 256
    for c in range(2):
        cols = slice(half * c, half * (c + 1))
        normed[:, cols] = norm_rows(whole[:, cols].astype(F32), gain[...])
    for z in range(0, 8, 2):
        loads[z // 2].wait()
        rows = [jnp.concatenate([w[z + i, k] for k in range(8)], axis=1) for i in range(2)]
        value = jnp.dot(
            jnp.concatenate(rows, axis=0), normed[...], preferred_element_type=F32
        )
        hidden[LANES * z : LANES * (z + 2), :] = (value * jax.nn.sigmoid(value)).astype(BF)
    loads[4].wait()
    for k in range(0, 8, 2):
        rows = [jnp.concatenate([w[z, 8 + k + i] for z in range(8)], axis=1) for i in range(2)]
        value = jnp.dot(
            jnp.concatenate(rows, axis=0), hidden[...], preferred_element_type=F32
        )
        rows = slice(LANES * k, LANES * (k + 2))
        mine = jnp.where(xhi == k // 4, 1.0, 0.0)
        keep[rows, :] = 0.5 * value[:, :half] + mine * whole[rows, :half].astype(F32)
        give[rows, :] = (0.5 * value[:, half:]).astype(BF)


def sum_kernel(parts, out):
    nz, run = parts.shape[0] // 2, parts.shape[2]
    for z in range(nz):
        value = parts[z].astype(F32) + parts[nz + z].astype(F32)
        out[:, run * z : run * (z + 1)] = value.astype(BF)


def body(
    tokens,
    ln_conv_gain,
    glu_weight,
    depth_weight,
    bn_gain,
    bn_shift,
    conv_out_weight,
    ln_ff_gain,
    ff_in_weight,
    ff_out_weight,
):
    nz = lax.axis_size(Z)
    frames, width = tokens.shape
    full = ln_conv_gain.shape[0]
    run = frames // nz

    first, tok, head, tail = pl.pallas_call(
        weight_kernel,
        out_shape=(
            shape((112, full), BF),
            shape((width, frames), BF),
            shape((width, LANES), BF),
            shape((width, LANES), BF),
        ),
        in_specs=[HBM] * 6,
        out_specs=(HBM, VMEM, VMEM, VMEM),
        scratch_shapes=[
            pltpu.VMEM((48, LANES), F32),
            pltpu.VMEM((112, full), BF),
            pltpu.VMEM((48, width), F32),
            pltpu.SemaphoreType.DMA((10,)),
        ],
        compiler_params=PARAMS,
        name="weights",
    )(
        *in_hbm(
            glu_weight.transpose(1, 2, 0),
            conv_out_weight.T,
            depth_weight,
            bn_gain[None],
            bn_shift[None],
            tokens.T,
        )
    )
    first = lax.all_gather(first, Z)

    tm = lax.axis_size((XLO, Y, CORE))
    up = [(i, i + 1) for i in range(tm - 1)]
    left = lax.ppermute(tail, (XLO, Y, CORE), up)
    right = lax.ppermute(head, (XLO, Y, CORE), [(j, i) for i, j in up])
    parts = pl.pallas_call(
        pack_kernel,
        out_shape=shape((nz, 144, LANES), BF),
        in_specs=[VMEM] * 3,
        out_specs=VMEM,
        compiler_params=PARAMS,
        name="pack",
    )(tok, left, right)
    parts = lax.all_to_all(parts, Z, 0, 0, tiled=True)

    blocks = pl.pallas_call(
        block_kernel,
        out_shape=shape((16, LANES, LANES), BF),
        in_specs=[VMEM] * 2,
        out_specs=VMEM,
        compiler_params=PARAMS,
        name="blocks",
    )(ff_in_weight, ff_out_weight)
    blocks, parts = lax.optimization_barrier((blocks, parts))
    blocks = lax.all_gather(blocks, Z)

    whole = group_gather(parts)
    conv, stats, par, res = pl.pallas_call(
        conv_kernel,
        out_shape=(
            shape((2 * run, 256), F32),
            shape((lax.axis_size((Y, Z)), 4, LANES), F32),
            shape((8, 256), F32),
            shape((256, 2 * run), BF),
        ),
        in_specs=[VMEM] * 4 + [HBM, VMEM],
        out_specs=(VMEM,) * 4,
        scratch_shapes=[
            pltpu.VMEM((full, 2 * run), BF),
            pltpu.VMEM((full, LANES), F32),
            pltpu.VMEM((2, run + 40, 256), F32),
            pltpu.VMEM((nz, 64, full), BF),
            pltpu.VMEM((nz, 16, 3 * LANES), BF),
            pltpu.SemaphoreType.DMA((2,)),
        ],
        compiler_params=PARAMS,
        name="conv",
    )(*whole, *in_hbm(first), ln_conv_gain[:, None])
    stats = lax.all_to_all(stats, (Y, Z), 0, 0, tiled=True)
    stats = pl.pallas_call(
        merge_kernel,
        out_shape=shape((4, LANES), F32),
        in_specs=[VMEM],
        out_specs=VMEM,
        compiler_params=PARAMS,
        name="merge",
    )(stats)
    activated = pl.pallas_call(
        bn_kernel,
        out_shape=shape((256, 2 * run), BF),
        in_specs=[VMEM] * 4,
        out_specs=VMEM,
        compiler_params=PARAMS,
        name="bn",
    )(conv, stats, swap(stats, XLO), par)
    block = pl.pallas_call(
        mix_kernel,
        out_shape=shape((256, 2 * run), BF),
        grid=(1,),
        in_specs=[VMEM] * 4
        + [
            pl.BlockSpec((nz, 32, full), lambda i: (0, 2, 0)),
            VMEM,
        ],
        out_specs=VMEM,
        scratch_shapes=[pltpu.VMEM((full, 2 * run), BF)],
        compiler_params=PARAMS,
        name="mix",
    )(*group_gather(activated), first, res)
    keep, give = pl.pallas_call(
        ff_kernel,
        out_shape=(shape((full, run), F32), shape((full, run), BF)),
        in_specs=[VMEM] * 4 + [HBM, VMEM],
        out_specs=(VMEM,) * 2,
        scratch_shapes=[
            pltpu.VMEM((full, 2 * run), BF),
            pltpu.VMEM((full, 2 * run), BF),
            pltpu.VMEM((full, 2 * run), BF),
            pltpu.VMEM((nz, 16, LANES, LANES), BF),
            pltpu.SemaphoreType.DMA((5,)),
        ],
        compiler_params=PARAMS,
        name="ff",
    )(*group_gather(block), *in_hbm(blocks), ln_ff_gain[:, None])
    keep = (keep + swap(give, CORE).astype(F32)).astype(BF)
    keep = lax.all_to_all(keep.reshape(2 * nz, width, run), (XHI, Z), 0, 0, tiled=True)
    out = pl.pallas_call(
        sum_kernel,
        out_shape=shape((width, frames), BF),
        in_specs=[VMEM],
        out_specs=VMEM,
        compiler_params=PARAMS,
        name="sum",
    )(keep)
    return out.T


def solution(mesh):
    fine = Mesh(mesh.devices.reshape(2, 8, 2, 2, 8), (XLO, Y, CORE, XHI, Z))
    tm, mp = ((XLO, Y, CORE), (XHI, Z))
    in_specs = (
        P(tm, mp),
        P(),
        P(None, None, mp),
        P(None, mp),
        P(mp),
        P(mp),
        P(None, mp),
        P(),
        P(None, mp),
        P(mp, None),
    )
    return jax.shard_map(body, mesh=fine, in_specs=in_specs, out_specs=P(tm, mp), check_vma=False)
```

```python
import jax
import jax.numpy as jnp
from jax import lax
from jax.experimental import pallas as pl
from jax.experimental.pallas import tpu as pltpu
from jax.sharding import Mesh, PartitionSpec as P

XLO, Y, CORE, XHI, Z = ("xlo", "y", "core", "xhi", "z")
BF, F32 = (jnp.bfloat16, jnp.float32)
EPS = 1e-05
LANES = 128
SPAN = 15
VMEM = pl.BlockSpec(memory_space=pltpu.VMEM)
HBM = pl.BlockSpec(memory_space=pltpu.HBM)
PARAMS = pltpu.CompilerParams(vmem_limit_bytes=40 << 20)


def shape(dims, dtype):
    return jax.ShapeDtypeStruct(dims, dtype)


def in_hbm(*arrays):
    return [pltpu.with_memory_space_constraint(x, pltpu.HBM) for x in arrays]


def swap(x, axis):
    return lax.ppermute(x, axis, [(0, 1), (1, 0)])


def group_gather(x):
    across = swap(x, XHI)
    beside = swap(x, CORE)
    return x, across, beside, swap(across, CORE)


def norm_rows(x, gain):
    inv = 1.0 / x.shape[0]
    centred = x - jnp.sum(x, axis=0, keepdims=True) * inv
    spread = jnp.sum(centred * centred, axis=0, keepdims=True) * inv
    return (centred * lax.rsqrt(spread + EPS) * gain).astype(BF)


def place():
    return lax.axis_index(CORE), lax.axis_index(XHI)


def at(start, size, step):
    return pl.ds(pl.multiple_of(start, step), size)


def weight_kernel(
    glu, conv_out, depth, gain, shift, tok,
    out, near, first, last,
    table, parts, small, sems,
):
    core, _ = place()
    half = at(32 * core, 32, 32)
    taps, width = depth.shape
    frames = tok.shape[1]
    pairs = [
        (depth, small.at[0:taps]),
        (gain, small.at[32:33]),
        (shift, small.at[40:41]),
        (glu.at[0, half], parts.at[0:32]),
        (glu.at[1, half], parts.at[32:64]),
        (conv_out.at[half], parts.at[64:96]),
        (tok.at[:, 0:LANES], first),
        (tok.at[:, frames - LANES : frames], last),
        (tok, near),
    ]
    loads = [pltpu.make_async_copy(a, b, sems.at[i]) for i, (a, b) in enumerate(pairs)]
    for copy in loads:
        copy.start()
    table[...] = jnp.zeros_like(table)
    for copy in loads[:3]:
        copy.wait()
    table[0:taps, 0:width] = small[0:taps]
    table[taps : taps + 1, 0:width] = small[32:33]
    table[taps + 1 : taps + 2, 0:width] = small[40:41]
    lane = lax.broadcasted_iota(jnp.int32, table.shape, 1)
    rest = jnp.where(core == 0, table[...], pltpu.roll(table[...], LANES - 32, 1))
    rest = jnp.where(lane < 32, rest, 0.0)
    packed = jnp.zeros_like(rest)
    for i in range(3):
        piece = rest.astype(BF).astype(F32)
        packed = packed + (piece if i == 0 else pltpu.roll(piece, 32 * i, 1))
        rest = rest - piece
    parts[96:112] = jnp.zeros((16, parts.shape[1]), BF)
    for i in range(3):
        parts[96:112, LANES * i : LANES * (i + 1)] = packed[16 * i : 16 * i + 16].astype(BF)
    for copy in loads[3:6]:
        copy.wait()
    final = pltpu.make_async_copy(parts, out, sems.at[9])
    final.start()
    for copy in loads[6:] + [final]:
        copy.wait()


def block_kernel(ff_in, ff_out, out):
    half = at(place()[0] * LANES, LANES, LANES)
    for k in range(8):
        tile = slice(LANES * k, LANES * (k + 1))
        out[k] = ff_in[tile, half].astype(F32).T.astype(BF)
        out[8 + k] = ff_out[half, tile].astype(F32).T.astype(BF)


def pack_kernel(tok, left, right, out):
    lane = lax.broadcasted_iota(jnp.int32, (16, LANES), 1)
    nz = out.shape[0]
    for z in range(nz):
        out[z, 0:64] = tok[:, 2 * z * LANES : (2 * z + 1) * LANES]
        out[z, 64:128] = tok[:, (2 * z + 1) * LANES : (2 * z + 2) * LANES]
        packed = jnp.zeros((16, LANES), F32)
        for i in range(4):
            rows = slice(16 * i, 16 * i + 16)
            if z == 0:
                before = left[rows]
            else:
                before = tok[rows, (2 * z - 1) * LANES : 2 * z * LANES]
            if z == nz - 1:
                after = right[rows]
            else:
                after = tok[rows, (2 * z + 2) * LANES : (2 * z + 3) * LANES]
            low = pltpu.roll(before.astype(F32), (32 * i + SPAN) % LANES, 1)
            high = pltpu.roll(after.astype(F32), 32 * i + SPAN, 1)
            packed = jnp.where((lane >= 32 * i) & (lane < 32 * i + SPAN), low, packed)
            packed = jnp.where(
                (lane >= 32 * i + SPAN) & (lane < 32 * i + 2 * SPAN), high, packed
            )
        out[z, 128:144] = packed.astype(BF)


def conv_kernel(
    own, across, beside, far, first, gain,
    conv, stats, par, res,
    tok, edge, win, weight, small, sems,
):
    loads = [
        pltpu.make_async_copy(first.at[:, 0:64], weight, sems.at[0]),
        pltpu.make_async_copy(first.at[:, 96:112, 0:384], small, sems.at[1]),
    ]
    for copy in loads:
        copy.start()
    core, xhi = place()
    lane = lax.broadcasted_iota(jnp.int32, (16, LANES), 1)
    nz = small.shape[0]
    for near, away, side in ((own, beside, xhi), (across, far, 1 - xhi)):
        for z in range(nz):
            row = side * (64 * nz) + 64 * z
            for c, blk in ((0, near), (1, away)):
                tok[at(row, 64, 64), 256 * c : 256 * c + 128] = blk[z, 0:64]
                tok[at(row, 64, 64), 256 * c + 128 : 256 * c + 256] = blk[z, 64:128]
            one = near[z, 128:144].astype(F32)
            two = away[z, 128:144].astype(F32)
            for i in range(4):
                low = pltpu.roll(one, (LANES - 32 * i) % LANES, 1)
                high = pltpu.roll(two, (LANES + 32 - 32 * i) % LANES, 1)
                part = jnp.where(lane < 32, low, jnp.where(lane < 64, high, 0.0))
                edge[at(row + 16 * i, 16, 16), :] = part
    for z in range(nz):
        row = xhi * (64 * nz) + 64 * z + 32 * core
        res[32 * z : 32 * z + 32, :] = tok[at(row, 32, 32), :]

    for copy in loads:
        copy.wait()
    table = []
    lane = lax.broadcasted_iota(jnp.int32, (48, LANES), 1)
    for h in range(2):
        total = jnp.zeros((48, LANES), F32)
        for i in range(4):
            x = [small[4 * h + i, :, LANES * k : LANES * (k + 1)] for k in range(3)]
            x = jnp.concatenate(x, axis=0).astype(F32)
            x = x + (pltpu.roll(x, LANES - 32, 1) + pltpu.roll(x, LANES - 64, 1))
            x = jnp.where(lane < 32, x, 0.0)
            total = total + (x if i == 0 else pltpu.roll(x, 32 * i, 1))
        par[:, LANES * h : LANES * (h + 1)] = total[31:39]
        table.append(total)
    glu = weight[...].reshape(64 * nz, weight.shape[2])
    scale = gain[...]
    for c in range(3):
        x = edge[...] if c == 2 else tok[:, 256 * c : 256 * (c + 1)].astype(F32)
        paired = jnp.dot(glu, norm_rows(x, scale), preferred_element_type=F32)
        cols = x.shape[1]
        paired = paired.reshape(nz, 2, 32, cols)
        gated = (paired[:, 0] * jax.nn.sigmoid(paired[:, 1])).astype(BF).astype(F32)
        gated = gated.reshape(32 * nz, cols).T
        if c < 2:
            win[c, 16:272, :] = gated
        else:
            for r in range(2):
                win[r, 1:16, :] = gated[32 * r : 32 * r + 15]
                win[r, 272:287, :] = gated[32 * r + 15 : 32 * r + 30]

    step = 64
    for h in range(2):
        cols = slice(LANES * h, LANES * (h + 1))
        total = jnp.zeros((1, LANES), F32)
        for r in range(2):
            for k in range(256 // step):
                acc = jnp.zeros((step, LANES), F32)
                for j in range(31):
                    first = step * k + 1 + j
                    acc = acc + table[h][j : j + 1] * win[r, first : first + step, cols]
                conv[256 * r + step * k : 256 * r + step * (k + 1), cols] = acc
                total = total + jnp.sum(acc, axis=0, keepdims=True)
        mean = total * (1.0 / 512)
        apart = conv[:, cols] - mean
        square = jnp.sum(apart * apart, axis=0, keepdims=True)
        n = stats.shape[0]
        stats[:, h : h + 1, :] = jnp.broadcast_to(mean[None], (n, 1, LANES))
        stats[:, 2 + h : 3 + h, :] = jnp.broadcast_to(square[None], (n, 1, LANES))


def bn_kernel(conv, stats, par, out):
    n, frames = stats.shape[0], conv.shape[0]
    s = stats[...]
    total = jnp.sum(s, axis=0)
    mean = total * (1.0 / n)
    apart = s - mean[None]
    apart = jnp.sum(apart * apart, axis=0)
    square = total[2:4] + frames * apart[0:2]
    scale = lax.rsqrt(square * (1.0 / (n * frames)) + EPS)
    for h in range(2):
        cols = slice(LANES * h, LANES * (h + 1))
        value = (conv[:, cols] - mean[h : h + 1]) * (scale[h : h + 1] * par[0:1, cols])
        value = value + par[1:2, cols]
        out[cols, :] = (value * jax.nn.sigmoid(value)).T.astype(BF)


def place_blocks(own, across, beside, far, whole):
    core, xhi = place()
    nz, half = 8, 256
    for blk, c, x in ((own, core, xhi), (across, core, 1 - xhi)):
        for z in range(nz):
            row = x * 512 + 64 * z + 32 * c
            whole[at(row, 32, 32), :] = blk[32 * z : 32 * z + 32, :]
    for blk, c, x in ((beside, 1 - core, xhi), (far, 1 - core, 1 - xhi)):
        for z in range(nz):
            row = x * 512 + 64 * z + 32 * c
            whole[at(row, 32, 32), :half] = blk[32 * z : 32 * z + 32, half:]
            whole[at(row, 32, 32), half:] = blk[32 * z : 32 * z + 32, :half]


def mix_kernel(own, across, beside, far, blocks, res, out, whole):
    place_blocks(own, across, beside, far, whole)
    weight = blocks[...].reshape(256, blocks.shape[2])
    mixed = jnp.dot(weight, whole[...], preferred_element_type=F32)
    out[...] = (res[...].astype(F32) + mixed).astype(BF)


def norm_kernel(own, across, beside, far, gain, near, normed, whole):
    place_blocks(own, across, beside, far, whole)
    half = normed.shape[1] // 2
    near[...] = whole[:, :half]
    for c in range(2):
        cols = slice(half * c, half * (c + 1))
        normed[:, cols] = norm_rows(whole[:, cols].astype(F32), gain[...])


def ff_kernel(near, normed, blocks, keep, give, hidden, w, sems):
    loads = [
        pltpu.make_async_copy(
            blocks.at[2 * i : 2 * i + 2, 0:8], w.at[2 * i : 2 * i + 2, 0:8], sems.at[i]
        )
        for i in range(4)
    ]
    loads.append(pltpu.make_async_copy(blocks.at[:, 8:16], w.at[:, 8:16], sems.at[4]))
    for copy in loads:
        copy.start()
    xhi = place()[1]
    half = normed.shape[1] // 2
    for z in range(0, 8, 2):
        loads[z // 2].wait()
        rows = [jnp.concatenate([w[z + i, k] for k in range(8)], axis=1) for i in range(2)]
        value = jnp.dot(
            jnp.concatenate(rows, axis=0), normed[...], preferred_element_type=F32
        )
        hidden[LANES * z : LANES * (z + 2), :] = (value * jax.nn.sigmoid(value)).astype(BF)
    loads[4].wait()
    for k in range(0, 8, 2):
        rows = [jnp.concatenate([w[z, 8 + k + i] for z in range(8)], axis=1) for i in range(2)]
        value = jnp.dot(
            jnp.concatenate(rows, axis=0), hidden[...], preferred_element_type=F32
        )
        rows = slice(LANES * k, LANES * (k + 2))
        mine = jnp.where(xhi == k // 4, 1.0, 0.0)
        keep[rows, :] = 0.5 * value[:, :half] + mine * near[rows, :].astype(F32)
        give[rows, :] = (0.5 * value[:, half:]).astype(BF)


def sum_kernel(parts, out):
    nz, run = parts.shape[0] // 2, parts.shape[2]
    for z in range(nz):
        value = parts[z].astype(F32) + parts[nz + z].astype(F32)
        out[:, run * z : run * (z + 1)] = value.astype(BF)


def body(
    tokens,
    ln_conv_gain,
    glu_weight,
    depth_weight,
    bn_gain,
    bn_shift,
    conv_out_weight,
    ln_ff_gain,
    ff_in_weight,
    ff_out_weight,
):
    nz = lax.axis_size(Z)
    frames, width = tokens.shape
    full = ln_conv_gain.shape[0]
    run = frames // nz

    first, tok, head, tail = pl.pallas_call(
        weight_kernel,
        out_shape=(
            shape((112, full), BF),
            shape((width, frames), BF),
            shape((width, LANES), BF),
            shape((width, LANES), BF),
        ),
        in_specs=[HBM] * 6,
        out_specs=(HBM, VMEM, VMEM, VMEM),
        scratch_shapes=[
            pltpu.VMEM((48, LANES), F32),
            pltpu.VMEM((112, full), BF),
            pltpu.VMEM((48, width), F32),
            pltpu.SemaphoreType.DMA((10,)),
        ],
        compiler_params=PARAMS,
        name="weights",
    )(
        *in_hbm(
            glu_weight.transpose(1, 2, 0),
            conv_out_weight.T,
            depth_weight,
            bn_gain[None],
            bn_shift[None],
            tokens.T,
        )
    )
    first = lax.all_gather(first, Z)

    tm = lax.axis_size((XLO, Y, CORE))
    up = [(i, i + 1) for i in range(tm - 1)]
    left = lax.ppermute(tail, (XLO, Y, CORE), up)
    right = lax.ppermute(head, (XLO, Y, CORE), [(j, i) for i, j in up])
    parts = pl.pallas_call(
        pack_kernel,
        out_shape=shape((nz, 144, LANES), BF),
        in_specs=[VMEM] * 3,
        out_specs=VMEM,
        compiler_params=PARAMS,
        name="pack",
    )(tok, left, right)
    parts = lax.all_to_all(parts, Z, 0, 0, tiled=True)

    blocks = pl.pallas_call(
        block_kernel,
        out_shape=shape((16, LANES, LANES), BF),
        in_specs=[VMEM] * 2,
        out_specs=VMEM,
        compiler_params=PARAMS,
        name="blocks",
    )(ff_in_weight, ff_out_weight)
    blocks, parts = lax.optimization_barrier((blocks, parts))
    blocks = lax.all_gather(blocks, Z)

    whole = group_gather(parts)
    conv, stats, par, res = pl.pallas_call(
        conv_kernel,
        out_shape=(
            shape((2 * run, 256), F32),
            shape((lax.axis_size((XLO, Y, Z)), 4, LANES), F32),
            shape((8, 256), F32),
            shape((256, 2 * run), BF),
        ),
        in_specs=[VMEM] * 4 + [HBM, VMEM],
        out_specs=(VMEM,) * 4,
        scratch_shapes=[
            pltpu.VMEM((full, 2 * run), BF),
            pltpu.VMEM((full, LANES), F32),
            pltpu.VMEM((2, run + 40, 256), F32),
            pltpu.VMEM((nz, 64, full), BF),
            pltpu.VMEM((nz, 16, 3 * LANES), BF),
            pltpu.SemaphoreType.DMA((2,)),
        ],
        compiler_params=PARAMS,
        name="conv",
    )(*whole, *in_hbm(first), ln_conv_gain[:, None])
    stats = lax.all_to_all(stats, (XLO, Y, Z), 0, 0, tiled=True)
    activated = pl.pallas_call(
        bn_kernel,
        out_shape=shape((256, 2 * run), BF),
        in_specs=[VMEM] * 3,
        out_specs=VMEM,
        compiler_params=PARAMS,
        name="bn",
    )(conv, stats, par)
    block = pl.pallas_call(
        mix_kernel,
        out_shape=shape((256, 2 * run), BF),
        grid=(1,),
        in_specs=[VMEM] * 4
        + [
            pl.BlockSpec((nz, 32, full), lambda i: (0, 2, 0)),
            VMEM,
        ],
        out_specs=VMEM,
        scratch_shapes=[pltpu.VMEM((full, 2 * run), BF)],
        compiler_params=PARAMS,
        name="mix",
    )(*group_gather(activated), first, res)
    near, normed = pl.pallas_call(
        norm_kernel,
        out_shape=(shape((full, run), BF), shape((full, 2 * run), BF)),
        in_specs=[VMEM] * 5,
        out_specs=(VMEM,) * 2,
        scratch_shapes=[pltpu.VMEM((full, 2 * run), BF)],
        compiler_params=PARAMS,
        name="norm",
    )(*group_gather(block), ln_ff_gain[:, None])
    keep, give = pl.pallas_call(
        ff_kernel,
        out_shape=(shape((full, run), F32), shape((full, run), BF)),
        in_specs=[VMEM] * 2 + [HBM],
        out_specs=(VMEM,) * 2,
        scratch_shapes=[
            pltpu.VMEM((full, 2 * run), BF),
            pltpu.VMEM((nz, 16, LANES, LANES), BF),
            pltpu.SemaphoreType.DMA((5,)),
        ],
        compiler_params=PARAMS,
        name="ff",
    )(near, normed, *in_hbm(blocks))
    keep = (keep + swap(give, CORE).astype(F32)).astype(BF)
    keep = lax.all_to_all(keep.reshape(2 * nz, width, run), (XHI, Z), 0, 0, tiled=True)
    out = pl.pallas_call(
        sum_kernel,
        out_shape=shape((width, frames), BF),
        in_specs=[VMEM],
        out_specs=VMEM,
        compiler_params=PARAMS,
        name="sum",
    )(keep)
    return out.T


def solution(mesh):
    fine = Mesh(mesh.devices.reshape(2, 8, 2, 2, 8), (XLO, Y, CORE, XHI, Z))
    tm, mp = ((XLO, Y, CORE), (XHI, Z))
    in_specs = (
        P(tm, mp),
        P(),
        P(None, None, mp),
        P(None, mp),
        P(mp),
        P(mp),
        P(None, mp),
        P(),
        P(None, mp),
        P(mp, None),
    )
    return jax.shard_map(body, mesh=fine, in_specs=in_specs, out_specs=P(tm, mp), check_vma=False)
```

```python
import jax
import jax.numpy as jnp
from jax import lax
from jax.experimental import pallas as pl
from jax.experimental.pallas import tpu as pltpu
from jax.sharding import Mesh, PartitionSpec as P

XLO, Y, CORE, XHI, Z = ("xlo", "y", "core", "xhi", "z")
BF, F32 = (jnp.bfloat16, jnp.float32)
EPS = 1e-05
LANES = 128
SPAN = 15
VMEM = pl.BlockSpec(memory_space=pltpu.VMEM)
HBM = pl.BlockSpec(memory_space=pltpu.HBM)
PARAMS = pltpu.CompilerParams(vmem_limit_bytes=40 << 20)


def shape(dims, dtype):
    return jax.ShapeDtypeStruct(dims, dtype)


def in_hbm(*arrays):
    return [pltpu.with_memory_space_constraint(x, pltpu.HBM) for x in arrays]


def swap(x, axis):
    return lax.ppermute(x, axis, [(0, 1), (1, 0)])


def group_gather(x):
    across = swap(x, XHI)
    beside = swap(x, CORE)
    return x, across, beside, swap(across, CORE)


def norm_rows(x, gain):
    inv = 1.0 / x.shape[0]
    centred = x - jnp.sum(x, axis=0, keepdims=True) * inv
    spread = jnp.sum(centred * centred, axis=0, keepdims=True) * inv
    return (centred * lax.rsqrt(spread + EPS) * gain).astype(BF)


def place():
    return lax.axis_index(CORE), lax.axis_index(XHI)


def at(start, size, step):
    return pl.ds(pl.multiple_of(start, step), size)


def weight_kernel(
    glu, conv_out, depth, gain, shift, tok,
    out, near, first, last,
    table, parts, small, sems,
):
    core, _ = place()
    half = at(32 * core, 32, 32)
    taps, width = depth.shape
    frames = tok.shape[1]
    pairs = [
        (depth, small.at[0:taps]),
        (gain, small.at[32:33]),
        (shift, small.at[40:41]),
        (glu.at[0, half], parts.at[0:32]),
        (glu.at[1, half], parts.at[32:64]),
        (conv_out.at[half], parts.at[64:96]),
        (tok.at[:, 0:LANES], first),
        (tok.at[:, frames - LANES : frames], last),
        (tok, near),
    ]
    loads = [pltpu.make_async_copy(a, b, sems.at[i]) for i, (a, b) in enumerate(pairs)]
    for copy in loads:
        copy.start()
    table[...] = jnp.zeros_like(table)
    for copy in loads[:3]:
        copy.wait()
    table[0:taps, 0:width] = small[0:taps]
    table[taps : taps + 1, 0:width] = small[32:33]
    table[taps + 1 : taps + 2, 0:width] = small[40:41]
    lane = lax.broadcasted_iota(jnp.int32, table.shape, 1)
    rest = jnp.where(core == 0, table[...], pltpu.roll(table[...], LANES - 32, 1))
    rest = jnp.where(lane < 32, rest, 0.0)
    packed = jnp.zeros_like(rest)
    for i in range(3):
        piece = rest.astype(BF).astype(F32)
        packed = packed + (piece if i == 0 else pltpu.roll(piece, 32 * i, 1))
        rest = rest - piece
    parts[96:112] = jnp.zeros((16, parts.shape[1]), BF)
    for i in range(3):
        parts[96:112, LANES * i : LANES * (i + 1)] = packed[16 * i : 16 * i + 16].astype(BF)
    for copy in loads[3:6]:
        copy.wait()
    final = pltpu.make_async_copy(parts, out, sems.at[9])
    final.start()
    for copy in loads[6:] + [final]:
        copy.wait()


def block_kernel(ff_in, ff_out, out):
    half = at(place()[0] * LANES, LANES, LANES)
    for k in range(8):
        tile = slice(LANES * k, LANES * (k + 1))
        out[k] = ff_in[tile, half].astype(F32).T.astype(BF)
        out[8 + k] = ff_out[half, tile].astype(F32).T.astype(BF)


def pack_kernel(tok, left, right, out):
    lane = lax.broadcasted_iota(jnp.int32, (16, LANES), 1)
    nz = out.shape[0]
    for z in range(nz):
        out[z, 0:64] = tok[:, 2 * z * LANES : (2 * z + 1) * LANES]
        out[z, 64:128] = tok[:, (2 * z + 1) * LANES : (2 * z + 2) * LANES]
        packed = jnp.zeros((16, LANES), F32)
        for i in range(4):
            rows = slice(16 * i, 16 * i + 16)
            if z == 0:
                before = left[rows]
            else:
                before = tok[rows, (2 * z - 1) * LANES : 2 * z * LANES]
            if z == nz - 1:
                after = right[rows]
            else:
                after = tok[rows, (2 * z + 2) * LANES : (2 * z + 3) * LANES]
            low = pltpu.roll(before.astype(F32), (32 * i + SPAN) % LANES, 1)
            high = pltpu.roll(after.astype(F32), 32 * i + SPAN, 1)
            packed = jnp.where((lane >= 32 * i) & (lane < 32 * i + SPAN), low, packed)
            packed = jnp.where(
                (lane >= 32 * i + SPAN) & (lane < 32 * i + 2 * SPAN), high, packed
            )
        out[z, 128:144] = packed.astype(BF)


def conv_kernel(
    own, across, beside, far, first, gain,
    conv, stats, par, res,
    tok, edge, win, weight, small, sems,
):
    loads = [
        pltpu.make_async_copy(first.at[:, 0:64], weight, sems.at[0]),
        pltpu.make_async_copy(first.at[:, 96:112, 0:384], small, sems.at[1]),
    ]
    for copy in loads:
        copy.start()
    core, xhi = place()
    lane = lax.broadcasted_iota(jnp.int32, (16, LANES), 1)
    nz = small.shape[0]
    for near, away, side in ((own, beside, xhi), (across, far, 1 - xhi)):
        for z in range(nz):
            row = side * (64 * nz) + 64 * z
            for c, blk in ((0, near), (1, away)):
                tok[at(row, 64, 64), 256 * c : 256 * c + 128] = blk[z, 0:64]
                tok[at(row, 64, 64), 256 * c + 128 : 256 * c + 256] = blk[z, 64:128]
            one = near[z, 128:144].astype(F32)
            two = away[z, 128:144].astype(F32)
            for i in range(4):
                low = pltpu.roll(one, (LANES - 32 * i) % LANES, 1)
                high = pltpu.roll(two, (LANES + 32 - 32 * i) % LANES, 1)
                part = jnp.where(lane < 32, low, jnp.where(lane < 64, high, 0.0))
                edge[at(row + 16 * i, 16, 16), :] = part
    for z in range(nz):
        row = xhi * (64 * nz) + 64 * z + 32 * core
        res[32 * z : 32 * z + 32, :] = tok[at(row, 32, 32), :]

    for copy in loads:
        copy.wait()
    table = []
    lane = lax.broadcasted_iota(jnp.int32, (48, LANES), 1)
    for h in range(2):
        total = jnp.zeros((48, LANES), F32)
        for i in range(4):
            x = [small[4 * h + i, :, LANES * k : LANES * (k + 1)] for k in range(3)]
            x = jnp.concatenate(x, axis=0).astype(F32)
            x = x + (pltpu.roll(x, LANES - 32, 1) + pltpu.roll(x, LANES - 64, 1))
            x = jnp.where(lane < 32, x, 0.0)
            total = total + (x if i == 0 else pltpu.roll(x, 32 * i, 1))
        par[:, LANES * h : LANES * (h + 1)] = total[31:39]
        table.append(total)
    glu = weight[...].reshape(64 * nz, weight.shape[2])
    scale = gain[...]
    for c in range(3):
        x = edge[...] if c == 2 else tok[:, 256 * c : 256 * (c + 1)].astype(F32)
        paired = jnp.dot(glu, norm_rows(x, scale), preferred_element_type=F32)
        cols = x.shape[1]
        paired = paired.reshape(nz, 2, 32, cols)
        gated = (paired[:, 0] * jax.nn.sigmoid(paired[:, 1])).astype(BF).astype(F32)
        gated = gated.reshape(32 * nz, cols).T
        if c < 2:
            win[c, 16:272, :] = gated
        else:
            for r in range(2):
                win[r, 1:16, :] = gated[32 * r : 32 * r + 15]
                win[r, 272:287, :] = gated[32 * r + 15 : 32 * r + 30]

    step = 64
    for h in range(2):
        cols = slice(LANES * h, LANES * (h + 1))
        total = jnp.zeros((1, LANES), F32)
        for r in range(2):
            for k in range(256 // step):
                acc = jnp.zeros((step, LANES), F32)
                for j in range(31):
                    first = step * k + 1 + j
                    acc = acc + table[h][j : j + 1] * win[r, first : first + step, cols]
                conv[256 * r + step * k : 256 * r + step * (k + 1), cols] = acc
                total = total + jnp.sum(acc, axis=0, keepdims=True)
        mean = total * (1.0 / 512)
        apart = conv[:, cols] - mean
        square = jnp.sum(apart * apart, axis=0, keepdims=True)
        n = stats.shape[0]
        stats[:, h : h + 1, :] = jnp.broadcast_to(mean[None], (n, 1, LANES))
        stats[:, 2 + h : 3 + h, :] = jnp.broadcast_to(square[None], (n, 1, LANES))


def merged(stats, count):
    total = jnp.sum(stats, axis=0)
    mean = total * (1.0 / stats.shape[0])
    apart = stats - mean[None]
    apart = jnp.sum(apart * apart, axis=0)
    return mean[0:2], total[2:4] + count * apart[0:2]


def merge_kernel(stats, out):
    mean, square = merged(stats[...], 512)
    out[:, 0:2] = jnp.broadcast_to(mean[None], (out.shape[0],) + mean.shape)
    out[:, 2:4] = jnp.broadcast_to(square[None], (out.shape[0],) + square.shape)


def bn_kernel(conv, stats, par, out):
    frames = 8 * conv.shape[0]
    mean, square = merged(stats[...], frames)
    scale = lax.rsqrt(square * (1.0 / (frames * stats.shape[0])) + EPS)
    for h in range(2):
        cols = slice(LANES * h, LANES * (h + 1))
        value = (conv[:, cols] - mean[h : h + 1]) * (scale[h : h + 1] * par[0:1, cols])
        value = value + par[1:2, cols]
        out[cols, :] = (value * jax.nn.sigmoid(value)).T.astype(BF)


def place_blocks(own, across, beside, far, whole):
    core, xhi = place()
    nz, half = 8, 256
    for blk, c, x in ((own, core, xhi), (across, core, 1 - xhi)):
        for z in range(nz):
            row = x * 512 + 64 * z + 32 * c
            whole[at(row, 32, 32), :] = blk[32 * z : 32 * z + 32, :]
    for blk, c, x in ((beside, 1 - core, xhi), (far, 1 - core, 1 - xhi)):
        for z in range(nz):
            row = x * 512 + 64 * z + 32 * c
            whole[at(row, 32, 32), :half] = blk[32 * z : 32 * z + 32, half:]
            whole[at(row, 32, 32), half:] = blk[32 * z : 32 * z + 32, :half]


def mix_kernel(own, across, beside, far, blocks, res, out, whole):
    place_blocks(own, across, beside, far, whole)
    weight = blocks[...].reshape(256, blocks.shape[2])
    mixed = jnp.dot(weight, whole[...], preferred_element_type=F32)
    out[...] = (res[...].astype(F32) + mixed).astype(BF)


def norm_kernel(own, across, beside, far, gain, near, normed, whole):
    place_blocks(own, across, beside, far, whole)
    half = normed.shape[1] // 2
    near[...] = whole[:, :half]
    for c in range(2):
        cols = slice(half * c, half * (c + 1))
        normed[:, cols] = norm_rows(whole[:, cols].astype(F32), gain[...])


def ff_kernel(near, normed, blocks, keep, give, hidden, w, sems):
    loads = [
        pltpu.make_async_copy(
            blocks.at[2 * i : 2 * i + 2, 0:8], w.at[2 * i : 2 * i + 2, 0:8], sems.at[i]
        )
        for i in range(4)
    ]
    loads.append(pltpu.make_async_copy(blocks.at[:, 8:16], w.at[:, 8:16], sems.at[4]))
    for copy in loads:
        copy.start()
    xhi = place()[1]
    half = normed.shape[1] // 2
    for z in range(0, 8, 2):
        loads[z // 2].wait()
        rows = [jnp.concatenate([w[z + i, k] for k in range(8)], axis=1) for i in range(2)]
        value = jnp.dot(
            jnp.concatenate(rows, axis=0), normed[...], preferred_element_type=F32
        )
        hidden[LANES * z : LANES * (z + 2), :] = (value * jax.nn.sigmoid(value)).astype(BF)
    loads[4].wait()
    for k in range(0, 8, 2):
        rows = [jnp.concatenate([w[z, 8 + k + i] for z in range(8)], axis=1) for i in range(2)]
        value = jnp.dot(
            jnp.concatenate(rows, axis=0), hidden[...], preferred_element_type=F32
        )
        rows = slice(LANES * k, LANES * (k + 2))
        mine = jnp.where(xhi == k // 4, 1.0, 0.0)
        keep[rows, :] = 0.5 * value[:, :half] + mine * near[rows, :].astype(F32)
        give[rows, :] = (0.5 * value[:, half:]).astype(BF)


def sum_kernel(parts, out):
    nz, run = parts.shape[0] // 2, parts.shape[2]
    for z in range(nz):
        value = parts[z].astype(F32) + parts[nz + z].astype(F32)
        out[:, run * z : run * (z + 1)] = value.astype(BF)


def body(
    tokens,
    ln_conv_gain,
    glu_weight,
    depth_weight,
    bn_gain,
    bn_shift,
    conv_out_weight,
    ln_ff_gain,
    ff_in_weight,
    ff_out_weight,
):
    nz = lax.axis_size(Z)
    frames, width = tokens.shape
    full = ln_conv_gain.shape[0]
    run = frames // nz

    first, tok, head, tail = pl.pallas_call(
        weight_kernel,
        out_shape=(
            shape((112, full), BF),
            shape((width, frames), BF),
            shape((width, LANES), BF),
            shape((width, LANES), BF),
        ),
        in_specs=[HBM] * 6,
        out_specs=(HBM, VMEM, VMEM, VMEM),
        scratch_shapes=[
            pltpu.VMEM((48, LANES), F32),
            pltpu.VMEM((112, full), BF),
            pltpu.VMEM((48, width), F32),
            pltpu.SemaphoreType.DMA((10,)),
        ],
        compiler_params=PARAMS,
        name="weights",
    )(
        *in_hbm(
            glu_weight.transpose(1, 2, 0),
            conv_out_weight.T,
            depth_weight,
            bn_gain[None],
            bn_shift[None],
            tokens.T,
        )
    )
    first = lax.all_gather(first, Z)

    tm = lax.axis_size((XLO, Y, CORE))
    up = [(i, i + 1) for i in range(tm - 1)]
    left = lax.ppermute(tail, (XLO, Y, CORE), up)
    right = lax.ppermute(head, (XLO, Y, CORE), [(j, i) for i, j in up])
    parts = pl.pallas_call(
        pack_kernel,
        out_shape=shape((nz, 144, LANES), BF),
        in_specs=[VMEM] * 3,
        out_specs=VMEM,
        compiler_params=PARAMS,
        name="pack",
    )(tok, left, right)
    parts = lax.all_to_all(parts, Z, 0, 0, tiled=True)

    blocks = pl.pallas_call(
        block_kernel,
        out_shape=shape((16, LANES, LANES), BF),
        in_specs=[VMEM] * 2,
        out_specs=VMEM,
        compiler_params=PARAMS,
        name="blocks",
    )(ff_in_weight, ff_out_weight)
    blocks, parts = lax.optimization_barrier((blocks, parts))
    blocks = lax.all_gather(blocks, Z)

    whole = group_gather(parts)
    conv, stats, par, res = pl.pallas_call(
        conv_kernel,
        out_shape=(
            shape((2 * run, 256), F32),
            shape((nz, 4, LANES), F32),
            shape((8, 256), F32),
            shape((256, 2 * run), BF),
        ),
        in_specs=[VMEM] * 4 + [HBM, VMEM],
        out_specs=(VMEM,) * 4,
        scratch_shapes=[
            pltpu.VMEM((full, 2 * run), BF),
            pltpu.VMEM((full, LANES), F32),
            pltpu.VMEM((2, run + 40, 256), F32),
            pltpu.VMEM((nz, 64, full), BF),
            pltpu.VMEM((nz, 16, 3 * LANES), BF),
            pltpu.SemaphoreType.DMA((2,)),
        ],
        compiler_params=PARAMS,
        name="conv",
    )(*whole, *in_hbm(first), ln_conv_gain[:, None])
    stats = lax.all_to_all(stats, Z, 0, 0, tiled=True)
    stats = pl.pallas_call(
        merge_kernel,
        out_shape=shape((lax.axis_size((XLO, Y)), 4, LANES), F32),
        in_specs=[VMEM],
        out_specs=VMEM,
        compiler_params=PARAMS,
        name="merge",
    )(stats)
    stats = lax.all_to_all(stats, (XLO, Y), 0, 0, tiled=True)
    activated = pl.pallas_call(
        bn_kernel,
        out_shape=shape((256, 2 * run), BF),
        in_specs=[VMEM] * 3,
        out_specs=VMEM,
        compiler_params=PARAMS,
        name="bn",
    )(conv, stats, par)
    block = pl.pallas_call(
        mix_kernel,
        out_shape=shape((256, 2 * run), BF),
        grid=(1,),
        in_specs=[VMEM] * 4
        + [
            pl.BlockSpec((nz, 32, full), lambda i: (0, 2, 0)),
            VMEM,
        ],
        out_specs=VMEM,
        scratch_shapes=[pltpu.VMEM((full, 2 * run), BF)],
        compiler_params=PARAMS,
        name="mix",
    )(*group_gather(activated), first, res)
    near, normed = pl.pallas_call(
        norm_kernel,
        out_shape=(shape((full, run), BF), shape((full, 2 * run), BF)),
        in_specs=[VMEM] * 5,
        out_specs=(VMEM,) * 2,
        scratch_shapes=[pltpu.VMEM((full, 2 * run), BF)],
        compiler_params=PARAMS,
        name="norm",
    )(*group_gather(block), ln_ff_gain[:, None])
    keep, give = pl.pallas_call(
        ff_kernel,
        out_shape=(shape((full, run), F32), shape((full, run), BF)),
        in_specs=[VMEM] * 2 + [HBM],
        out_specs=(VMEM,) * 2,
        scratch_shapes=[
            pltpu.VMEM((full, 2 * run), BF),
            pltpu.VMEM((nz, 16, LANES, LANES), BF),
            pltpu.SemaphoreType.DMA((5,)),
        ],
        compiler_params=PARAMS,
        name="ff",
    )(near, normed, *in_hbm(blocks))
    keep = (keep + swap(give, CORE).astype(F32)).astype(BF)
    keep = lax.all_to_all(keep.reshape(2 * nz, width, run), (XHI, Z), 0, 0, tiled=True)
    out = pl.pallas_call(
        sum_kernel,
        out_shape=shape((width, frames), BF),
        in_specs=[VMEM],
        out_specs=VMEM,
        compiler_params=PARAMS,
        name="sum",
    )(keep)
    return out.T


def solution(mesh):
    fine = Mesh(mesh.devices.reshape(2, 8, 2, 2, 8), (XLO, Y, CORE, XHI, Z))
    tm, mp = ((XLO, Y, CORE), (XHI, Z))
    in_specs = (
        P(tm, mp),
        P(),
        P(None, None, mp),
        P(None, mp),
        P(mp),
        P(mp),
        P(None, mp),
        P(),
        P(None, mp),
        P(mp, None),
    )
    return jax.shard_map(body, mesh=fine, in_specs=in_specs, out_specs=P(tm, mp), check_vma=False)
```

```python
import jax
import jax.numpy as jnp
from jax import lax
from jax.experimental import pallas as pl
from jax.experimental.pallas import tpu as pltpu
from jax.sharding import Mesh, PartitionSpec as P

XLO, Y, CORE, XHI, Z = ("xlo", "y", "core", "xhi", "z")
BF, F32 = (jnp.bfloat16, jnp.float32)
EPS = 1e-05
LANES = 128
SPAN = 15
VMEM = pl.BlockSpec(memory_space=pltpu.VMEM)
HBM = pl.BlockSpec(memory_space=pltpu.HBM)
PARAMS = pltpu.CompilerParams(vmem_limit_bytes=40 << 20)


def shape(dims, dtype):
    return jax.ShapeDtypeStruct(dims, dtype)


def in_hbm(*arrays):
    return [pltpu.with_memory_space_constraint(x, pltpu.HBM) for x in arrays]


def swap(x, axis):
    return lax.ppermute(x, axis, [(0, 1), (1, 0)])


def group_gather(x):
    across = swap(x, XHI)
    beside = swap(x, CORE)
    return x, across, beside, swap(across, CORE)


def norm_rows(x, gain):
    inv = 1.0 / x.shape[0]
    centred = x - jnp.sum(x, axis=0, keepdims=True) * inv
    spread = jnp.sum(centred * centred, axis=0, keepdims=True) * inv
    return (centred * lax.rsqrt(spread + EPS) * gain).astype(BF)


def place():
    return lax.axis_index(CORE), lax.axis_index(XHI)


def at(start, size, step):
    return pl.ds(pl.multiple_of(start, step), size)


def weight_kernel(
    glu, conv_out, depth, gain, shift, tok,
    out, near, first, last,
    table, parts, small, sems,
):
    core, _ = place()
    half = at(32 * core, 32, 32)
    taps, width = depth.shape
    frames = tok.shape[1]
    pairs = [
        (depth, small.at[0:taps]),
        (gain, small.at[32:33]),
        (shift, small.at[40:41]),
        (glu.at[0, half], parts.at[0:32]),
        (glu.at[1, half], parts.at[32:64]),
        (conv_out, parts.at[64:128]),
        (tok.at[:, 0:LANES], first),
        (tok.at[:, frames - LANES : frames], last),
        (tok, near),
    ]
    loads = [pltpu.make_async_copy(a, b, sems.at[i]) for i, (a, b) in enumerate(pairs)]
    for copy in loads:
        copy.start()
    table[...] = jnp.zeros_like(table)
    for copy in loads[:3]:
        copy.wait()
    table[0:taps, 0:width] = small[0:taps]
    table[taps : taps + 1, 0:width] = small[32:33]
    table[taps + 1 : taps + 2, 0:width] = small[40:41]
    lane = lax.broadcasted_iota(jnp.int32, table.shape, 1)
    rest = jnp.where(core == 0, table[...], pltpu.roll(table[...], LANES - 32, 1))
    rest = jnp.where(lane < 32, rest, 0.0)
    packed = jnp.zeros_like(rest)
    for i in range(3):
        piece = rest.astype(BF).astype(F32)
        packed = packed + (piece if i == 0 else pltpu.roll(piece, 32 * i, 1))
        rest = rest - piece
    parts[128:144] = jnp.zeros((16, parts.shape[1]), BF)
    for i in range(3):
        parts[128:144, LANES * i : LANES * (i + 1)] = packed[16 * i : 16 * i + 16].astype(BF)
    for copy in loads[3:6]:
        copy.wait()
    final = pltpu.make_async_copy(parts, out, sems.at[9])
    final.start()
    for copy in loads[6:] + [final]:
        copy.wait()


def block_kernel(ff_in, ff_out, out):
    half = at(place()[0] * LANES, LANES, LANES)
    for k in range(8):
        tile = slice(LANES * k, LANES * (k + 1))
        out[k] = ff_in[tile, half].astype(F32).T.astype(BF)
        out[8 + k] = ff_out[half, tile].astype(F32).T.astype(BF)


def pack_kernel(tok, left, right, out):
    lane = lax.broadcasted_iota(jnp.int32, (16, LANES), 1)
    nz = out.shape[0]
    for z in range(nz):
        out[z, 0:64] = tok[:, 2 * z * LANES : (2 * z + 1) * LANES]
        out[z, 64:128] = tok[:, (2 * z + 1) * LANES : (2 * z + 2) * LANES]
        packed = jnp.zeros((16, LANES), F32)
        for i in range(4):
            rows = slice(16 * i, 16 * i + 16)
            if z == 0:
                before = left[rows]
            else:
                before = tok[rows, (2 * z - 1) * LANES : 2 * z * LANES]
            if z == nz - 1:
                after = right[rows]
            else:
                after = tok[rows, (2 * z + 2) * LANES : (2 * z + 3) * LANES]
            low = pltpu.roll(before.astype(F32), (32 * i + SPAN) % LANES, 1)
            high = pltpu.roll(after.astype(F32), 32 * i + SPAN, 1)
            packed = jnp.where((lane >= 32 * i) & (lane < 32 * i + SPAN), low, packed)
            packed = jnp.where(
                (lane >= 32 * i + SPAN) & (lane < 32 * i + 2 * SPAN), high, packed
            )
        out[z, 128:144] = packed.astype(BF)


def conv_kernel(
    own, across, beside, far, first, gain,
    conv, stats, par, res,
    tok, edge, win, weight, small, sems,
):
    loads = [
        pltpu.make_async_copy(first.at[:, 0:64], weight, sems.at[0]),
        pltpu.make_async_copy(first.at[:, 128:144, 0:384], small, sems.at[1]),
    ]
    for copy in loads:
        copy.start()
    core, xhi = place()
    lane = lax.broadcasted_iota(jnp.int32, (16, LANES), 1)
    nz = small.shape[0]
    for near, away, side in ((own, beside, xhi), (across, far, 1 - xhi)):
        for z in range(nz):
            row = side * (64 * nz) + 64 * z
            for c, blk in ((0, near), (1, away)):
                tok[at(row, 64, 64), 256 * c : 256 * c + 128] = blk[z, 0:64]
                tok[at(row, 64, 64), 256 * c + 128 : 256 * c + 256] = blk[z, 64:128]
            one = near[z, 128:144].astype(F32)
            two = away[z, 128:144].astype(F32)
            for i in range(4):
                low = pltpu.roll(one, (LANES - 32 * i) % LANES, 1)
                high = pltpu.roll(two, (LANES + 32 - 32 * i) % LANES, 1)
                part = jnp.where(lane < 32, low, jnp.where(lane < 64, high, 0.0))
                edge[at(row + 16 * i, 16, 16), :] = part
    res[...] = tok[at(xhi * (64 * nz), 64 * nz, 64 * nz), 0:256]

    for copy in loads:
        copy.wait()
    table = []
    lane = lax.broadcasted_iota(jnp.int32, (48, LANES), 1)
    for h in range(2):
        total = jnp.zeros((48, LANES), F32)
        for i in range(4):
            x = [small[4 * h + i, :, LANES * k : LANES * (k + 1)] for k in range(3)]
            x = jnp.concatenate(x, axis=0).astype(F32)
            x = x + (pltpu.roll(x, LANES - 32, 1) + pltpu.roll(x, LANES - 64, 1))
            x = jnp.where(lane < 32, x, 0.0)
            total = total + (x if i == 0 else pltpu.roll(x, 32 * i, 1))
        par[:, LANES * h : LANES * (h + 1)] = total[31:39]
        table.append(total)
    glu = weight[...].reshape(64 * nz, weight.shape[2])
    scale = gain[...]
    for c in range(3):
        x = edge[...] if c == 2 else tok[:, 256 * c : 256 * (c + 1)].astype(F32)
        paired = jnp.dot(glu, norm_rows(x, scale), preferred_element_type=F32)
        cols = x.shape[1]
        paired = paired.reshape(nz, 2, 32, cols)
        gated = (paired[:, 0] * jax.nn.sigmoid(paired[:, 1])).astype(BF).astype(F32)
        gated = gated.reshape(32 * nz, cols).T
        if c < 2:
            win[c, 16:272, :] = gated
        else:
            for r in range(2):
                win[r, 1:16, :] = gated[32 * r : 32 * r + 15]
                win[r, 272:287, :] = gated[32 * r + 15 : 32 * r + 30]

    step = 64
    for h in range(2):
        cols = slice(LANES * h, LANES * (h + 1))
        total = jnp.zeros((1, LANES), F32)
        for r in range(2):
            for k in range(256 // step):
                acc = jnp.zeros((step, LANES), F32)
                for j in range(31):
                    first = step * k + 1 + j
                    acc = acc + table[h][j : j + 1] * win[r, first : first + step, cols]
                conv[256 * r + step * k : 256 * r + step * (k + 1), cols] = acc
                total = total + jnp.sum(acc, axis=0, keepdims=True)
        mean = total * (1.0 / 512)
        apart = conv[:, cols] - mean
        square = jnp.sum(apart * apart, axis=0, keepdims=True)
        n = stats.shape[0]
        stats[:, h : h + 1, :] = jnp.broadcast_to(mean[None], (n, 1, LANES))
        stats[:, 2 + h : 3 + h, :] = jnp.broadcast_to(square[None], (n, 1, LANES))


def merged(stats, count):
    total = jnp.sum(stats, axis=0)
    mean = total * (1.0 / stats.shape[0])
    apart = stats - mean[None]
    apart = jnp.sum(apart * apart, axis=0)
    return mean[0:2], total[2:4] + count * apart[0:2]


def merge_kernel(stats, out):
    mean, square = merged(stats[...], 512)
    out[:, 0:2] = jnp.broadcast_to(mean[None], (out.shape[0],) + mean.shape)
    out[:, 2:4] = jnp.broadcast_to(square[None], (out.shape[0],) + square.shape)


def bn_kernel(conv, stats, par, near, away):
    frames = 8 * conv.shape[0]
    mean, square = merged(stats[...], frames)
    scale = lax.rsqrt(square * (1.0 / (frames * stats.shape[0])) + EPS)
    for h in range(2):
        cols = slice(LANES * h, LANES * (h + 1))
        value = (conv[:, cols] - mean[h : h + 1]) * (scale[h : h + 1] * par[0:1, cols])
        value = value + par[1:2, cols]
        value = (value * jax.nn.sigmoid(value)).T.astype(BF)
        half = near.shape[1]
        near[cols, :] = value[:, :half]
        away[cols, :] = value[:, half:]


def mix_kernel(own, across, beside, far, weight, res, out, whole):
    core, xhi = place()
    for blk, c, x in (
        (own, core, xhi),
        (across, core, 1 - xhi),
        (beside, 1 - core, xhi),
        (far, 1 - core, 1 - xhi),
    ):
        for z in range(8):
            row = x * 512 + 64 * z + 32 * c
            whole[at(row, 32, 32), :] = blk[32 * z : 32 * z + 32, :]
    w = weight[...].reshape(512, weight.shape[2])
    mixed = jnp.dot(w, whole[...], preferred_element_type=F32)
    out[...] = (res[...].astype(F32) + mixed).astype(BF)


def norm_kernel(own, across, beside, far, gain, near, normed, whole):
    xhi = place()[1]
    size, half = own.shape
    whole[at(xhi * size, size, size), :half] = own[...]
    whole[at((1 - xhi) * size, size, size), :half] = across[...]
    whole[at(xhi * size, size, size), half:] = beside[...]
    whole[at((1 - xhi) * size, size, size), half:] = far[...]
    near[...] = whole[:, :half]
    for c in range(2):
        cols = slice(half * c, half * (c + 1))
        normed[:, cols] = norm_rows(whole[:, cols].astype(F32), gain[...])


def ff_kernel(near, normed, blocks, keep, give, hidden, w, sems):
    loads = [
        pltpu.make_async_copy(
            blocks.at[2 * i : 2 * i + 2, 0:8], w.at[2 * i : 2 * i + 2, 0:8], sems.at[i]
        )
        for i in range(4)
    ]
    loads.append(pltpu.make_async_copy(blocks.at[:, 8:16], w.at[:, 8:16], sems.at[4]))
    for copy in loads:
        copy.start()
    xhi = place()[1]
    half = normed.shape[1] // 2
    for z in range(0, 8, 2):
        loads[z // 2].wait()
        rows = [jnp.concatenate([w[z + i, k] for k in range(8)], axis=1) for i in range(2)]
        value = jnp.dot(
            jnp.concatenate(rows, axis=0), normed[...], preferred_element_type=F32
        )
        hidden[LANES * z : LANES * (z + 2), :] = (value * jax.nn.sigmoid(value)).astype(BF)
    loads[4].wait()
    for k in range(0, 8, 2):
        rows = [jnp.concatenate([w[z, 8 + k + i] for z in range(8)], axis=1) for i in range(2)]
        value = jnp.dot(
            jnp.concatenate(rows, axis=0), hidden[...], preferred_element_type=F32
        )
        rows = slice(LANES * k, LANES * (k + 2))
        mine = jnp.where(xhi == k // 4, 1.0, 0.0)
        keep[rows, :] = 0.5 * value[:, :half] + mine * near[rows, :].astype(F32)
        give[rows, :] = (0.5 * value[:, half:]).astype(BF)


def sum_kernel(parts, out):
    nz, run = parts.shape[0] // 2, parts.shape[2]
    for z in range(nz):
        value = parts[z].astype(F32) + parts[nz + z].astype(F32)
        out[:, run * z : run * (z + 1)] = value.astype(BF)


def body(
    tokens,
    ln_conv_gain,
    glu_weight,
    depth_weight,
    bn_gain,
    bn_shift,
    conv_out_weight,
    ln_ff_gain,
    ff_in_weight,
    ff_out_weight,
):
    nz = lax.axis_size(Z)
    frames, width = tokens.shape
    full = ln_conv_gain.shape[0]
    run = frames // nz

    first, tok, head, tail = pl.pallas_call(
        weight_kernel,
        out_shape=(
            shape((144, full), BF),
            shape((width, frames), BF),
            shape((width, LANES), BF),
            shape((width, LANES), BF),
        ),
        in_specs=[HBM] * 6,
        out_specs=(HBM, VMEM, VMEM, VMEM),
        scratch_shapes=[
            pltpu.VMEM((48, LANES), F32),
            pltpu.VMEM((144, full), BF),
            pltpu.VMEM((48, width), F32),
            pltpu.SemaphoreType.DMA((10,)),
        ],
        compiler_params=PARAMS,
        name="weights",
    )(
        *in_hbm(
            glu_weight.transpose(1, 2, 0),
            conv_out_weight.T,
            depth_weight,
            bn_gain[None],
            bn_shift[None],
            tokens.T,
        )
    )
    first = lax.all_gather(first, Z)

    tm = lax.axis_size((XLO, Y, CORE))
    up = [(i, i + 1) for i in range(tm - 1)]
    left = lax.ppermute(tail, (XLO, Y, CORE), up)
    right = lax.ppermute(head, (XLO, Y, CORE), [(j, i) for i, j in up])
    parts = pl.pallas_call(
        pack_kernel,
        out_shape=shape((nz, 144, LANES), BF),
        in_specs=[VMEM] * 3,
        out_specs=VMEM,
        compiler_params=PARAMS,
        name="pack",
    )(tok, left, right)
    parts = lax.all_to_all(parts, Z, 0, 0, tiled=True)

    blocks = pl.pallas_call(
        block_kernel,
        out_shape=shape((16, LANES, LANES), BF),
        in_specs=[VMEM] * 2,
        out_specs=VMEM,
        compiler_params=PARAMS,
        name="blocks",
    )(ff_in_weight, ff_out_weight)
    blocks, parts = lax.optimization_barrier((blocks, parts))
    blocks = lax.all_gather(blocks, Z)

    whole = group_gather(parts)
    conv, stats, par, res = pl.pallas_call(
        conv_kernel,
        out_shape=(
            shape((2 * run, 256), F32),
            shape((nz, 4, LANES), F32),
            shape((8, 256), F32),
            shape((full // 2, run), BF),
        ),
        in_specs=[VMEM] * 4 + [HBM, VMEM],
        out_specs=(VMEM,) * 4,
        scratch_shapes=[
            pltpu.VMEM((full, 2 * run), BF),
            pltpu.VMEM((full, LANES), F32),
            pltpu.VMEM((2, run + 40, 256), F32),
            pltpu.VMEM((nz, 64, full), BF),
            pltpu.VMEM((nz, 16, 3 * LANES), BF),
            pltpu.SemaphoreType.DMA((2,)),
        ],
        compiler_params=PARAMS,
        name="conv",
    )(*whole, *in_hbm(first), ln_conv_gain[:, None])
    stats = lax.all_to_all(stats, Z, 0, 0, tiled=True)
    stats = pl.pallas_call(
        merge_kernel,
        out_shape=shape((lax.axis_size((XLO, Y)), 4, LANES), F32),
        in_specs=[VMEM],
        out_specs=VMEM,
        compiler_params=PARAMS,
        name="merge",
    )(stats)
    stats = lax.all_to_all(stats, (XLO, Y), 0, 0, tiled=True)
    own, other = pl.pallas_call(
        bn_kernel,
        out_shape=(shape((256, run), BF),) * 2,
        in_specs=[VMEM] * 3,
        out_specs=(VMEM,) * 2,
        compiler_params=PARAMS,
        name="bn",
    )(conv, stats, par)
    across = swap(own, XHI)
    far = lax.ppermute(other, (CORE, XHI), [(i, 3 - i) for i in range(4)])
    beside = swap(other, CORE)
    block = pl.pallas_call(
        mix_kernel,
        out_shape=shape((full // 2, run), BF),
        grid=(1,),
        in_specs=[VMEM] * 4
        + [
            pl.BlockSpec((nz, 64, full), lambda i: (0, 1, 0)),
            VMEM,
        ],
        out_specs=VMEM,
        scratch_shapes=[pltpu.VMEM((full, run), BF)],
        compiler_params=PARAMS,
        name="mix",
    )(own, across, beside, far, first, res)
    near, normed = pl.pallas_call(
        norm_kernel,
        out_shape=(shape((full, run), BF), shape((full, 2 * run), BF)),
        in_specs=[VMEM] * 5,
        out_specs=(VMEM,) * 2,
        scratch_shapes=[pltpu.VMEM((full, 2 * run), BF)],
        compiler_params=PARAMS,
        name="norm",
    )(*group_gather(block), ln_ff_gain[:, None])
    keep, give = pl.pallas_call(
        ff_kernel,
        out_shape=(shape((full, run), F32), shape((full, run), BF)),
        in_specs=[VMEM] * 2 + [HBM],
        out_specs=(VMEM,) * 2,
        scratch_shapes=[
            pltpu.VMEM((full, 2 * run), BF),
            pltpu.VMEM((nz, 16, LANES, LANES), BF),
            pltpu.SemaphoreType.DMA((5,)),
        ],
        compiler_params=PARAMS,
        name="ff",
    )(near, normed, *in_hbm(blocks))
    keep = (keep + swap(give, CORE).astype(F32)).astype(BF)
    keep = lax.all_to_all(keep.reshape(2 * nz, width, run), (XHI, Z), 0, 0, tiled=True)
    out = pl.pallas_call(
        sum_kernel,
        out_shape=shape((width, frames), BF),
        in_specs=[VMEM],
        out_specs=VMEM,
        compiler_params=PARAMS,
        name="sum",
    )(keep)
    return out.T


def solution(mesh):
    fine = Mesh(mesh.devices.reshape(2, 8, 2, 2, 8), (XLO, Y, CORE, XHI, Z))
    tm, mp = ((XLO, Y, CORE), (XHI, Z))
    in_specs = (
        P(tm, mp),
        P(),
        P(None, None, mp),
        P(None, mp),
        P(mp),
        P(mp),
        P(None, mp),
        P(),
        P(None, mp),
        P(mp, None),
    )
    return jax.shard_map(body, mesh=fine, in_specs=in_specs, out_specs=P(tm, mp), check_vma=False)
```

```python
import jax
import jax.numpy as jnp
from jax import lax
from jax.experimental import pallas as pl
from jax.experimental.pallas import tpu as pltpu
from jax.sharding import Mesh, PartitionSpec as P

XLO, Y, CORE, XHI, Z = ("xlo", "y", "core", "xhi", "z")
BF, F32 = (jnp.bfloat16, jnp.float32)
EPS = 1e-05
LANES = 128
SPAN = 15
VMEM = pl.BlockSpec(memory_space=pltpu.VMEM)
HBM = pl.BlockSpec(memory_space=pltpu.HBM)
PARAMS = pltpu.CompilerParams(vmem_limit_bytes=40 << 20)


def shape(dims, dtype):
    return jax.ShapeDtypeStruct(dims, dtype)


def in_hbm(*arrays):
    return [pltpu.with_memory_space_constraint(x, pltpu.HBM) for x in arrays]


def swap(x, axis):
    return lax.ppermute(x, axis, [(0, 1), (1, 0)])


def group_gather(x):
    across = swap(x, XHI)
    beside = swap(x, CORE)
    return x, across, beside, swap(across, CORE)


def norm_rows(x, gain):
    inv = 1.0 / x.shape[0]
    centred = x - jnp.sum(x, axis=0, keepdims=True) * inv
    spread = jnp.sum(centred * centred, axis=0, keepdims=True) * inv
    return (centred * lax.rsqrt(spread + EPS) * gain).astype(BF)


def place():
    return lax.axis_index(CORE), lax.axis_index(XHI)


def at(start, size, step):
    return pl.ds(pl.multiple_of(start, step), size)


def weight_kernel(
    glu, conv_out, depth, gain, shift, tok,
    out, near, first, last,
    table, parts, small, sems,
):
    core, _ = place()
    half = at(32 * core, 32, 32)
    taps, width = depth.shape
    frames = tok.shape[1]
    pairs = [
        (depth, small.at[0:taps]),
        (gain, small.at[32:33]),
        (shift, small.at[40:41]),
        (glu.at[0, half], parts.at[0:32]),
        (glu.at[1, half], parts.at[32:64]),
        (conv_out.at[half], parts.at[64:96]),
        (tok.at[:, 0:LANES], first),
        (tok.at[:, frames - LANES : frames], last),
        (tok, near),
    ]
    loads = [pltpu.make_async_copy(a, b, sems.at[i]) for i, (a, b) in enumerate(pairs)]
    for copy in loads:
        copy.start()
    table[...] = jnp.zeros_like(table)
    for copy in loads[:3]:
        copy.wait()
    table[0:taps, 0:width] = small[0:taps]
    table[taps : taps + 1, 0:width] = small[32:33]
    table[taps + 1 : taps + 2, 0:width] = small[40:41]
    lane = lax.broadcasted_iota(jnp.int32, table.shape, 1)
    rest = jnp.where(core == 0, table[...], pltpu.roll(table[...], LANES - 32, 1))
    rest = jnp.where(lane < 32, rest, 0.0)
    packed = jnp.zeros_like(rest)
    for i in range(3):
        piece = rest.astype(BF).astype(F32)
        packed = packed + (piece if i == 0 else pltpu.roll(piece, 32 * i, 1))
        rest = rest - piece
    parts[96:112] = jnp.zeros((16, parts.shape[1]), BF)
    for i in range(3):
        parts[96:112, LANES * i : LANES * (i + 1)] = packed[16 * i : 16 * i + 16].astype(BF)
    for copy in loads[3:6]:
        copy.wait()
    final = pltpu.make_async_copy(parts, out, sems.at[9])
    final.start()
    for copy in loads[6:] + [final]:
        copy.wait()


def block_kernel(ff_in, ff_out, out):
    half = at(place()[0] * LANES, LANES, LANES)
    for k in range(8):
        tile = slice(LANES * k, LANES * (k + 1))
        out[k] = ff_in[tile, half].astype(F32).T.astype(BF)
        out[8 + k] = ff_out[half, tile].astype(F32).T.astype(BF)


def pack_kernel(tok, left, right, out):
    lane = lax.broadcasted_iota(jnp.int32, (16, LANES), 1)
    nz = out.shape[0]
    for z in range(nz):
        out[z, 0:64] = tok[:, 2 * z * LANES : (2 * z + 1) * LANES]
        out[z, 64:128] = tok[:, (2 * z + 1) * LANES : (2 * z + 2) * LANES]
        packed = jnp.zeros((16, LANES), F32)
        for i in range(4):
            rows = slice(16 * i, 16 * i + 16)
            if z == 0:
                before = left[rows]
            else:
                before = tok[rows, (2 * z - 1) * LANES : 2 * z * LANES]
            if z == nz - 1:
                after = right[rows]
            else:
                after = tok[rows, (2 * z + 2) * LANES : (2 * z + 3) * LANES]
            low = pltpu.roll(before.astype(F32), (32 * i + SPAN) % LANES, 1)
            high = pltpu.roll(after.astype(F32), 32 * i + SPAN, 1)
            packed = jnp.where((lane >= 32 * i) & (lane < 32 * i + SPAN), low, packed)
            packed = jnp.where(
                (lane >= 32 * i + SPAN) & (lane < 32 * i + 2 * SPAN), high, packed
            )
        out[z, 128:144] = packed.astype(BF)


def gather_kernel(own, across, beside, far, gain, normed, res, tok, edge):
    core, xhi = place()
    lane = lax.broadcasted_iota(jnp.int32, (16, LANES), 1)
    nz = own.shape[0]
    for near, away, side in ((own, beside, xhi), (across, far, 1 - xhi)):
        for z in range(nz):
            row = side * (64 * nz) + 64 * z
            for c, blk in ((0, near), (1, away)):
                tok[at(row, 64, 64), 256 * c : 256 * c + 128] = blk[z, 0:64]
                tok[at(row, 64, 64), 256 * c + 128 : 256 * c + 256] = blk[z, 64:128]
            one = near[z, 128:144].astype(F32)
            two = away[z, 128:144].astype(F32)
            for i in range(4):
                low = pltpu.roll(one, (LANES - 32 * i) % LANES, 1)
                high = pltpu.roll(two, (LANES + 32 - 32 * i) % LANES, 1)
                part = jnp.where(lane < 32, low, jnp.where(lane < 64, high, 0.0))
                edge[at(row + 16 * i, 16, 16), :] = part
    for z in range(nz):
        row = xhi * (64 * nz) + 64 * z + 32 * core
        res[32 * z : 32 * z + 32, :] = tok[at(row, 32, 32), :]

    scale = gain[...]
    for c in range(2):
        cols = slice(256 * c, 256 * (c + 1))
        normed[:, cols] = norm_rows(tok[:, cols].astype(F32), scale)
    normed[:, 512:640] = norm_rows(edge[...], scale)


def conv_kernel(normed, first, conv, stats, par, win, weight, small, sems):
    loads = [
        pltpu.make_async_copy(first.at[:, 96:112, 0:384], small, sems.at[1]),
        pltpu.make_async_copy(first.at[:, 0:64], weight, sems.at[0]),
    ]
    for copy in loads:
        copy.start()
    nz = small.shape[0]
    loads[0].wait()
    table = []
    lane = lax.broadcasted_iota(jnp.int32, (48, LANES), 1)
    for h in range(2):
        total = jnp.zeros((48, LANES), F32)
        for i in range(4):
            x = [small[4 * h + i, :, LANES * k : LANES * (k + 1)] for k in range(3)]
            x = jnp.concatenate(x, axis=0).astype(F32)
            x = x + (pltpu.roll(x, LANES - 32, 1) + pltpu.roll(x, LANES - 64, 1))
            x = jnp.where(lane < 32, x, 0.0)
            total = total + (x if i == 0 else pltpu.roll(x, 32 * i, 1))
        par[:, LANES * h : LANES * (h + 1)] = total[31:39]
        table.append(total)
    loads[1].wait()
    glu = weight[...].reshape(64 * nz, weight.shape[2])
    for c in range(3):
        x = normed[:, 512:640] if c == 2 else normed[:, 256 * c : 256 * (c + 1)]
        paired = jnp.dot(glu, x, preferred_element_type=F32)
        cols = x.shape[1]
        paired = paired.reshape(nz, 2, 32, cols)
        gated = (paired[:, 0] * jax.nn.sigmoid(paired[:, 1])).astype(BF).astype(F32)
        gated = gated.reshape(32 * nz, cols).T
        if c < 2:
            win[c, 16:272, :] = gated
        else:
            for r in range(2):
                win[r, 1:16, :] = gated[32 * r : 32 * r + 15]
                win[r, 272:287, :] = gated[32 * r + 15 : 32 * r + 30]

    step = 64
    for h in range(2):
        cols = slice(LANES * h, LANES * (h + 1))
        total = jnp.zeros((1, LANES), F32)
        for r in range(2):
            for k in range(256 // step):
                acc = jnp.zeros((step, LANES), F32)
                for j in range(31):
                    first = step * k + 1 + j
                    acc = acc + table[h][j : j + 1] * win[r, first : first + step, cols]
                conv[256 * r + step * k : 256 * r + step * (k + 1), cols] = acc
                total = total + jnp.sum(acc, axis=0, keepdims=True)
        mean = total * (1.0 / 512)
        apart = conv[:, cols] - mean
        square = jnp.sum(apart * apart, axis=0, keepdims=True)
        n = stats.shape[0]
        stats[:, h : h + 1, :] = jnp.broadcast_to(mean[None], (n, 1, LANES))
        stats[:, 2 + h : 3 + h, :] = jnp.broadcast_to(square[None], (n, 1, LANES))


def merged(stats, count):
    total = jnp.sum(stats, axis=0)
    mean = total * (1.0 / stats.shape[0])
    apart = stats - mean[None]
    apart = jnp.sum(apart * apart, axis=0)
    return mean[0:2], total[2:4] + count * apart[0:2]


def merge_kernel(stats, out):
    mean, square = merged(stats[...], 512)
    out[:, 0:2] = jnp.broadcast_to(mean[None], (out.shape[0],) + mean.shape)
    out[:, 2:4] = jnp.broadcast_to(square[None], (out.shape[0],) + square.shape)


def bn_kernel(conv, stats, par, out):
    frames = 8 * conv.shape[0]
    mean, square = merged(stats[...], frames)
    scale = lax.rsqrt(square * (1.0 / (frames * stats.shape[0])) + EPS)
    for h in range(2):
        cols = slice(LANES * h, LANES * (h + 1))
        value = (conv[:, cols] - mean[h : h + 1]) * (scale[h : h + 1] * par[0:1, cols])
        value = value + par[1:2, cols]
        out[cols, :] = (value * jax.nn.sigmoid(value)).T.astype(BF)


def place_blocks(own, across, beside, far, whole):
    core, xhi = place()
    nz, half = 8, 256
    for blk, c, x in ((own, core, xhi), (across, core, 1 - xhi)):
        for z in range(nz):
            row = x * 512 + 64 * z + 32 * c
            whole[at(row, 32, 32), :] = blk[32 * z : 32 * z + 32, :]
    for blk, c, x in ((beside, 1 - core, xhi), (far, 1 - core, 1 - xhi)):
        for z in range(nz):
            row = x * 512 + 64 * z + 32 * c
            whole[at(row, 32, 32), :half] = blk[32 * z : 32 * z + 32, half:]
            whole[at(row, 32, 32), half:] = blk[32 * z : 32 * z + 32, :half]


def mix_kernel(own, across, beside, far, blocks, res, out, whole):
    place_blocks(own, across, beside, far, whole)
    weight = blocks[...].reshape(256, blocks.shape[2])
    mixed = jnp.dot(weight, whole[...], preferred_element_type=F32)
    out[...] = (res[...].astype(F32) + mixed).astype(BF)


def norm_kernel(own, across, beside, far, gain, near, normed, whole):
    place_blocks(own, across, beside, far, whole)
    half = normed.shape[1] // 2
    near[...] = whole[:, :half]
    for c in range(2):
        cols = slice(half * c, half * (c + 1))
        normed[:, cols] = norm_rows(whole[:, cols].astype(F32), gain[...])


def ff_kernel(near, normed, blocks, keep, give, hidden, w, sems):
    loads = [
        pltpu.make_async_copy(
            blocks.at[2 * i : 2 * i + 2, 0:8], w.at[2 * i : 2 * i + 2, 0:8], sems.at[i]
        )
        for i in range(4)
    ]
    loads.append(pltpu.make_async_copy(blocks.at[:, 8:16], w.at[:, 8:16], sems.at[4]))
    for copy in loads:
        copy.start()
    xhi = place()[1]
    half = normed.shape[1] // 2
    for z in range(0, 8, 2):
        loads[z // 2].wait()
        rows = [jnp.concatenate([w[z + i, k] for k in range(8)], axis=1) for i in range(2)]
        value = jnp.dot(
            jnp.concatenate(rows, axis=0), normed[...], preferred_element_type=F32
        )
        hidden[LANES * z : LANES * (z + 2), :] = (value * jax.nn.sigmoid(value)).astype(BF)
    loads[4].wait()
    for k in range(0, 8, 2):
        rows = [jnp.concatenate([w[z, 8 + k + i] for z in range(8)], axis=1) for i in range(2)]
        value = jnp.dot(
            jnp.concatenate(rows, axis=0), hidden[...], preferred_element_type=F32
        )
        rows = slice(LANES * k, LANES * (k + 2))
        mine = jnp.where(xhi == k // 4, 1.0, 0.0)
        keep[rows, :] = 0.5 * value[:, :half] + mine * near[rows, :].astype(F32)
        give[rows, :] = (0.5 * value[:, half:]).astype(BF)


def sum_kernel(parts, out):
    nz, run = parts.shape[0] // 2, parts.shape[2]
    for z in range(nz):
        value = parts[z].astype(F32) + parts[nz + z].astype(F32)
        out[:, run * z : run * (z + 1)] = value.astype(BF)


def body(
    tokens,
    ln_conv_gain,
    glu_weight,
    depth_weight,
    bn_gain,
    bn_shift,
    conv_out_weight,
    ln_ff_gain,
    ff_in_weight,
    ff_out_weight,
):
    nz = lax.axis_size(Z)
    frames, width = tokens.shape
    full = ln_conv_gain.shape[0]
    run = frames // nz

    first, tok, head, tail = pl.pallas_call(
        weight_kernel,
        out_shape=(
            shape((112, full), BF),
            shape((width, frames), BF),
            shape((width, LANES), BF),
            shape((width, LANES), BF),
        ),
        in_specs=[HBM] * 6,
        out_specs=(HBM, VMEM, VMEM, VMEM),
        scratch_shapes=[
            pltpu.VMEM((48, LANES), F32),
            pltpu.VMEM((112, full), BF),
            pltpu.VMEM((48, width), F32),
            pltpu.SemaphoreType.DMA((10,)),
        ],
        compiler_params=PARAMS,
        name="weights",
    )(
        *in_hbm(
            glu_weight.transpose(1, 2, 0),
            conv_out_weight.T,
            depth_weight,
            bn_gain[None],
            bn_shift[None],
            tokens.T,
        )
    )
    first = lax.all_gather(first, Z)

    tm = lax.axis_size((XLO, Y, CORE))
    up = [(i, i + 1) for i in range(tm - 1)]
    left = lax.ppermute(tail, (XLO, Y, CORE), up)
    right = lax.ppermute(head, (XLO, Y, CORE), [(j, i) for i, j in up])
    parts = pl.pallas_call(
        pack_kernel,
        out_shape=shape((nz, 144, LANES), BF),
        in_specs=[VMEM] * 3,
        out_specs=VMEM,
        compiler_params=PARAMS,
        name="pack",
    )(tok, left, right)
    parts = lax.all_to_all(parts, Z, 0, 0, tiled=True)

    blocks = pl.pallas_call(
        block_kernel,
        out_shape=shape((16, LANES, LANES), BF),
        in_specs=[VMEM] * 2,
        out_specs=VMEM,
        compiler_params=PARAMS,
        name="blocks",
    )(ff_in_weight, ff_out_weight)
    blocks, parts = lax.optimization_barrier((blocks, parts))
    blocks = lax.all_gather(blocks, Z)

    whole = group_gather(parts)
    normed, res = pl.pallas_call(
        gather_kernel,
        out_shape=(shape((full, 2 * run + LANES), BF), shape((256, 2 * run), BF)),
        in_specs=[VMEM] * 5,
        out_specs=(VMEM,) * 2,
        scratch_shapes=[pltpu.VMEM((full, 2 * run), BF), pltpu.VMEM((full, LANES), F32)],
        compiler_params=PARAMS,
        name="gather",
    )(*whole, ln_conv_gain[:, None])
    conv, stats, par = pl.pallas_call(
        conv_kernel,
        out_shape=(
            shape((2 * run, 256), F32),
            shape((nz, 4, LANES), F32),
            shape((8, 256), F32),
        ),
        in_specs=[VMEM, HBM],
        out_specs=(VMEM,) * 3,
        scratch_shapes=[
            pltpu.VMEM((2, run + 40, 256), F32),
            pltpu.VMEM((nz, 64, full), BF),
            pltpu.VMEM((nz, 16, 3 * LANES), BF),
            pltpu.SemaphoreType.DMA((2,)),
        ],
        compiler_params=PARAMS,
        name="conv",
    )(normed, *in_hbm(first))
    stats = lax.all_to_all(stats, Z, 0, 0, tiled=True)
    stats = pl.pallas_call(
        merge_kernel,
        out_shape=shape((lax.axis_size((XLO, Y)), 4, LANES), F32),
        in_specs=[VMEM],
        out_specs=VMEM,
        compiler_params=PARAMS,
        name="merge",
    )(stats)
    stats = lax.all_to_all(stats, (XLO, Y), 0, 0, tiled=True)
    activated = pl.pallas_call(
        bn_kernel,
        out_shape=shape((256, 2 * run), BF),
        in_specs=[VMEM] * 3,
        out_specs=VMEM,
        compiler_params=PARAMS,
        name="bn",
    )(conv, stats, par)
    block = pl.pallas_call(
        mix_kernel,
        out_shape=shape((256, 2 * run), BF),
        grid=(1,),
        in_specs=[VMEM] * 4
        + [
            pl.BlockSpec((nz, 32, full), lambda i: (0, 2, 0)),
            VMEM,
        ],
        out_specs=VMEM,
        scratch_shapes=[pltpu.VMEM((full, 2 * run), BF)],
        compiler_params=PARAMS,
        name="mix",
    )(*group_gather(activated), first, res)
    near, normed = pl.pallas_call(
        norm_kernel,
        out_shape=(shape((full, run), BF), shape((full, 2 * run), BF)),
        in_specs=[VMEM] * 5,
        out_specs=(VMEM,) * 2,
        scratch_shapes=[pltpu.VMEM((full, 2 * run), BF)],
        compiler_params=PARAMS,
        name="norm",
    )(*group_gather(block), ln_ff_gain[:, None])
    keep, give = pl.pallas_call(
        ff_kernel,
        out_shape=(shape((full, run), F32), shape((full, run), BF)),
        in_specs=[VMEM] * 2 + [HBM],
        out_specs=(VMEM,) * 2,
        scratch_shapes=[
            pltpu.VMEM((full, 2 * run), BF),
            pltpu.VMEM((nz, 16, LANES, LANES), BF),
            pltpu.SemaphoreType.DMA((5,)),
        ],
        compiler_params=PARAMS,
        name="ff",
    )(near, normed, *in_hbm(blocks))
    keep = (keep + swap(give, CORE).astype(F32)).astype(BF)
    keep = lax.all_to_all(keep.reshape(2 * nz, width, run), (XHI, Z), 0, 0, tiled=True)
    out = pl.pallas_call(
        sum_kernel,
        out_shape=shape((width, frames), BF),
        in_specs=[VMEM],
        out_specs=VMEM,
        compiler_params=PARAMS,
        name="sum",
    )(keep)
    return out.T


def solution(mesh):
    fine = Mesh(mesh.devices.reshape(2, 8, 2, 2, 8), (XLO, Y, CORE, XHI, Z))
    tm, mp = ((XLO, Y, CORE), (XHI, Z))
    in_specs = (
        P(tm, mp),
        P(),
        P(None, None, mp),
        P(None, mp),
        P(mp),
        P(mp),
        P(None, mp),
        P(),
        P(None, mp),
        P(mp, None),
    )
    return jax.shard_map(body, mesh=fine, in_specs=in_specs, out_specs=P(tm, mp), check_vma=False)
```

```python
import jax
import jax.numpy as jnp
from jax import lax
from jax.experimental import pallas as pl
from jax.experimental.pallas import tpu as pltpu
from jax.sharding import Mesh, PartitionSpec as P

XLO, Y, CORE, XHI, Z = ("xlo", "y", "core", "xhi", "z")
BF, F32 = (jnp.bfloat16, jnp.float32)
EPS = 1e-05
LANES = 128
SPAN = 15
VMEM = pl.BlockSpec(memory_space=pltpu.VMEM)
HBM = pl.BlockSpec(memory_space=pltpu.HBM)
PARAMS = pltpu.CompilerParams(vmem_limit_bytes=40 << 20)


def shape(dims, dtype):
    return jax.ShapeDtypeStruct(dims, dtype)


def in_hbm(*arrays):
    return [pltpu.with_memory_space_constraint(x, pltpu.HBM) for x in arrays]


def swap(x, axis):
    return lax.ppermute(x, axis, [(0, 1), (1, 0)])


def group_gather(x):
    across = swap(x, XHI)
    beside = swap(x, CORE)
    return x, across, beside, swap(across, CORE)


def norm_rows(x, gain):
    inv = 1.0 / x.shape[0]
    centred = x - jnp.sum(x, axis=0, keepdims=True) * inv
    spread = jnp.sum(centred * centred, axis=0, keepdims=True) * inv
    return (centred * lax.rsqrt(spread + EPS) * gain).astype(BF)


def place():
    return lax.axis_index(CORE), lax.axis_index(XHI)


def at(start, size, step):
    return pl.ds(pl.multiple_of(start, step), size)


def weight_kernel(
    glu, conv_out, depth, gain, shift, tok,
    out, near, first, last,
    table, parts, small, sems,
):
    core, _ = place()
    half = at(32 * core, 32, 32)
    taps, width = depth.shape
    frames = tok.shape[1]
    pairs = [
        (depth, small.at[0:taps]),
        (gain, small.at[32:33]),
        (shift, small.at[40:41]),
        (glu.at[0, half], parts.at[0:32]),
        (glu.at[1, half], parts.at[32:64]),
        (conv_out.at[half], parts.at[64:96]),
        (tok.at[:, 0:LANES], first),
        (tok.at[:, frames - LANES : frames], last),
        (tok, near),
    ]
    loads = [pltpu.make_async_copy(a, b, sems.at[i]) for i, (a, b) in enumerate(pairs)]
    for copy in loads:
        copy.start()
    table[...] = jnp.zeros_like(table)
    for copy in loads[:3]:
        copy.wait()
    table[0:taps, 0:width] = small[0:taps]
    table[taps : taps + 1, 0:width] = small[32:33]
    table[taps + 1 : taps + 2, 0:width] = small[40:41]
    lane = lax.broadcasted_iota(jnp.int32, table.shape, 1)
    rest = jnp.where(core == 0, table[...], pltpu.roll(table[...], LANES - 32, 1))
    rest = jnp.where(lane < 32, rest, 0.0)
    packed = jnp.zeros_like(rest)
    for i in range(3):
        piece = rest.astype(BF).astype(F32)
        packed = packed + (piece if i == 0 else pltpu.roll(piece, 32 * i, 1))
        rest = rest - piece
    parts[96:112] = jnp.zeros((16, parts.shape[1]), BF)
    for i in range(3):
        parts[96:112, LANES * i : LANES * (i + 1)] = packed[16 * i : 16 * i + 16].astype(BF)
    for copy in loads[3:6]:
        copy.wait()
    final = pltpu.make_async_copy(parts, out, sems.at[9])
    final.start()
    for copy in loads[6:] + [final]:
        copy.wait()


def block_kernel(ff_in, ff_out, out):
    half = at(place()[0] * LANES, LANES, LANES)
    for k in range(8):
        tile = slice(LANES * k, LANES * (k + 1))
        out[k] = ff_in[tile, half].astype(F32).T.astype(BF)
        out[8 + k] = ff_out[half, tile].astype(F32).T.astype(BF)


def pack_kernel(tok, left, right, out):
    lane = lax.broadcasted_iota(jnp.int32, (16, LANES), 1)
    nz = out.shape[0]
    for z in range(nz):
        out[z, 0:64] = tok[:, 2 * z * LANES : (2 * z + 1) * LANES]
        out[z, 64:128] = tok[:, (2 * z + 1) * LANES : (2 * z + 2) * LANES]
        packed = jnp.zeros((16, LANES), F32)
        for i in range(4):
            rows = slice(16 * i, 16 * i + 16)
            if z == 0:
                before = left[rows]
            else:
                before = tok[rows, (2 * z - 1) * LANES : 2 * z * LANES]
            if z == nz - 1:
                after = right[rows]
            else:
                after = tok[rows, (2 * z + 2) * LANES : (2 * z + 3) * LANES]
            low = pltpu.roll(before.astype(F32), (32 * i + SPAN) % LANES, 1)
            high = pltpu.roll(after.astype(F32), 32 * i + SPAN, 1)
            packed = jnp.where((lane >= 32 * i) & (lane < 32 * i + SPAN), low, packed)
            packed = jnp.where(
                (lane >= 32 * i + SPAN) & (lane < 32 * i + 2 * SPAN), high, packed
            )
        out[z, 128:144] = packed.astype(BF)


def gather_kernel(own, across, beside, far, gain, normed, res, tok, edge):
    core, xhi = place()
    lane = lax.broadcasted_iota(jnp.int32, (16, LANES), 1)
    nz = own.shape[0]
    for near, away, side in ((own, beside, xhi), (across, far, 1 - xhi)):
        for z in range(nz):
            row = side * (64 * nz) + 64 * z
            for c, blk in ((0, near), (1, away)):
                tok[at(row, 64, 64), 256 * c : 256 * c + 128] = blk[z, 0:64]
                tok[at(row, 64, 64), 256 * c + 128 : 256 * c + 256] = blk[z, 64:128]
            one = near[z, 128:144].astype(F32)
            two = away[z, 128:144].astype(F32)
            for i in range(4):
                low = pltpu.roll(one, (LANES - 32 * i) % LANES, 1)
                high = pltpu.roll(two, (LANES + 32 - 32 * i) % LANES, 1)
                part = jnp.where(lane < 32, low, jnp.where(lane < 64, high, 0.0))
                edge[at(row + 16 * i, 16, 16), :] = part
    for z in range(nz):
        row = xhi * (64 * nz) + 64 * z + 32 * core
        res[32 * z : 32 * z + 32, :] = tok[at(row, 32, 32), :]

    scale = gain[...]
    for c in range(2):
        cols = slice(256 * c, 256 * (c + 1))
        normed[:, cols] = norm_rows(tok[:, cols].astype(F32), scale)
    normed[:, 512:640] = norm_rows(edge[...], scale)


def conv_kernel(normed, first, conv, stats, par, win, weight, small, sems):
    loads = [
        pltpu.make_async_copy(first.at[:, 96:112, 0:384], small, sems.at[1]),
        pltpu.make_async_copy(first.at[:, 0:64], weight, sems.at[0]),
    ]
    for copy in loads:
        copy.start()
    nz = small.shape[0]
    loads[0].wait()
    table = []
    lane = lax.broadcasted_iota(jnp.int32, (48, LANES), 1)
    for h in range(2):
        total = jnp.zeros((48, LANES), F32)
        for i in range(4):
            x = [small[4 * h + i, :, LANES * k : LANES * (k + 1)] for k in range(3)]
            x = jnp.concatenate(x, axis=0).astype(F32)
            x = x + (pltpu.roll(x, LANES - 32, 1) + pltpu.roll(x, LANES - 64, 1))
            x = jnp.where(lane < 32, x, 0.0)
            total = total + (x if i == 0 else pltpu.roll(x, 32 * i, 1))
        par[:, LANES * h : LANES * (h + 1)] = total[31:39]
        table.append(total)
    loads[1].wait()
    glu = weight[...].reshape(64 * nz, weight.shape[2])
    for c in range(3):
        x = normed[:, 512:640] if c == 2 else normed[:, 256 * c : 256 * (c + 1)]
        paired = jnp.dot(glu, x, preferred_element_type=F32)
        cols = x.shape[1]
        paired = paired.reshape(nz, 2, 32, cols)
        gated = (paired[:, 0] * jax.nn.sigmoid(paired[:, 1])).astype(BF).astype(F32)
        gated = gated.reshape(32 * nz, cols).T
        if c < 2:
            win[c, 16:272, :] = gated
        else:
            for r in range(2):
                win[r, 1:16, :] = gated[32 * r : 32 * r + 15]
                win[r, 272:287, :] = gated[32 * r + 15 : 32 * r + 30]

    step = 64
    for h in range(2):
        cols = slice(LANES * h, LANES * (h + 1))
        total = jnp.zeros((1, LANES), F32)
        for r in range(2):
            for k in range(256 // step):
                acc = jnp.zeros((step, LANES), F32)
                for j in range(31):
                    first = step * k + 1 + j
                    acc = acc + table[h][j : j + 1] * win[r, first : first + step, cols]
                conv[256 * r + step * k : 256 * r + step * (k + 1), cols] = acc
                total = total + jnp.sum(acc, axis=0, keepdims=True)
        mean = total * (1.0 / 512)
        apart = conv[:, cols] - mean
        square = jnp.sum(apart * apart, axis=0, keepdims=True)
        n = stats.shape[0]
        stats[:, h : h + 1, :] = jnp.broadcast_to(mean[None], (n, 1, LANES))
        stats[:, 2 + h : 3 + h, :] = jnp.broadcast_to(square[None], (n, 1, LANES))


def merged(stats, count):
    total = jnp.sum(stats, axis=0)
    mean = total * (1.0 / stats.shape[0])
    apart = stats - mean[None]
    apart = jnp.sum(apart * apart, axis=0)
    return mean[0:2], total[2:4] + count * apart[0:2]


def merge_kernel(stats, out):
    mean, square = merged(stats[...], 512)
    out[:, 0:2] = jnp.broadcast_to(mean[None], (out.shape[0],) + mean.shape)
    out[:, 2:4] = jnp.broadcast_to(square[None], (out.shape[0],) + square.shape)


def bn_kernel(conv, stats, par, out):
    frames = 8 * conv.shape[0]
    mean, square = merged(stats[...], frames)
    scale = lax.rsqrt(square * (1.0 / (frames * stats.shape[0])) + EPS)
    for h in range(2):
        cols = slice(LANES * h, LANES * (h + 1))
        value = (conv[:, cols] - mean[h : h + 1]) * (scale[h : h + 1] * par[0:1, cols])
        value = value + par[1:2, cols]
        out[cols, :] = (value * jax.nn.sigmoid(value)).T.astype(BF)


def place_blocks(own, across, beside, far, whole):
    core, xhi = place()
    nz, half = 8, 256
    for blk, c, x in ((own, core, xhi), (across, core, 1 - xhi)):
        for z in range(nz):
            row = x * 512 + 64 * z + 32 * c
            whole[at(row, 32, 32), :] = blk[32 * z : 32 * z + 32, :]
    for blk, c, x in ((beside, 1 - core, xhi), (far, 1 - core, 1 - xhi)):
        for z in range(nz):
            row = x * 512 + 64 * z + 32 * c
            whole[at(row, 32, 32), :half] = blk[32 * z : 32 * z + 32, half:]
            whole[at(row, 32, 32), half:] = blk[32 * z : 32 * z + 32, :half]


def mix_kernel(own, across, beside, far, blocks, res, out, whole):
    place_blocks(own, across, beside, far, whole)
    weight = blocks[...].reshape(256, blocks.shape[2])
    mixed = jnp.dot(weight, whole[...], preferred_element_type=F32)
    out[...] = (res[...].astype(F32) + mixed).astype(BF)


def norm_kernel(own, across, beside, far, gain, near, here, there, whole):
    place_blocks(own, across, beside, far, whole)
    half = here.shape[1]
    near[...] = whole[:, :half]
    for c, normed in ((0, here), (1, there)):
        cols = slice(half * c, half * (c + 1))
        normed[...] = norm_rows(whole[:, cols].astype(F32), gain[...])


def feed_forward(normed, w, hidden, ready):
    for z in range(0, 8, 2):
        ready(z // 2)
        rows = [jnp.concatenate([w[z + i, k] for k in range(8)], axis=1) for i in range(2)]
        value = jnp.dot(
            jnp.concatenate(rows, axis=0), normed[...], preferred_element_type=F32
        )
        hidden[LANES * z : LANES * (z + 2), :] = (value * jax.nn.sigmoid(value)).astype(BF)
    ready(4)
    for k in range(0, 8, 2):
        rows = [jnp.concatenate([w[z, 8 + k + i] for z in range(8)], axis=1) for i in range(2)]
        value = jnp.dot(
            jnp.concatenate(rows, axis=0), hidden[...], preferred_element_type=F32
        )
        yield k, slice(LANES * k, LANES * (k + 2)), 0.5 * value


def give_kernel(normed, blocks, give, w, hidden, sems):
    loads = [
        pltpu.make_async_copy(
            blocks.at[2 * i : 2 * i + 2, 0:8], w.at[2 * i : 2 * i + 2, 0:8], sems.at[i]
        )
        for i in range(4)
    ]
    loads.append(pltpu.make_async_copy(blocks.at[:, 8:16], w.at[:, 8:16], sems.at[4]))
    for copy in loads:
        copy.start()
    for _, rows, value in feed_forward(normed, w, hidden, lambda i: loads[i].wait()):
        give[rows, :] = value.astype(BF)


def keep_kernel(near, normed, w, keep, hidden):
    xhi = place()[1]
    for k, rows, value in feed_forward(normed, w, hidden, lambda i: None):
        mine = jnp.where(xhi == k // 4, 1.0, 0.0)
        keep[rows, :] = value + mine * near[rows, :].astype(F32)


def sum_kernel(parts, out):
    nz, run = parts.shape[0] // 2, parts.shape[2]
    for z in range(nz):
        value = parts[z].astype(F32) + parts[nz + z].astype(F32)
        out[:, run * z : run * (z + 1)] = value.astype(BF)


def body(
    tokens,
    ln_conv_gain,
    glu_weight,
    depth_weight,
    bn_gain,
    bn_shift,
    conv_out_weight,
    ln_ff_gain,
    ff_in_weight,
    ff_out_weight,
):
    nz = lax.axis_size(Z)
    frames, width = tokens.shape
    full = ln_conv_gain.shape[0]
    run = frames // nz

    first, tok, head, tail = pl.pallas_call(
        weight_kernel,
        out_shape=(
            shape((112, full), BF),
            shape((width, frames), BF),
            shape((width, LANES), BF),
            shape((width, LANES), BF),
        ),
        in_specs=[HBM] * 6,
        out_specs=(HBM, VMEM, VMEM, VMEM),
        scratch_shapes=[
            pltpu.VMEM((48, LANES), F32),
            pltpu.VMEM((112, full), BF),
            pltpu.VMEM((48, width), F32),
            pltpu.SemaphoreType.DMA((10,)),
        ],
        compiler_params=PARAMS,
        name="weights",
    )(
        *in_hbm(
            glu_weight.transpose(1, 2, 0),
            conv_out_weight.T,
            depth_weight,
            bn_gain[None],
            bn_shift[None],
            tokens.T,
        )
    )
    first = lax.all_gather(first, Z)

    tm = lax.axis_size((XLO, Y, CORE))
    up = [(i, i + 1) for i in range(tm - 1)]
    left = lax.ppermute(tail, (XLO, Y, CORE), up)
    right = lax.ppermute(head, (XLO, Y, CORE), [(j, i) for i, j in up])
    parts = pl.pallas_call(
        pack_kernel,
        out_shape=shape((nz, 144, LANES), BF),
        in_specs=[VMEM] * 3,
        out_specs=VMEM,
        compiler_params=PARAMS,
        name="pack",
    )(tok, left, right)
    parts = lax.all_to_all(parts, Z, 0, 0, tiled=True)

    blocks = pl.pallas_call(
        block_kernel,
        out_shape=shape((16, LANES, LANES), BF),
        in_specs=[VMEM] * 2,
        out_specs=VMEM,
        compiler_params=PARAMS,
        name="blocks",
    )(ff_in_weight, ff_out_weight)
    blocks, parts = lax.optimization_barrier((blocks, parts))
    blocks = lax.all_gather(blocks, Z)

    whole = group_gather(parts)
    normed, res = pl.pallas_call(
        gather_kernel,
        out_shape=(shape((full, 2 * run + LANES), BF), shape((256, 2 * run), BF)),
        in_specs=[VMEM] * 5,
        out_specs=(VMEM,) * 2,
        scratch_shapes=[pltpu.VMEM((full, 2 * run), BF), pltpu.VMEM((full, LANES), F32)],
        compiler_params=PARAMS,
        name="gather",
    )(*whole, ln_conv_gain[:, None])
    conv, stats, par = pl.pallas_call(
        conv_kernel,
        out_shape=(
            shape((2 * run, 256), F32),
            shape((nz, 4, LANES), F32),
            shape((8, 256), F32),
        ),
        in_specs=[VMEM, HBM],
        out_specs=(VMEM,) * 3,
        scratch_shapes=[
            pltpu.VMEM((2, run + 40, 256), F32),
            pltpu.VMEM((nz, 64, full), BF),
            pltpu.VMEM((nz, 16, 3 * LANES), BF),
            pltpu.SemaphoreType.DMA((2,)),
        ],
        compiler_params=PARAMS,
        name="conv",
    )(normed, *in_hbm(first))
    stats = lax.all_to_all(stats, Z, 0, 0, tiled=True)
    stats = pl.pallas_call(
        merge_kernel,
        out_shape=shape((lax.axis_size((XLO, Y)), 4, LANES), F32),
        in_specs=[VMEM],
        out_specs=VMEM,
        compiler_params=PARAMS,
        name="merge",
    )(stats)
    stats = lax.all_to_all(stats, (XLO, Y), 0, 0, tiled=True)
    activated = pl.pallas_call(
        bn_kernel,
        out_shape=shape((256, 2 * run), BF),
        in_specs=[VMEM] * 3,
        out_specs=VMEM,
        compiler_params=PARAMS,
        name="bn",
    )(conv, stats, par)
    block = pl.pallas_call(
        mix_kernel,
        out_shape=shape((256, 2 * run), BF),
        grid=(1,),
        in_specs=[VMEM] * 4
        + [
            pl.BlockSpec((nz, 32, full), lambda i: (0, 2, 0)),
            VMEM,
        ],
        out_specs=VMEM,
        scratch_shapes=[pltpu.VMEM((full, 2 * run), BF)],
        compiler_params=PARAMS,
        name="mix",
    )(*group_gather(activated), first, res)
    near, here, there = pl.pallas_call(
        norm_kernel,
        out_shape=(shape((full, run), BF),) * 3,
        in_specs=[VMEM] * 5,
        out_specs=(VMEM,) * 3,
        scratch_shapes=[pltpu.VMEM((full, 2 * run), BF)],
        compiler_params=PARAMS,
        name="norm",
    )(*group_gather(block), ln_ff_gain[:, None])
    give, blocks = pl.pallas_call(
        give_kernel,
        out_shape=(shape((full, run), BF), shape((nz, 16, LANES, LANES), BF)),
        in_specs=[VMEM, HBM],
        out_specs=(VMEM,) * 2,
        scratch_shapes=[pltpu.VMEM((full, run), BF), pltpu.SemaphoreType.DMA((5,))],
        compiler_params=PARAMS,
        name="give",
    )(there, *in_hbm(blocks))
    keep = pl.pallas_call(
        keep_kernel,
        out_shape=shape((full, run), F32),
        in_specs=[VMEM] * 3,
        out_specs=VMEM,
        scratch_shapes=[pltpu.VMEM((full, run), BF)],
        compiler_params=PARAMS,
        cost_estimate=pl.CostEstimate(
            flops=4 * full * full * run, bytes_accessed=6 << 20, transcendentals=full * run
        ),
        name="keep",
    )(near, here, blocks)
    keep = (keep + swap(give, CORE).astype(F32)).astype(BF)
    keep = lax.all_to_all(keep.reshape(2 * nz, width, run), (XHI, Z), 0, 0, tiled=True)
    out = pl.pallas_call(
        sum_kernel,
        out_shape=shape((width, frames), BF),
        in_specs=[VMEM],
        out_specs=VMEM,
        compiler_params=PARAMS,
        name="sum",
    )(keep)
    return out.T


def solution(mesh):
    fine = Mesh(mesh.devices.reshape(2, 8, 2, 2, 8), (XLO, Y, CORE, XHI, Z))
    tm, mp = ((XLO, Y, CORE), (XHI, Z))
    in_specs = (
        P(tm, mp),
        P(),
        P(None, None, mp),
        P(None, mp),
        P(mp),
        P(mp),
        P(None, mp),
        P(),
        P(None, mp),
        P(mp, None),
    )
    return jax.shard_map(body, mesh=fine, in_specs=in_specs, out_specs=P(tm, mp), check_vma=False)
```

```python
import jax
import jax.numpy as jnp
from jax import lax
from jax.experimental import pallas as pl
from jax.experimental.pallas import tpu as pltpu
from jax.sharding import Mesh, PartitionSpec as P

XLO, Y, CORE, XHI, Z = ("xlo", "y", "core", "xhi", "z")
BF, F32 = (jnp.bfloat16, jnp.float32)
EPS = 1e-05
LANES = 128
SPAN = 15
VMEM = pl.BlockSpec(memory_space=pltpu.VMEM)
HBM = pl.BlockSpec(memory_space=pltpu.HBM)
PARAMS = pltpu.CompilerParams(vmem_limit_bytes=40 << 20)


def shape(dims, dtype):
    return jax.ShapeDtypeStruct(dims, dtype)


def in_hbm(*arrays):
    return [pltpu.with_memory_space_constraint(x, pltpu.HBM) for x in arrays]


def swap(x, axis):
    return lax.ppermute(x, axis, [(0, 1), (1, 0)])


def group_gather(x):
    across = swap(x, XHI)
    beside = swap(x, CORE)
    return x, across, beside, swap(across, CORE)


def norm_rows(x, gain):
    inv = 1.0 / x.shape[0]
    centred = x - jnp.sum(x, axis=0, keepdims=True) * inv
    spread = jnp.sum(centred * centred, axis=0, keepdims=True) * inv
    return (centred * lax.rsqrt(spread + EPS) * gain).astype(BF)


def place():
    return lax.axis_index(CORE), lax.axis_index(XHI)


def at(start, size, step):
    return pl.ds(pl.multiple_of(start, step), size)


def weight_kernel(
    glu, conv_out, depth, gain, shift, tok,
    out, near, first, last,
    table, parts, small, sems,
):
    core, _ = place()
    half = at(32 * core, 32, 32)
    taps, width = depth.shape
    frames = tok.shape[1]
    pairs = [
        (depth, small.at[0:taps]),
        (gain, small.at[32:33]),
        (shift, small.at[40:41]),
        (glu.at[0, half], parts.at[0:32]),
        (glu.at[1, half], parts.at[32:64]),
        (conv_out.at[half], parts.at[64:96]),
        (tok.at[:, 0:LANES], first),
        (tok.at[:, frames - LANES : frames], last),
        (tok, near),
    ]
    loads = [pltpu.make_async_copy(a, b, sems.at[i]) for i, (a, b) in enumerate(pairs)]
    for copy in loads:
        copy.start()
    table[...] = jnp.zeros_like(table)
    for copy in loads[:3]:
        copy.wait()
    table[0:taps, 0:width] = small[0:taps]
    table[taps : taps + 1, 0:width] = small[32:33]
    table[taps + 1 : taps + 2, 0:width] = small[40:41]
    lane = lax.broadcasted_iota(jnp.int32, table.shape, 1)
    rest = jnp.where(core == 0, table[...], pltpu.roll(table[...], LANES - 32, 1))
    rest = jnp.where(lane < 32, rest, 0.0)
    packed = jnp.zeros_like(rest)
    for i in range(3):
        piece = rest.astype(BF).astype(F32)
        packed = packed + (piece if i == 0 else pltpu.roll(piece, 32 * i, 1))
        rest = rest - piece
    parts[96:112] = jnp.zeros((16, parts.shape[1]), BF)
    for i in range(3):
        parts[96:112, LANES * i : LANES * (i + 1)] = packed[16 * i : 16 * i + 16].astype(BF)
    for copy in loads[3:6]:
        copy.wait()
    final = pltpu.make_async_copy(parts, out, sems.at[9])
    final.start()
    for copy in loads[6:] + [final]:
        copy.wait()


def block_kernel(ff_in, ff_out, out):
    half = at(place()[0] * LANES, LANES, LANES)
    for k in range(8):
        tile = slice(LANES * k, LANES * (k + 1))
        out[k] = ff_in[tile, half].astype(F32).T.astype(BF)
        out[8 + k] = ff_out[half, tile].astype(F32).T.astype(BF)


def pack_kernel(tok, left, right, out):
    lane = lax.broadcasted_iota(jnp.int32, (16, LANES), 1)
    nz = out.shape[0]
    for z in range(nz):
        out[z, 0:64] = tok[:, 2 * z * LANES : (2 * z + 1) * LANES]
        out[z, 64:128] = tok[:, (2 * z + 1) * LANES : (2 * z + 2) * LANES]
        packed = jnp.zeros((16, LANES), F32)
        for i in range(4):
            rows = slice(16 * i, 16 * i + 16)
            if z == 0:
                before = left[rows]
            else:
                before = tok[rows, (2 * z - 1) * LANES : 2 * z * LANES]
            if z == nz - 1:
                after = right[rows]
            else:
                after = tok[rows, (2 * z + 2) * LANES : (2 * z + 3) * LANES]
            low = pltpu.roll(before.astype(F32), (32 * i + SPAN) % LANES, 1)
            high = pltpu.roll(after.astype(F32), 32 * i + SPAN, 1)
            packed = jnp.where((lane >= 32 * i) & (lane < 32 * i + SPAN), low, packed)
            packed = jnp.where(
                (lane >= 32 * i + SPAN) & (lane < 32 * i + 2 * SPAN), high, packed
            )
        out[z, 128:144] = packed.astype(BF)


def gather_kernel(own, across, beside, far, gain, normed, res, tok, edge):
    core, xhi = place()
    lane = lax.broadcasted_iota(jnp.int32, (16, LANES), 1)
    nz = own.shape[0]
    for near, away, side in ((own, beside, xhi), (across, far, 1 - xhi)):
        for z in range(nz):
            row = side * (64 * nz) + 64 * z
            for c, blk in ((0, near), (1, away)):
                tok[at(row, 64, 64), 256 * c : 256 * c + 128] = blk[z, 0:64]
                tok[at(row, 64, 64), 256 * c + 128 : 256 * c + 256] = blk[z, 64:128]
            one = near[z, 128:144].astype(F32)
            two = away[z, 128:144].astype(F32)
            for i in range(4):
                low = pltpu.roll(one, (LANES - 32 * i) % LANES, 1)
                high = pltpu.roll(two, (LANES + 32 - 32 * i) % LANES, 1)
                part = jnp.where(lane < 32, low, jnp.where(lane < 64, high, 0.0))
                edge[at(row + 16 * i, 16, 16), :] = part
    for z in range(nz):
        row = xhi * (64 * nz) + 64 * z + 32 * core
        res[32 * z : 32 * z + 32, :] = tok[at(row, 32, 32), :]

    scale = gain[...]
    for c in range(2):
        cols = slice(256 * c, 256 * (c + 1))
        normed[:, cols] = norm_rows(tok[:, cols].astype(F32), scale)
    normed[:, 512:640] = norm_rows(edge[...], scale)


def conv_kernel(normed, first, conv, stats, par, win, weight, small, sems):
    loads = [pltpu.make_async_copy(first.at[:, 96:112, 0:384], small, sems.at[8])]
    loads += [
        pltpu.make_async_copy(first.at[z, 0:64], weight.at[z], sems.at[z]) for z in range(8)
    ]
    for copy in loads:
        copy.start()
    nz = small.shape[0]
    loads[0].wait()
    table = []
    lane = lax.broadcasted_iota(jnp.int32, (48, LANES), 1)
    for h in range(2):
        total = jnp.zeros((48, LANES), F32)
        for i in range(4):
            x = [small[4 * h + i, :, LANES * k : LANES * (k + 1)] for k in range(3)]
            x = jnp.concatenate(x, axis=0).astype(F32)
            x = x + (pltpu.roll(x, LANES - 32, 1) + pltpu.roll(x, LANES - 64, 1))
            x = jnp.where(lane < 32, x, 0.0)
            total = total + (x if i == 0 else pltpu.roll(x, 32 * i, 1))
        par[:, LANES * h : LANES * (h + 1)] = total[31:39]
        table.append(total)
    for copy in loads[1:]:
        copy.wait()
    glu = weight[...].reshape(64 * nz, weight.shape[2])
    for c in range(3):
        x = normed[:, 512:640] if c == 2 else normed[:, 256 * c : 256 * (c + 1)]
        paired = jnp.dot(glu, x, preferred_element_type=F32)
        cols = x.shape[1]
        paired = paired.reshape(nz, 2, 32, cols)
        gated = (paired[:, 0] * jax.nn.sigmoid(paired[:, 1])).astype(BF).astype(F32)
        gated = gated.reshape(32 * nz, cols).T
        if c < 2:
            win[c, 16:272, :] = gated
        else:
            for r in range(2):
                win[r, 1:16, :] = gated[32 * r : 32 * r + 15]
                win[r, 272:287, :] = gated[32 * r + 15 : 32 * r + 30]

    step = 64
    for h in range(2):
        cols = slice(LANES * h, LANES * (h + 1))
        total = jnp.zeros((1, LANES), F32)
        for r in range(2):
            for k in range(256 // step):
                acc = jnp.zeros((step, LANES), F32)
                for j in range(31):
                    first = step * k + 1 + j
                    acc = acc + table[h][j : j + 1] * win[r, first : first + step, cols]
                conv[256 * r + step * k : 256 * r + step * (k + 1), cols] = acc
                total = total + jnp.sum(acc, axis=0, keepdims=True)
        mean = total * (1.0 / 512)
        apart = conv[:, cols] - mean
        square = jnp.sum(apart * apart, axis=0, keepdims=True)
        n = stats.shape[0]
        stats[:, h : h + 1, :] = jnp.broadcast_to(mean[None], (n, 1, LANES))
        stats[:, 2 + h : 3 + h, :] = jnp.broadcast_to(square[None], (n, 1, LANES))


def merged(stats, count):
    total = jnp.sum(stats, axis=0)
    mean = total * (1.0 / stats.shape[0])
    apart = stats - mean[None]
    apart = jnp.sum(apart * apart, axis=0)
    return mean[0:2], total[2:4] + count * apart[0:2]


def merge_kernel(stats, out):
    mean, square = merged(stats[...], 512)
    out[:, 0:2] = jnp.broadcast_to(mean[None], (out.shape[0],) + mean.shape)
    out[:, 2:4] = jnp.broadcast_to(square[None], (out.shape[0],) + square.shape)


def bn_kernel(conv, stats, par, out):
    frames = 8 * conv.shape[0]
    mean, square = merged(stats[...], frames)
    scale = lax.rsqrt(square * (1.0 / (frames * stats.shape[0])) + EPS)
    for h in range(2):
        cols = slice(LANES * h, LANES * (h + 1))
        value = (conv[:, cols] - mean[h : h + 1]) * (scale[h : h + 1] * par[0:1, cols])
        value = value + par[1:2, cols]
        out[cols, :] = (value * jax.nn.sigmoid(value)).T.astype(BF)


def place_blocks(own, across, beside, far, whole):
    core, xhi = place()
    nz, half = 8, 256
    for blk, c, x in ((own, core, xhi), (across, core, 1 - xhi)):
        for z in range(nz):
            row = x * 512 + 64 * z + 32 * c
            whole[at(row, 32, 32), :] = blk[32 * z : 32 * z + 32, :]
    for blk, c, x in ((beside, 1 - core, xhi), (far, 1 - core, 1 - xhi)):
        for z in range(nz):
            row = x * 512 + 64 * z + 32 * c
            whole[at(row, 32, 32), :half] = blk[32 * z : 32 * z + 32, half:]
            whole[at(row, 32, 32), half:] = blk[32 * z : 32 * z + 32, :half]


def mix_kernel(own, across, beside, far, blocks, res, out, whole):
    place_blocks(own, across, beside, far, whole)
    weight = blocks[...].reshape(256, blocks.shape[2])
    mixed = jnp.dot(weight, whole[...], preferred_element_type=F32)
    out[...] = (res[...].astype(F32) + mixed).astype(BF)


def norm_kernel(own, across, beside, far, gain, near, here, there, whole):
    place_blocks(own, across, beside, far, whole)
    half = here.shape[1]
    near[...] = whole[:, :half]
    for c, normed in ((0, here), (1, there)):
        cols = slice(half * c, half * (c + 1))
        normed[...] = norm_rows(whole[:, cols].astype(F32), gain[...])


def feed_forward(normed, w, hidden, ready):
    for z in range(0, 8, 2):
        ready(z // 2)
        rows = [jnp.concatenate([w[z + i, k] for k in range(8)], axis=1) for i in range(2)]
        value = jnp.dot(
            jnp.concatenate(rows, axis=0), normed[...], preferred_element_type=F32
        )
        hidden[LANES * z : LANES * (z + 2), :] = (value * jax.nn.sigmoid(value)).astype(BF)
    ready(4)
    for k in range(0, 8, 2):
        rows = [jnp.concatenate([w[z, 8 + k + i] for z in range(8)], axis=1) for i in range(2)]
        value = jnp.dot(
            jnp.concatenate(rows, axis=0), hidden[...], preferred_element_type=F32
        )
        yield k, slice(LANES * k, LANES * (k + 2)), 0.5 * value


def give_kernel(normed, blocks, give, w, hidden, sems):
    loads = [
        pltpu.make_async_copy(
            blocks.at[z, 8 * i : 8 * i + 8], w.at[z, 8 * i : 8 * i + 8], sems.at[8 * i + z]
        )
        for i in range(2)
        for z in range(8)
    ]
    for copy in loads:
        copy.start()

    def ready(step):
        for copy in loads[8:] if step == 4 else loads[2 * step : 2 * step + 2]:
            copy.wait()

    for _, rows, value in feed_forward(normed, w, hidden, ready):
        give[rows, :] = value.astype(BF)


def keep_kernel(near, normed, w, keep, hidden):
    xhi = place()[1]
    for k, rows, value in feed_forward(normed, w, hidden, lambda i: None):
        mine = jnp.where(xhi == k // 4, 1.0, 0.0)
        keep[rows, :] = value + mine * near[rows, :].astype(F32)


def sum_kernel(parts, out):
    nz, run = parts.shape[0] // 2, parts.shape[2]
    for z in range(nz):
        value = parts[z].astype(F32) + parts[nz + z].astype(F32)
        out[:, run * z : run * (z + 1)] = value.astype(BF)


def body(
    tokens,
    ln_conv_gain,
    glu_weight,
    depth_weight,
    bn_gain,
    bn_shift,
    conv_out_weight,
    ln_ff_gain,
    ff_in_weight,
    ff_out_weight,
):
    nz = lax.axis_size(Z)
    frames, width = tokens.shape
    full = ln_conv_gain.shape[0]
    run = frames // nz

    first, tok, head, tail = pl.pallas_call(
        weight_kernel,
        out_shape=(
            shape((112, full), BF),
            shape((width, frames), BF),
            shape((width, LANES), BF),
            shape((width, LANES), BF),
        ),
        in_specs=[HBM] * 6,
        out_specs=(HBM, VMEM, VMEM, VMEM),
        scratch_shapes=[
            pltpu.VMEM((48, LANES), F32),
            pltpu.VMEM((112, full), BF),
            pltpu.VMEM((48, width), F32),
            pltpu.SemaphoreType.DMA((10,)),
        ],
        compiler_params=PARAMS,
        name="weights",
    )(
        *in_hbm(
            glu_weight.transpose(1, 2, 0),
            conv_out_weight.T,
            depth_weight,
            bn_gain[None],
            bn_shift[None],
            tokens.T,
        )
    )
    first = lax.all_gather(first, Z)

    tm = lax.axis_size((XLO, Y, CORE))
    up = [(i, i + 1) for i in range(tm - 1)]
    left = lax.ppermute(tail, (XLO, Y, CORE), up)
    right = lax.ppermute(head, (XLO, Y, CORE), [(j, i) for i, j in up])
    parts = pl.pallas_call(
        pack_kernel,
        out_shape=shape((nz, 144, LANES), BF),
        in_specs=[VMEM] * 3,
        out_specs=VMEM,
        compiler_params=PARAMS,
        name="pack",
    )(tok, left, right)
    parts = lax.all_to_all(parts, Z, 0, 0, tiled=True)

    blocks = pl.pallas_call(
        block_kernel,
        out_shape=shape((16, LANES, LANES), BF),
        in_specs=[VMEM] * 2,
        out_specs=VMEM,
        compiler_params=PARAMS,
        name="blocks",
    )(ff_in_weight, ff_out_weight)
    blocks, parts = lax.optimization_barrier((blocks, parts))
    blocks = lax.all_gather(blocks, Z)

    whole = group_gather(parts)
    normed, res = pl.pallas_call(
        gather_kernel,
        out_shape=(shape((full, 2 * run + LANES), BF), shape((256, 2 * run), BF)),
        in_specs=[VMEM] * 5,
        out_specs=(VMEM,) * 2,
        scratch_shapes=[pltpu.VMEM((full, 2 * run), BF), pltpu.VMEM((full, LANES), F32)],
        compiler_params=PARAMS,
        name="gather",
    )(*whole, ln_conv_gain[:, None])
    conv, stats, par = pl.pallas_call(
        conv_kernel,
        out_shape=(
            shape((2 * run, 256), F32),
            shape((nz, 4, LANES), F32),
            shape((8, 256), F32),
        ),
        in_specs=[VMEM, HBM],
        out_specs=(VMEM,) * 3,
        scratch_shapes=[
            pltpu.VMEM((2, run + 40, 256), F32),
            pltpu.VMEM((nz, 64, full), BF),
            pltpu.VMEM((nz, 16, 3 * LANES), BF),
            pltpu.SemaphoreType.DMA((9,)),
        ],
        compiler_params=PARAMS,
        name="conv",
    )(normed, *in_hbm(first))
    stats = lax.all_to_all(stats, Z, 0, 0, tiled=True)
    stats = pl.pallas_call(
        merge_kernel,
        out_shape=shape((lax.axis_size((XLO, Y)), 4, LANES), F32),
        in_specs=[VMEM],
        out_specs=VMEM,
        compiler_params=PARAMS,
        name="merge",
    )(stats)
    stats = lax.all_to_all(stats, (XLO, Y), 0, 0, tiled=True)
    activated = pl.pallas_call(
        bn_kernel,
        out_shape=shape((256, 2 * run), BF),
        in_specs=[VMEM] * 3,
        out_specs=VMEM,
        compiler_params=PARAMS,
        name="bn",
    )(conv, stats, par)
    block = pl.pallas_call(
        mix_kernel,
        out_shape=shape((256, 2 * run), BF),
        grid=(1,),
        in_specs=[VMEM] * 4
        + [
            pl.BlockSpec((nz, 32, full), lambda i: (0, 2, 0)),
            VMEM,
        ],
        out_specs=VMEM,
        scratch_shapes=[pltpu.VMEM((full, 2 * run), BF)],
        compiler_params=PARAMS,
        name="mix",
    )(*group_gather(activated), first, res)
    near, here, there = pl.pallas_call(
        norm_kernel,
        out_shape=(shape((full, run), BF),) * 3,
        in_specs=[VMEM] * 5,
        out_specs=(VMEM,) * 3,
        scratch_shapes=[pltpu.VMEM((full, 2 * run), BF)],
        compiler_params=PARAMS,
        name="norm",
    )(*group_gather(block), ln_ff_gain[:, None])
    give, blocks = pl.pallas_call(
        give_kernel,
        out_shape=(shape((full, run), BF), shape((nz, 16, LANES, LANES), BF)),
        in_specs=[VMEM, HBM],
        out_specs=(VMEM,) * 2,
        scratch_shapes=[pltpu.VMEM((full, run), BF), pltpu.SemaphoreType.DMA((16,))],
        compiler_params=PARAMS,
        name="give",
    )(there, *in_hbm(blocks))
    keep = pl.pallas_call(
        keep_kernel,
        out_shape=shape((full, run), F32),
        in_specs=[VMEM] * 3,
        out_specs=VMEM,
        scratch_shapes=[pltpu.VMEM((full, run), BF)],
        compiler_params=PARAMS,
        cost_estimate=pl.CostEstimate(
            flops=4 * full * full * run, bytes_accessed=6 << 20, transcendentals=full * run
        ),
        name="keep",
    )(near, here, blocks)
    keep = (keep + swap(give, CORE).astype(F32)).astype(BF)
    keep = lax.all_to_all(keep.reshape(2 * nz, width, run), (XHI, Z), 0, 0, tiled=True)
    out = pl.pallas_call(
        sum_kernel,
        out_shape=shape((width, frames), BF),
        in_specs=[VMEM],
        out_specs=VMEM,
        compiler_params=PARAMS,
        name="sum",
    )(keep)
    return out.T


def solution(mesh):
    fine = Mesh(mesh.devices.reshape(2, 8, 2, 2, 8), (XLO, Y, CORE, XHI, Z))
    tm, mp = ((XLO, Y, CORE), (XHI, Z))
    in_specs = (
        P(tm, mp),
        P(),
        P(None, None, mp),
        P(None, mp),
        P(mp),
        P(mp),
        P(None, mp),
        P(),
        P(None, mp),
        P(mp, None),
    )
    return jax.shard_map(body, mesh=fine, in_specs=in_specs, out_specs=P(tm, mp), check_vma=False)
```

```python
import jax
import jax.numpy as jnp
from jax import lax
from jax.experimental import pallas as pl
from jax.experimental.pallas import tpu as pltpu
from jax.sharding import Mesh, PartitionSpec as P

XLO, Y, CORE, XHI, Z = ("xlo", "y", "core", "xhi", "z")
BF, F32 = (jnp.bfloat16, jnp.float32)
EPS = 1e-05
LANES = 128
SPAN = 15
VMEM = pl.BlockSpec(memory_space=pltpu.VMEM)
HBM = pl.BlockSpec(memory_space=pltpu.HBM)
PARAMS = pltpu.CompilerParams(vmem_limit_bytes=40 << 20)


def shape(dims, dtype):
    return jax.ShapeDtypeStruct(dims, dtype)


def in_hbm(*arrays):
    return [pltpu.with_memory_space_constraint(x, pltpu.HBM) for x in arrays]


def swap(x, axis):
    return lax.ppermute(x, axis, [(0, 1), (1, 0)])


def group_gather(x):
    across = swap(x, XHI)
    beside = swap(x, CORE)
    return x, across, beside, swap(across, CORE)


def norm_rows(x, gain):
    inv = 1.0 / x.shape[0]
    centred = x - jnp.sum(x, axis=0, keepdims=True) * inv
    spread = jnp.sum(centred * centred, axis=0, keepdims=True) * inv
    return (centred * lax.rsqrt(spread + EPS) * gain).astype(BF)


def place():
    return lax.axis_index(CORE), lax.axis_index(XHI)


def at(start, size, step):
    return pl.ds(pl.multiple_of(start, step), size)


def weight_kernel(
    glu, conv_out, depth, gain, shift, tok,
    out, near, first, last,
    table, parts, small, sems,
):
    core, _ = place()
    half = at(32 * core, 32, 32)
    taps, width = depth.shape
    frames = tok.shape[1]
    pairs = [
        (depth, small.at[0:taps]),
        (gain, small.at[32:33]),
        (shift, small.at[40:41]),
        (glu.at[0, half], parts.at[0:32]),
        (glu.at[1, half], parts.at[32:64]),
        (conv_out.at[half], parts.at[64:96]),
        (tok.at[:, 0:LANES], first),
        (tok.at[:, frames - LANES : frames], last),
        (tok, near),
    ]
    loads = [pltpu.make_async_copy(a, b, sems.at[i]) for i, (a, b) in enumerate(pairs)]
    for copy in loads:
        copy.start()
    table[...] = jnp.zeros_like(table)
    for copy in loads[:3]:
        copy.wait()
    table[0:taps, 0:width] = small[0:taps]
    table[taps : taps + 1, 0:width] = small[32:33]
    table[taps + 1 : taps + 2, 0:width] = small[40:41]
    lane = lax.broadcasted_iota(jnp.int32, table.shape, 1)
    rest = jnp.where(core == 0, table[...], pltpu.roll(table[...], LANES - 32, 1))
    rest = jnp.where(lane < 32, rest, 0.0)
    packed = jnp.zeros_like(rest)
    for i in range(3):
        piece = rest.astype(BF).astype(F32)
        packed = packed + (piece if i == 0 else pltpu.roll(piece, 32 * i, 1))
        rest = rest - piece
    parts[96:112] = jnp.zeros((16, parts.shape[1]), BF)
    for i in range(3):
        parts[96:112, LANES * i : LANES * (i + 1)] = packed[16 * i : 16 * i + 16].astype(BF)
    for copy in loads[3:6]:
        copy.wait()
    final = pltpu.make_async_copy(parts, out, sems.at[9])
    final.start()
    for copy in loads[6:] + [final]:
        copy.wait()


def block_kernel(ff_in, ff_out, out):
    half = at(place()[0] * LANES, LANES, LANES)
    for k in range(8):
        tile = slice(LANES * k, LANES * (k + 1))
        out[k] = ff_in[tile, half].astype(F32).T.astype(BF)
        out[8 + k] = ff_out[half, tile].astype(F32).T.astype(BF)


def pack_kernel(tok, left, right, out):
    lane = lax.broadcasted_iota(jnp.int32, (16, LANES), 1)
    nz = out.shape[0]
    for z in range(nz):
        out[z, 0:64] = tok[:, 2 * z * LANES : (2 * z + 1) * LANES]
        out[z, 64:128] = tok[:, (2 * z + 1) * LANES : (2 * z + 2) * LANES]
        packed = jnp.zeros((16, LANES), F32)
        for i in range(4):
            rows = slice(16 * i, 16 * i + 16)
            if z == 0:
                before = left[rows]
            else:
                before = tok[rows, (2 * z - 1) * LANES : 2 * z * LANES]
            if z == nz - 1:
                after = right[rows]
            else:
                after = tok[rows, (2 * z + 2) * LANES : (2 * z + 3) * LANES]
            low = pltpu.roll(before.astype(F32), (32 * i + SPAN) % LANES, 1)
            high = pltpu.roll(after.astype(F32), 32 * i + SPAN, 1)
            packed = jnp.where((lane >= 32 * i) & (lane < 32 * i + SPAN), low, packed)
            packed = jnp.where(
                (lane >= 32 * i + SPAN) & (lane < 32 * i + 2 * SPAN), high, packed
            )
        out[z, 128:144] = packed.astype(BF)


def gather_kernel(own, across, beside, far, gain, normed, res, tok, edge):
    core, xhi = place()
    lane = lax.broadcasted_iota(jnp.int32, (16, LANES), 1)
    nz = own.shape[0]
    for near, away, side in ((own, beside, xhi), (across, far, 1 - xhi)):
        for z in range(nz):
            row = side * (64 * nz) + 64 * z
            for c, blk in ((0, near), (1, away)):
                tok[at(row, 64, 64), 256 * c : 256 * c + 128] = blk[z, 0:64]
                tok[at(row, 64, 64), 256 * c + 128 : 256 * c + 256] = blk[z, 64:128]
            one = near[z, 128:144].astype(F32)
            two = away[z, 128:144].astype(F32)
            for i in range(4):
                low = pltpu.roll(one, (LANES - 32 * i) % LANES, 1)
                high = pltpu.roll(two, (LANES + 32 - 32 * i) % LANES, 1)
                part = jnp.where(lane < 32, low, jnp.where(lane < 64, high, 0.0))
                edge[at(row + 16 * i, 16, 16), :] = part
    for z in range(nz):
        row = xhi * (64 * nz) + 64 * z + 32 * core
        res[32 * z : 32 * z + 32, :] = tok[at(row, 32, 32), :]

    scale = gain[...]
    for c in range(2):
        cols = slice(256 * c, 256 * (c + 1))
        normed[:, cols] = norm_rows(tok[:, cols].astype(F32), scale)
    normed[:, 512:640] = norm_rows(edge[...], scale)


def conv_kernel(normed, first, conv, stats, par, win, weight, small, sems):
    loads = [
        pltpu.make_async_copy(first.at[:, 96:112, 0:384], small, sems.at[1]),
        pltpu.make_async_copy(first.at[:, 0:64], weight, sems.at[0]),
    ]
    for copy in loads:
        copy.start()
    nz = small.shape[0]
    loads[0].wait()
    table = []
    lane = lax.broadcasted_iota(jnp.int32, (48, LANES), 1)
    for h in range(2):
        total = jnp.zeros((48, LANES), F32)
        for i in range(4):
            x = [small[4 * h + i, :, LANES * k : LANES * (k + 1)] for k in range(3)]
            x = jnp.concatenate(x, axis=0).astype(F32)
            x = x + (pltpu.roll(x, LANES - 32, 1) + pltpu.roll(x, LANES - 64, 1))
            x = jnp.where(lane < 32, x, 0.0)
            total = total + (x if i == 0 else pltpu.roll(x, 32 * i, 1))
        par[:, LANES * h : LANES * (h + 1)] = total[31:39]
        table.append(total)
    loads[1].wait()
    glu = weight[...].reshape(64 * nz, weight.shape[2])
    for c in range(3):
        x = normed[:, 512:640] if c == 2 else normed[:, 256 * c : 256 * (c + 1)]
        paired = jnp.dot(glu, x, preferred_element_type=F32)
        cols = x.shape[1]
        paired = paired.reshape(nz, 2, 32, cols)
        gated = (paired[:, 0] * jax.nn.sigmoid(paired[:, 1])).astype(BF).astype(F32)
        gated = gated.reshape(32 * nz, cols).T
        if c < 2:
            win[c, 16:272, :] = gated
        else:
            for r in range(2):
                win[r, 1:16, :] = gated[32 * r : 32 * r + 15]
                win[r, 272:287, :] = gated[32 * r + 15 : 32 * r + 30]

    step = 64
    for h in range(2):
        cols = slice(LANES * h, LANES * (h + 1))
        total = jnp.zeros((1, LANES), F32)
        for r in range(2):
            for k in range(256 // step):
                acc = jnp.zeros((step, LANES), F32)
                for j in range(31):
                    first = step * k + 1 + j
                    acc = acc + table[h][j : j + 1] * win[r, first : first + step, cols]
                conv[256 * r + step * k : 256 * r + step * (k + 1), cols] = acc
                total = total + jnp.sum(acc, axis=0, keepdims=True)
        mean = total * (1.0 / 512)
        apart = conv[:, cols] - mean
        square = jnp.sum(apart * apart, axis=0, keepdims=True)
        n = stats.shape[0]
        stats[:, h : h + 1, :] = jnp.broadcast_to(mean[None], (n, 1, LANES))
        stats[:, 2 + h : 3 + h, :] = jnp.broadcast_to(square[None], (n, 1, LANES))


def merged(stats, count):
    total = jnp.sum(stats, axis=0)
    mean = total * (1.0 / stats.shape[0])
    apart = stats - mean[None]
    apart = jnp.sum(apart * apart, axis=0)
    return mean[0:2], total[2:4] + count * apart[0:2]


def merge_kernel(stats, out):
    mean, square = merged(stats[...], 512)
    out[:, 0:2] = jnp.broadcast_to(mean[None], (out.shape[0],) + mean.shape)
    out[:, 2:4] = jnp.broadcast_to(square[None], (out.shape[0],) + square.shape)


def bn_kernel(conv, stats, par, out):
    frames = 16 * conv.shape[0]
    mean, square = merged(stats[...], frames)
    scale = lax.rsqrt(square * (1.0 / (frames * stats.shape[0])) + EPS)
    for h in range(2):
        cols = slice(LANES * h, LANES * (h + 1))
        value = (conv[:, cols] - mean[h : h + 1]) * (scale[h : h + 1] * par[0:1, cols])
        value = value + par[1:2, cols]
        out[cols, :] = (value * jax.nn.sigmoid(value)).T.astype(BF)


def place_blocks(own, across, beside, far, whole):
    core, xhi = place()
    nz, half = 8, 256
    for blk, c, x in ((own, core, xhi), (across, core, 1 - xhi)):
        for z in range(nz):
            row = x * 512 + 64 * z + 32 * c
            whole[at(row, 32, 32), :] = blk[32 * z : 32 * z + 32, :]
    for blk, c, x in ((beside, 1 - core, xhi), (far, 1 - core, 1 - xhi)):
        for z in range(nz):
            row = x * 512 + 64 * z + 32 * c
            whole[at(row, 32, 32), :half] = blk[32 * z : 32 * z + 32, half:]
            whole[at(row, 32, 32), half:] = blk[32 * z : 32 * z + 32, :half]


def mix_kernel(own, across, beside, far, blocks, res, out, whole):
    place_blocks(own, across, beside, far, whole)
    weight = blocks[...].reshape(256, blocks.shape[2])
    mixed = jnp.dot(weight, whole[...], preferred_element_type=F32)
    out[...] = (res[...].astype(F32) + mixed).astype(BF)


def norm_kernel(own, across, beside, far, gain, near, here, there, whole):
    place_blocks(own, across, beside, far, whole)
    half = here.shape[1]
    near[...] = whole[:, :half]
    for c, normed in ((0, here), (1, there)):
        cols = slice(half * c, half * (c + 1))
        normed[...] = norm_rows(whole[:, cols].astype(F32), gain[...])


def feed_forward(normed, w, hidden, ready):
    for z in range(0, 8, 2):
        ready(z // 2)
        rows = [jnp.concatenate([w[z + i, k] for k in range(8)], axis=1) for i in range(2)]
        value = jnp.dot(
            jnp.concatenate(rows, axis=0), normed[...], preferred_element_type=F32
        )
        hidden[LANES * z : LANES * (z + 2), :] = (value * jax.nn.sigmoid(value)).astype(BF)
    ready(4)
    for k in range(0, 8, 2):
        rows = [jnp.concatenate([w[z, 8 + k + i] for z in range(8)], axis=1) for i in range(2)]
        value = jnp.dot(
            jnp.concatenate(rows, axis=0), hidden[...], preferred_element_type=F32
        )
        yield k, slice(LANES * k, LANES * (k + 2)), 0.5 * value


def give_kernel(normed, blocks, give, w, hidden, sems):
    loads = [
        pltpu.make_async_copy(
            blocks.at[2 * i : 2 * i + 2, 0:8], w.at[2 * i : 2 * i + 2, 0:8], sems.at[i]
        )
        for i in range(4)
    ]
    loads.append(pltpu.make_async_copy(blocks.at[:, 8:16], w.at[:, 8:16], sems.at[4]))
    for copy in loads:
        copy.start()
    for _, rows, value in feed_forward(normed, w, hidden, lambda i: loads[i].wait()):
        give[rows, :] = value.astype(BF)


def keep_kernel(near, normed, w, keep, hidden):
    xhi = place()[1]
    for k, rows, value in feed_forward(normed, w, hidden, lambda i: None):
        mine = jnp.where(xhi == k // 4, 1.0, 0.0)
        keep[rows, :] = value + mine * near[rows, :].astype(F32)


def sum_kernel(parts, out):
    nz, run = parts.shape[0] // 2, parts.shape[2]
    for z in range(nz):
        value = parts[z].astype(F32) + parts[nz + z].astype(F32)
        out[:, run * z : run * (z + 1)] = value.astype(BF)


def body(
    tokens,
    ln_conv_gain,
    glu_weight,
    depth_weight,
    bn_gain,
    bn_shift,
    conv_out_weight,
    ln_ff_gain,
    ff_in_weight,
    ff_out_weight,
):
    nz = lax.axis_size(Z)
    frames, width = tokens.shape
    full = ln_conv_gain.shape[0]
    run = frames // nz

    first, tok, head, tail = pl.pallas_call(
        weight_kernel,
        out_shape=(
            shape((112, full), BF),
            shape((width, frames), BF),
            shape((width, LANES), BF),
            shape((width, LANES), BF),
        ),
        in_specs=[HBM] * 6,
        out_specs=(HBM, VMEM, VMEM, VMEM),
        scratch_shapes=[
            pltpu.VMEM((48, LANES), F32),
            pltpu.VMEM((112, full), BF),
            pltpu.VMEM((48, width), F32),
            pltpu.SemaphoreType.DMA((10,)),
        ],
        compiler_params=PARAMS,
        name="weights",
    )(
        *in_hbm(
            glu_weight.transpose(1, 2, 0),
            conv_out_weight.T,
            depth_weight,
            bn_gain[None],
            bn_shift[None],
            tokens.T,
        )
    )
    first = lax.all_gather(first, Z)

    tm = lax.axis_size((XLO, Y, CORE))
    up = [(i, i + 1) for i in range(tm - 1)]
    left = lax.ppermute(tail, (XLO, Y, CORE), up)
    right = lax.ppermute(head, (XLO, Y, CORE), [(j, i) for i, j in up])
    parts = pl.pallas_call(
        pack_kernel,
        out_shape=shape((nz, 144, LANES), BF),
        in_specs=[VMEM] * 3,
        out_specs=VMEM,
        compiler_params=PARAMS,
        name="pack",
    )(tok, left, right)
    parts = lax.all_to_all(parts, Z, 0, 0, tiled=True)

    blocks = pl.pallas_call(
        block_kernel,
        out_shape=shape((16, LANES, LANES), BF),
        in_specs=[VMEM] * 2,
        out_specs=VMEM,
        compiler_params=PARAMS,
        name="blocks",
    )(ff_in_weight, ff_out_weight)
    blocks, parts = lax.optimization_barrier((blocks, parts))
    blocks = lax.all_gather(blocks, Z)

    whole = group_gather(parts)
    normed, res = pl.pallas_call(
        gather_kernel,
        out_shape=(shape((full, 2 * run + LANES), BF), shape((256, 2 * run), BF)),
        in_specs=[VMEM] * 5,
        out_specs=(VMEM,) * 2,
        scratch_shapes=[pltpu.VMEM((full, 2 * run), BF), pltpu.VMEM((full, LANES), F32)],
        compiler_params=PARAMS,
        name="gather",
    )(*whole, ln_conv_gain[:, None])
    conv, stats, par = pl.pallas_call(
        conv_kernel,
        out_shape=(
            shape((2 * run, 256), F32),
            shape((lax.axis_size((XLO, Y)), 4, LANES), F32),
            shape((8, 256), F32),
        ),
        in_specs=[VMEM, HBM],
        out_specs=(VMEM,) * 3,
        scratch_shapes=[
            pltpu.VMEM((2, run + 40, 256), F32),
            pltpu.VMEM((nz, 64, full), BF),
            pltpu.VMEM((nz, 16, 3 * LANES), BF),
            pltpu.SemaphoreType.DMA((2,)),
        ],
        compiler_params=PARAMS,
        name="conv",
    )(normed, *in_hbm(first))
    stats = lax.all_to_all(stats, (XLO, Y), 0, 0, tiled=True)
    stats = pl.pallas_call(
        merge_kernel,
        out_shape=shape((nz, 4, LANES), F32),
        in_specs=[VMEM],
        out_specs=VMEM,
        compiler_params=PARAMS,
        name="merge",
    )(stats)
    stats = lax.all_to_all(stats, Z, 0, 0, tiled=True)
    activated = pl.pallas_call(
        bn_kernel,
        out_shape=shape((256, 2 * run), BF),
        in_specs=[VMEM] * 3,
        out_specs=VMEM,
        compiler_params=PARAMS,
        name="bn",
    )(conv, stats, par)
    block = pl.pallas_call(
        mix_kernel,
        out_shape=shape((256, 2 * run), BF),
        grid=(1,),
        in_specs=[VMEM] * 4
        + [
            pl.BlockSpec((nz, 32, full), lambda i: (0, 2, 0)),
            VMEM,
        ],
        out_specs=VMEM,
        scratch_shapes=[pltpu.VMEM((full, 2 * run), BF)],
        compiler_params=PARAMS,
        name="mix",
    )(*group_gather(activated), first, res)
    near, here, there = pl.pallas_call(
        norm_kernel,
        out_shape=(shape((full, run), BF),) * 3,
        in_specs=[VMEM] * 5,
        out_specs=(VMEM,) * 3,
        scratch_shapes=[pltpu.VMEM((full, 2 * run), BF)],
        compiler_params=PARAMS,
        name="norm",
    )(*group_gather(block), ln_ff_gain[:, None])
    give, blocks = pl.pallas_call(
        give_kernel,
        out_shape=(shape((full, run), BF), shape((nz, 16, LANES, LANES), BF)),
        in_specs=[VMEM, HBM],
        out_specs=(VMEM,) * 2,
        scratch_shapes=[pltpu.VMEM((full, run), BF), pltpu.SemaphoreType.DMA((5,))],
        compiler_params=PARAMS,
        name="give",
    )(there, *in_hbm(blocks))
    keep = pl.pallas_call(
        keep_kernel,
        out_shape=shape((full, run), F32),
        in_specs=[VMEM] * 3,
        out_specs=VMEM,
        scratch_shapes=[pltpu.VMEM((full, run), BF)],
        compiler_params=PARAMS,
        cost_estimate=pl.CostEstimate(
            flops=4 * full * full * run, bytes_accessed=6 << 20, transcendentals=full * run
        ),
        name="keep",
    )(near, here, blocks)
    keep = (keep + swap(give, CORE).astype(F32)).astype(BF)
    keep = lax.all_to_all(keep.reshape(2 * nz, width, run), (XHI, Z), 0, 0, tiled=True)
    out = pl.pallas_call(
        sum_kernel,
        out_shape=shape((width, frames), BF),
        in_specs=[VMEM],
        out_specs=VMEM,
        compiler_params=PARAMS,
        name="sum",
    )(keep)
    return out.T


def solution(mesh):
    fine = Mesh(mesh.devices.reshape(2, 8, 2, 2, 8), (XLO, Y, CORE, XHI, Z))
    tm, mp = ((XLO, Y, CORE), (XHI, Z))
    in_specs = (
        P(tm, mp),
        P(),
        P(None, None, mp),
        P(None, mp),
        P(mp),
        P(mp),
        P(None, mp),
        P(),
        P(None, mp),
        P(mp, None),
    )
    return jax.shard_map(body, mesh=fine, in_specs=in_specs, out_specs=P(tm, mp), check_vma=False)
```

```python
import jax
import jax.numpy as jnp
from jax import lax
from jax.experimental import pallas as pl
from jax.experimental.pallas import tpu as pltpu
from jax.sharding import Mesh, PartitionSpec as P

XLO, Y, CORE, XHI, Z = ("xlo", "y", "core", "xhi", "z")
BF, F32 = (jnp.bfloat16, jnp.float32)
EPS = 1e-05
LANES = 128
SPAN = 15
VMEM = pl.BlockSpec(memory_space=pltpu.VMEM)
HBM = pl.BlockSpec(memory_space=pltpu.HBM)
PARAMS = pltpu.CompilerParams(vmem_limit_bytes=40 << 20)


def shape(dims, dtype):
    return jax.ShapeDtypeStruct(dims, dtype)


def in_hbm(*arrays):
    return [pltpu.with_memory_space_constraint(x, pltpu.HBM) for x in arrays]


def swap(x, axis):
    return lax.ppermute(x, axis, [(0, 1), (1, 0)])


def group_gather(x):
    across = swap(x, XHI)
    beside = swap(x, CORE)
    return x, across, beside, swap(across, CORE)


def norm_rows(x, gain):
    inv = 1.0 / x.shape[0]
    centred = x - jnp.sum(x, axis=0, keepdims=True) * inv
    spread = jnp.sum(centred * centred, axis=0, keepdims=True) * inv
    return (centred * lax.rsqrt(spread + EPS) * gain).astype(BF)


def place():
    return lax.axis_index(CORE), lax.axis_index(XHI)


def at(start, size, step):
    return pl.ds(pl.multiple_of(start, step), size)


def weight_kernel(
    glu, conv_out, depth, gain, shift, tok,
    out, near, first, last,
    table, parts, small, sems,
):
    core, _ = place()
    half = at(32 * core, 32, 32)
    taps, width = depth.shape
    frames = tok.shape[1]
    pairs = [
        (depth, small.at[0:taps]),
        (gain, small.at[32:33]),
        (shift, small.at[40:41]),
        (glu.at[0, half], parts.at[0:32]),
        (glu.at[1, half], parts.at[32:64]),
        (conv_out.at[half], parts.at[64:96]),
        (tok.at[:, 0:LANES], first),
        (tok.at[:, frames - LANES : frames], last),
        (tok, near),
    ]
    loads = [pltpu.make_async_copy(a, b, sems.at[i]) for i, (a, b) in enumerate(pairs)]
    for copy in loads:
        copy.start()
    table[...] = jnp.zeros_like(table)
    for copy in loads[:3]:
        copy.wait()
    table[0:taps, 0:width] = small[0:taps]
    table[taps : taps + 1, 0:width] = small[32:33]
    table[taps + 1 : taps + 2, 0:width] = small[40:41]
    lane = lax.broadcasted_iota(jnp.int32, table.shape, 1)
    rest = jnp.where(core == 0, table[...], pltpu.roll(table[...], LANES - 32, 1))
    rest = jnp.where(lane < 32, rest, 0.0)
    packed = jnp.zeros_like(rest)
    for i in range(3):
        piece = rest.astype(BF).astype(F32)
        packed = packed + (piece if i == 0 else pltpu.roll(piece, 32 * i, 1))
        rest = rest - piece
    parts[96:112] = jnp.zeros((16, parts.shape[1]), BF)
    for i in range(3):
        parts[96:112, LANES * i : LANES * (i + 1)] = packed[16 * i : 16 * i + 16].astype(BF)
    for copy in loads[3:6]:
        copy.wait()
    final = pltpu.make_async_copy(parts, out, sems.at[9])
    final.start()
    for copy in loads[6:] + [final]:
        copy.wait()


def block_kernel(ff_in, ff_out, out):
    half = at(place()[0] * LANES, LANES, LANES)
    for k in range(8):
        tile = slice(LANES * k, LANES * (k + 1))
        out[k] = ff_in[tile, half].astype(F32).T.astype(BF)
        out[8 + k] = ff_out[half, tile].astype(F32).T.astype(BF)


def pack_kernel(tok, left, right, out):
    lane = lax.broadcasted_iota(jnp.int32, (16, LANES), 1)
    nz = out.shape[0]
    for z in range(nz):
        out[z, 0:64] = tok[:, 2 * z * LANES : (2 * z + 1) * LANES]
        out[z, 64:128] = tok[:, (2 * z + 1) * LANES : (2 * z + 2) * LANES]
        packed = jnp.zeros((16, LANES), F32)
        for i in range(4):
            rows = slice(16 * i, 16 * i + 16)
            if z == 0:
                before = left[rows]
            else:
                before = tok[rows, (2 * z - 1) * LANES : 2 * z * LANES]
            if z == nz - 1:
                after = right[rows]
            else:
                after = tok[rows, (2 * z + 2) * LANES : (2 * z + 3) * LANES]
            low = pltpu.roll(before.astype(F32), (32 * i + SPAN) % LANES, 1)
            high = pltpu.roll(after.astype(F32), 32 * i + SPAN, 1)
            packed = jnp.where((lane >= 32 * i) & (lane < 32 * i + SPAN), low, packed)
            packed = jnp.where(
                (lane >= 32 * i + SPAN) & (lane < 32 * i + 2 * SPAN), high, packed
            )
        out[z, 128:144] = packed.astype(BF)


def gather_kernel(own, across, beside, far, gain, normed, res, tok, edge):
    core, xhi = place()
    lane = lax.broadcasted_iota(jnp.int32, (16, LANES), 1)
    nz = own.shape[0]
    for near, away, side in ((own, beside, xhi), (across, far, 1 - xhi)):
        for z in range(nz):
            row = side * (64 * nz) + 64 * z
            for c, blk in ((0, near), (1, away)):
                tok[at(row, 64, 64), 256 * c : 256 * c + 128] = blk[z, 0:64]
                tok[at(row, 64, 64), 256 * c + 128 : 256 * c + 256] = blk[z, 64:128]
            one = near[z, 128:144].astype(F32)
            two = away[z, 128:144].astype(F32)
            for i in range(4):
                low = pltpu.roll(one, (LANES - 32 * i) % LANES, 1)
                high = pltpu.roll(two, (LANES + 32 - 32 * i) % LANES, 1)
                part = jnp.where(lane < 32, low, jnp.where(lane < 64, high, 0.0))
                edge[at(row + 16 * i, 16, 16), :] = part
    for z in range(nz):
        row = xhi * (64 * nz) + 64 * z + 32 * core
        res[32 * z : 32 * z + 32, :] = tok[at(row, 32, 32), :]

    scale = gain[...]
    for c in range(2):
        cols = slice(256 * c, 256 * (c + 1))
        normed[:, cols] = norm_rows(tok[:, cols].astype(F32), scale)
    normed[:, 512:640] = norm_rows(edge[...], scale)


def conv_kernel(normed, first, conv, stats, par, win, weight, small, sems):
    loads = [
        pltpu.make_async_copy(first.at[:, 96:112, 0:384], small, sems.at[1]),
        pltpu.make_async_copy(first.at[:, 0:64], weight, sems.at[0]),
    ]
    for copy in loads:
        copy.start()
    nz = small.shape[0]
    loads[0].wait()
    table = []
    lane = lax.broadcasted_iota(jnp.int32, (48, LANES), 1)
    for h in range(2):
        total = jnp.zeros((48, LANES), F32)
        for i in range(4):
            x = [small[4 * h + i, :, LANES * k : LANES * (k + 1)] for k in range(3)]
            x = jnp.concatenate(x, axis=0).astype(F32)
            x = x + (pltpu.roll(x, LANES - 32, 1) + pltpu.roll(x, LANES - 64, 1))
            x = jnp.where(lane < 32, x, 0.0)
            total = total + (x if i == 0 else pltpu.roll(x, 32 * i, 1))
        par[:, LANES * h : LANES * (h + 1)] = total[31:39]
        table.append(total)
    loads[1].wait()
    glu = weight[...].reshape(64 * nz, weight.shape[2])
    for c in range(3):
        x = normed[:, 512:640] if c == 2 else normed[:, 256 * c : 256 * (c + 1)]
        paired = jnp.dot(glu, x, preferred_element_type=F32)
        cols = x.shape[1]
        paired = paired.reshape(nz, 2, 32, cols)
        gated = (paired[:, 0] * jax.nn.sigmoid(paired[:, 1])).astype(BF).astype(F32)
        gated = gated.reshape(32 * nz, cols).T
        if c < 2:
            win[c, 16:272, :] = gated
        else:
            for r in range(2):
                win[r, 1:16, :] = gated[32 * r : 32 * r + 15]
                win[r, 272:287, :] = gated[32 * r + 15 : 32 * r + 30]

    step = 64
    for h in range(2):
        cols = slice(LANES * h, LANES * (h + 1))
        total = jnp.zeros((1, LANES), F32)
        for r in range(2):
            for k in range(256 // step):
                acc = jnp.zeros((step, LANES), F32)
                for j in range(31):
                    first = step * k + 1 + j
                    acc = acc + table[h][j : j + 1] * win[r, first : first + step, cols]
                conv[256 * r + step * k : 256 * r + step * (k + 1), cols] = acc
                total = total + jnp.sum(acc, axis=0, keepdims=True)
        mean = total * (1.0 / 512)
        apart = conv[:, cols] - mean
        square = jnp.sum(apart * apart, axis=0, keepdims=True)
        n = stats.shape[0]
        stats[:, h : h + 1, :] = jnp.broadcast_to(mean[None], (n, 1, LANES))
        stats[:, 2 + h : 3 + h, :] = jnp.broadcast_to(square[None], (n, 1, LANES))


def merged(stats, count):
    total = jnp.sum(stats, axis=0)
    mean = total * (1.0 / stats.shape[0])
    apart = stats - mean[None]
    apart = jnp.sum(apart * apart, axis=0)
    return mean[0:2], total[2:4] + count * apart[0:2]


def merge_kernel(stats, out):
    mean, square = merged(stats[...], 512)
    out[:, 0:2] = jnp.broadcast_to(mean[None], (out.shape[0],) + mean.shape)
    out[:, 2:4] = jnp.broadcast_to(square[None], (out.shape[0],) + square.shape)


def bn_kernel(conv, stats, par, out):
    frames = 16 * conv.shape[0]
    mean, square = merged(stats[...], frames)
    scale = lax.rsqrt(square * (1.0 / (frames * stats.shape[0])) + EPS)
    for h in range(2):
        cols = slice(LANES * h, LANES * (h + 1))
        value = (conv[:, cols] - mean[h : h + 1]) * (scale[h : h + 1] * par[0:1, cols])
        value = value + par[1:2, cols]
        out[cols, :] = (value * jax.nn.sigmoid(value)).T.astype(BF)


def place_blocks(own, across, beside, far, whole):
    core, xhi = place()
    nz, half = 8, 256
    for blk, c, x in ((own, core, xhi), (across, core, 1 - xhi)):
        for z in range(nz):
            row = x * 512 + 64 * z + 32 * c
            whole[at(row, 32, 32), :] = blk[32 * z : 32 * z + 32, :]
    for blk, c, x in ((beside, 1 - core, xhi), (far, 1 - core, 1 - xhi)):
        for z in range(nz):
            row = x * 512 + 64 * z + 32 * c
            whole[at(row, 32, 32), :half] = blk[32 * z : 32 * z + 32, half:]
            whole[at(row, 32, 32), half:] = blk[32 * z : 32 * z + 32, :half]


def mix_kernel(own, across, beside, far, blocks, res, out, whole):
    place_blocks(own, across, beside, far, whole)
    weight = blocks[...].reshape(256, blocks.shape[2])
    mixed = jnp.dot(weight, whole[...], preferred_element_type=F32)
    out[...] = (res[...].astype(F32) + mixed).astype(BF)


def feed_forward(normed, w, hidden, ready):
    for z in range(0, 8, 2):
        ready(z // 2)
        rows = [jnp.concatenate([w[z + i, k] for k in range(8)], axis=1) for i in range(2)]
        value = jnp.dot(
            jnp.concatenate(rows, axis=0), normed[...], preferred_element_type=F32
        )
        hidden[LANES * z : LANES * (z + 2), :] = (value * jax.nn.sigmoid(value)).astype(BF)
    ready(4)
    for k in range(0, 8, 2):
        rows = [jnp.concatenate([w[z, 8 + k + i] for z in range(8)], axis=1) for i in range(2)]
        value = jnp.dot(
            jnp.concatenate(rows, axis=0), hidden[...], preferred_element_type=F32
        )
        yield k, slice(LANES * k, LANES * (k + 2)), 0.5 * value


def give_kernel(
    own, across, beside, far, gain, blocks,
    give, w, near, here,
    whole, there, hidden, sems,
):
    loads = [
        pltpu.make_async_copy(
            blocks.at[2 * i : 2 * i + 2, 0:8], w.at[2 * i : 2 * i + 2, 0:8], sems.at[i]
        )
        for i in range(4)
    ]
    loads.append(pltpu.make_async_copy(blocks.at[:, 8:16], w.at[:, 8:16], sems.at[4]))
    for copy in loads:
        copy.start()
    place_blocks(own, across, beside, far, whole)
    half = here.shape[1]
    near[...] = whole[:, :half]
    for c, normed in ((0, here), (1, there)):
        cols = slice(half * c, half * (c + 1))
        normed[...] = norm_rows(whole[:, cols].astype(F32), gain[...])
    for _, rows, value in feed_forward(there, w, hidden, lambda i: loads[i].wait()):
        give[rows, :] = value.astype(BF)


def keep_kernel(near, normed, w, keep, hidden):
    xhi = place()[1]
    for k, rows, value in feed_forward(normed, w, hidden, lambda i: None):
        mine = jnp.where(xhi == k // 4, 1.0, 0.0)
        keep[rows, :] = value + mine * near[rows, :].astype(F32)


def sum_kernel(parts, out):
    nz, run = parts.shape[0] // 2, parts.shape[2]
    for z in range(nz):
        value = parts[z].astype(F32) + parts[nz + z].astype(F32)
        out[:, run * z : run * (z + 1)] = value.astype(BF)


def body(
    tokens,
    ln_conv_gain,
    glu_weight,
    depth_weight,
    bn_gain,
    bn_shift,
    conv_out_weight,
    ln_ff_gain,
    ff_in_weight,
    ff_out_weight,
):
    nz = lax.axis_size(Z)
    frames, width = tokens.shape
    full = ln_conv_gain.shape[0]
    run = frames // nz

    first, tok, head, tail = pl.pallas_call(
        weight_kernel,
        out_shape=(
            shape((112, full), BF),
            shape((width, frames), BF),
            shape((width, LANES), BF),
            shape((width, LANES), BF),
        ),
        in_specs=[HBM] * 6,
        out_specs=(HBM, VMEM, VMEM, VMEM),
        scratch_shapes=[
            pltpu.VMEM((48, LANES), F32),
            pltpu.VMEM((112, full), BF),
            pltpu.VMEM((48, width), F32),
            pltpu.SemaphoreType.DMA((10,)),
        ],
        compiler_params=PARAMS,
        name="weights",
    )(
        *in_hbm(
            glu_weight.transpose(1, 2, 0),
            conv_out_weight.T,
            depth_weight,
            bn_gain[None],
            bn_shift[None],
            tokens.T,
        )
    )
    first = lax.all_gather(first, Z)

    tm = lax.axis_size((XLO, Y, CORE))
    up = [(i, i + 1) for i in range(tm - 1)]
    left = lax.ppermute(tail, (XLO, Y, CORE), up)
    right = lax.ppermute(head, (XLO, Y, CORE), [(j, i) for i, j in up])
    parts = pl.pallas_call(
        pack_kernel,
        out_shape=shape((nz, 144, LANES), BF),
        in_specs=[VMEM] * 3,
        out_specs=VMEM,
        compiler_params=PARAMS,
        name="pack",
    )(tok, left, right)
    parts = lax.all_to_all(parts, Z, 0, 0, tiled=True)

    blocks = pl.pallas_call(
        block_kernel,
        out_shape=shape((16, LANES, LANES), BF),
        in_specs=[VMEM] * 2,
        out_specs=VMEM,
        compiler_params=PARAMS,
        name="blocks",
    )(ff_in_weight, ff_out_weight)
    blocks, parts = lax.optimization_barrier((blocks, parts))
    blocks = lax.all_gather(blocks, Z)

    whole = group_gather(parts)
    normed, res = pl.pallas_call(
        gather_kernel,
        out_shape=(shape((full, 2 * run + LANES), BF), shape((256, 2 * run), BF)),
        in_specs=[VMEM] * 5,
        out_specs=(VMEM,) * 2,
        scratch_shapes=[pltpu.VMEM((full, 2 * run), BF), pltpu.VMEM((full, LANES), F32)],
        compiler_params=PARAMS,
        name="gather",
    )(*whole, ln_conv_gain[:, None])
    conv, stats, par = pl.pallas_call(
        conv_kernel,
        out_shape=(
            shape((2 * run, 256), F32),
            shape((lax.axis_size((XLO, Y)), 4, LANES), F32),
            shape((8, 256), F32),
        ),
        in_specs=[VMEM, HBM],
        out_specs=(VMEM,) * 3,
        scratch_shapes=[
            pltpu.VMEM((2, run + 40, 256), F32),
            pltpu.VMEM((nz, 64, full), BF),
            pltpu.VMEM((nz, 16, 3 * LANES), BF),
            pltpu.SemaphoreType.DMA((2,)),
        ],
        compiler_params=PARAMS,
        name="conv",
    )(normed, *in_hbm(first))
    stats = lax.all_to_all(stats, (XLO, Y), 0, 0, tiled=True)
    stats = pl.pallas_call(
        merge_kernel,
        out_shape=shape((nz, 4, LANES), F32),
        in_specs=[VMEM],
        out_specs=VMEM,
        compiler_params=PARAMS,
        name="merge",
    )(stats)
    stats = lax.all_to_all(stats, Z, 0, 0, tiled=True)
    activated = pl.pallas_call(
        bn_kernel,
        out_shape=shape((256, 2 * run), BF),
        in_specs=[VMEM] * 3,
        out_specs=VMEM,
        compiler_params=PARAMS,
        name="bn",
    )(conv, stats, par)
    block = pl.pallas_call(
        mix_kernel,
        out_shape=shape((256, 2 * run), BF),
        grid=(1,),
        in_specs=[VMEM] * 4
        + [
            pl.BlockSpec((nz, 32, full), lambda i: (0, 2, 0)),
            VMEM,
        ],
        out_specs=VMEM,
        scratch_shapes=[pltpu.VMEM((full, 2 * run), BF)],
        compiler_params=PARAMS,
        name="mix",
    )(*group_gather(activated), first, res)
    give, blocks, near, here = pl.pallas_call(
        give_kernel,
        out_shape=(
            shape((full, run), BF),
            shape((nz, 16, LANES, LANES), BF),
            shape((full, run), BF),
            shape((full, run), BF),
        ),
        in_specs=[VMEM] * 5 + [HBM],
        out_specs=(VMEM,) * 4,
        scratch_shapes=[
            pltpu.VMEM((full, 2 * run), BF),
            pltpu.VMEM((full, run), BF),
            pltpu.VMEM((full, run), BF),
            pltpu.SemaphoreType.DMA((5,)),
        ],
        compiler_params=PARAMS,
        name="give",
    )(*group_gather(block), ln_ff_gain[:, None], *in_hbm(blocks))
    keep = pl.pallas_call(
        keep_kernel,
        out_shape=shape((full, run), F32),
        in_specs=[VMEM] * 3,
        out_specs=VMEM,
        scratch_shapes=[pltpu.VMEM((full, run), BF)],
        compiler_params=PARAMS,
        cost_estimate=pl.CostEstimate(
            flops=4 * full * full * run, bytes_accessed=6 << 20, transcendentals=full * run
        ),
        name="keep",
    )(near, here, blocks)
    keep = (keep + swap(give, CORE).astype(F32)).astype(BF)
    keep = lax.all_to_all(keep.reshape(2 * nz, width, run), (XHI, Z), 0, 0, tiled=True)
    out = pl.pallas_call(
        sum_kernel,
        out_shape=shape((width, frames), BF),
        in_specs=[VMEM],
        out_specs=VMEM,
        compiler_params=PARAMS,
        name="sum",
    )(keep)
    return out.T


def solution(mesh):
    fine = Mesh(mesh.devices.reshape(2, 8, 2, 2, 8), (XLO, Y, CORE, XHI, Z))
    tm, mp = ((XLO, Y, CORE), (XHI, Z))
    in_specs = (
        P(tm, mp),
        P(),
        P(None, None, mp),
        P(None, mp),
        P(mp),
        P(mp),
        P(None, mp),
        P(),
        P(None, mp),
        P(mp, None),
    )
    return jax.shard_map(body, mesh=fine, in_specs=in_specs, out_specs=P(tm, mp), check_vma=False)
```
